32 devices in a mesh: seq: 4 (over y, x), tensor: 8 (over z, core).
Axes of the slice: x: 2, y: 2, z: 4, core: 2. Of those that a mesh axis runs over, the one named last changes fastest.
Arguments:
- states: bfloat16 [16, 2048], P('tensor'), may hold values from -6 to 6
- attn_gain: bfloat16 [2048], replicated, may hold values from 0.5 to 1.5
- w_qkv: bfloat16 [2048, 3, 2048], P(None, None, 'tensor'), may hold values from -0.125 to 0.125
- w_out: bfloat16 [2048, 2048], P('tensor'), may hold values from -0.125 to 0.125
- mlp_gain: bfloat16 [2048], replicated, may hold values from 0.5 to 1.5
- w_gate_up: bfloat16 [2048, 2, 8192], P(None, None, 'tensor'), may hold values from -0.125 to 0.125
- w_down: bfloat16 [8192, 2048], P('tensor'), may hold values from -0.0625 to 0.0625
- key_cache: bfloat16 [16, 2048, 4096], P('tensor', None, 'seq')
- value_cache: bfloat16 [16, 2048, 4096], P('tensor', None, 'seq')
- sink_keys: bfloat16 [16, 2048, 4], P('tensor'), may hold values from -8 to 8
- sink_values: bfloat16 [16, 2048, 4], P('tensor'), may hold values from -6 to 6
- cache_len: int32 [16], replicated, may hold values from 1 to 4096, as said below
- slot_mask: int32 [16, 4096], P('tensor', 'seq'), may hold values 0 or 1
- slot_pos: int32 [16, 4096], P('tensor', 'seq'), may hold values from 0 to 8191
- new_pos: int32 [16], replicated, may hold values from 4096 to 8191
Outputs:
- out_states: bfloat16 [16, 2048], P('tensor')
- new_keys: bfloat16 [16, 2048], P(None, 'tensor')
- new_values: bfloat16 [16, 2048], P(None, 'tensor')
The draws below stay inside these ranges and needn't reach their ends.
Inputs may be any that keep to these rules, and one draw needn't show every extreme that they name: `cache_len`: at least one request has all 4096 slots filled in every draw.
All inputs are finite; a program needn't handle non-finite values. No bound on the sum of `slot_mask` on one device may be relied on, other than what follows from the above.
Results may differ from the reference program's by a relative error of at most 0.02.
The reference program's roundings to bfloat16 on the way count: a program that leaves them out, or rounds other values in their place, can miss the bound.
Values may be sent and summed in bfloat16 or wider, within the bound.
No kernel may reach another device: no remote copies, remote signals or barrier semaphores. Data moves between devices by JAX's collectives and lax.ppermute only.
A program may use at most 128 MiB of HBM per device.

```python
import jax
import jax.numpy as jnp
from jax import lax

D = 2048
ATTENTION_HEADS = 32
HEAD_SIZE = 64
FF = 8192
SINK_COUNT = 4
WINDOW = 4096
REQ = 16


def draw_key_cache(key, part):
    first = jax.random.fold_in(jax.random.fold_in(key, 11), 0)
    shape = (REQ, ATTENTION_HEADS * HEAD_SIZE, WINDOW)
    base = jax.random.normal(first, shape, jnp.float32)
    return base.astype(jnp.bfloat16)


def draw_value_cache(key, part):
    first = jax.random.fold_in(jax.random.fold_in(key, 23), 0)
    shape = (REQ, ATTENTION_HEADS * HEAD_SIZE, WINDOW)
    base = jax.random.normal(first, shape, jnp.float32)
    return base.astype(jnp.bfloat16)


def draw_cache_len(key, part):
    first, second, third = jax.random.split(jax.random.fold_in(key, 37), 3)
    left = jax.random.randint(first, (REQ,), 1, WINDOW + 1)
    right = jax.random.randint(second, (REQ,), 1, WINDOW + 1)
    lengths = jnp.maximum(left * right // WINDOW, 1)
    chosen = jax.random.randint(third, (), 0, REQ)
    lengths = jnp.where(jnp.arange(REQ) == chosen, WINDOW, lengths)
    return lengths.astype(jnp.int32)


def with_ends(values, key, smallest, largest):
    extent = values.shape
    place = [jax.random.randint(jax.random.fold_in(key, axis), (), 0, extent[axis]) for axis in range(len(extent))]
    values = values.at[tuple(place)].set(smallest)
    longest = extent.index(max(extent))
    place[longest] = (place[longest] + 1) % extent[longest]
    return values.at[tuple(place)].set(largest)


def levels(key, shape, shards, least, high):
    loudness = 1.0
    for axis_at, blocks in shards:
        heights = jax.random.uniform(jax.random.fold_in(jax.random.fold_in(key, 6), axis_at), (blocks,), jnp.float32, least / len(shards), high / len(shards))
        loudness = loudness * jnp.repeat(jnp.exp(heights), shape[axis_at] // blocks).reshape((-1,) + (1,) * (len(shape) - 1 - axis_at))
    return loudness


def scatter_about(own_key, shape, spread, reach, pieces=(), kind=jnp.bfloat16):
    result = spread * jax.random.normal(own_key, shape, jnp.float32)
    if pieces:
        result = result * levels(own_key, shape, pieces, -0.22, 0.18)
    return jnp.clip(result, -reach, reach).astype(kind)


def setup_inputs(seed: int = 0) -> dict:
    streams_of = jax.random.split(jax.random.key(seed), 16)
    return {
        "states": scatter_about(streams_of[0], (REQ, D), 1.0, 6.0, ((0, 8),)),
        "attn_gain": jnp.clip(1.0 + 0.1 * jax.random.normal(streams_of[1], (D,), jnp.float32), 0.5, 1.5).astype(jnp.bfloat16),
        "w_qkv": scatter_about(streams_of[2], (D, 3, ATTENTION_HEADS * HEAD_SIZE), D ** -0.5, 0.125, ((2, 8),)),
        "w_out": scatter_about(streams_of[3], (ATTENTION_HEADS * HEAD_SIZE, D), (ATTENTION_HEADS * HEAD_SIZE) ** -0.5, 0.125, ((0, 8),)),
        "mlp_gain": jnp.clip(1.0 + 0.1 * jax.random.normal(streams_of[4], (D,), jnp.float32), 0.5, 1.5).astype(jnp.bfloat16),
        "w_gate_up": scatter_about(streams_of[5], (D, 2, FF), D ** -0.5, 0.125, ((2, 8),)),
        "w_down": scatter_about(streams_of[6], (FF, D), FF ** -0.5, 0.0625, ((0, 8),)),
        "key_cache": draw_key_cache(jax.random.fold_in(streams_of[15], 71), 0),
        "value_cache": draw_value_cache(jax.random.fold_in(streams_of[15], 71), 0),
        "sink_keys": scatter_about(streams_of[9], (REQ, ATTENTION_HEADS * HEAD_SIZE, SINK_COUNT), 2.0, 8.0, ((0, 8),)),
        "sink_values": scatter_about(streams_of[10], (REQ, ATTENTION_HEADS * HEAD_SIZE, SINK_COUNT), 1.0, 6.0, ((0, 8),)),
        "cache_len": draw_cache_len(jax.random.fold_in(streams_of[15], 71), 0),
        "slot_mask": with_ends((jax.random.randint(streams_of[12], (REQ, WINDOW), 0, 4) < 3).astype(jnp.int32), jax.random.fold_in(streams_of[12], 1), 0, 1),
        "slot_pos": with_ends(jax.random.randint(streams_of[13], (REQ, WINDOW), 0, 2 * WINDOW), jax.random.fold_in(streams_of[13], 1), 0, (2 * WINDOW) - 1).astype(jnp.int32),
        "new_pos": with_ends(jax.random.randint(streams_of[14], (REQ,), WINDOW, 2 * WINDOW), jax.random.fold_in(streams_of[14], 1), WINDOW, (2 * WINDOW) - 1).astype(jnp.int32),
    }


NEG = -1e+30

def rms_norm(values, gain):
    meansq = lax.optimization_barrier(jnp.mean(values * values, axis=-1, keepdims=True))
    return (values * lax.rsqrt(meansq + 1e-05) * gain.astype(jnp.float32)).astype(jnp.bfloat16)

def rotary(tensor, cosine, sine):
    half = tensor.shape[-1] // 2
    turned = jnp.concatenate([-tensor[..., half:], tensor[..., :half]], axis=-1)
    return tensor * cosine + turned * sine

def undo_round(weights):
    rounded = lax.optimization_barrier(weights.astype(jnp.bfloat16))
    return rounded.astype(jnp.float32)

def reference(states, attn_gain, w_qkv, w_out, mlp_gain, w_gate_up, w_down, key_cache, value_cache, sink_keys, sink_values, cache_len, slot_mask, slot_pos, new_pos):
    floats = states.astype(jnp.float32)
    normed = rms_norm(floats, attn_gain)
    projected = jnp.dot(normed, w_qkv.reshape(D, 3 * ATTENTION_HEADS * HEAD_SIZE), preferred_element_type=jnp.float32)
    projected = projected.reshape(REQ, 3, ATTENTION_HEADS, HEAD_SIZE)
    half = HEAD_SIZE // 2
    inverse = jnp.exp(-jnp.log(jnp.float32(130000.0)) * jnp.arange(half, dtype=jnp.float32) * (2.0 / HEAD_SIZE))
    angle = new_pos.astype(jnp.float32)[:, None] * inverse[None, :]
    angle = jnp.concatenate([angle, angle], axis=-1)[:, None, :]
    cosine = jnp.cos(angle)
    sine = jnp.sin(angle)
    queries = rotary(projected[:, 0], cosine, sine).astype(jnp.bfloat16)
    keys_new = rotary(projected[:, 1], cosine, sine).astype(jnp.bfloat16)
    values_new = projected[:, 2].astype(jnp.bfloat16)
    slots = jnp.arange(WINDOW, dtype=jnp.int32)
    live = (slots[None, :] < cache_len[:, None]) & (slot_mask == 1)
    live = live & (slot_pos < new_pos[:, None]) & (new_pos[:, None] - slot_pos < WINDOW)

    def one_request(entry_list):
        query_vector, single_key, single_value, window_key_cache, window_value_cache, sink_key_block, sink_value_block, valid_mask = entry_list
        qfloat = query_vector.astype(jnp.float32)
        kwin = window_key_cache.astype(jnp.float32).reshape(ATTENTION_HEADS, HEAD_SIZE, WINDOW)
        vwin = window_value_cache.astype(jnp.float32).reshape(ATTENTION_HEADS, HEAD_SIZE, WINDOW)
        sink_key_rows = sink_key_block.astype(jnp.float32).reshape(ATTENTION_HEADS, HEAD_SIZE, SINK_COUNT)
        vsink = sink_value_block.astype(jnp.float32).reshape(ATTENTION_HEADS, HEAD_SIZE, SINK_COUNT)
        score_win = jnp.einsum('hd,hds->hs', qfloat, kwin) * 0.125
        score_win = jnp.where(valid_mask[None, :], score_win, NEG)
        score_sink = jnp.einsum('hd,hds->hs', qfloat, sink_key_rows) * 0.125
        score_new = lax.optimization_barrier(jnp.sum(qfloat * single_key.astype(jnp.float32), axis=-1)) * 0.125
        top = jnp.maximum(jnp.maximum(lax.optimization_barrier(jnp.max(score_win, axis=-1)), lax.optimization_barrier(jnp.max(score_sink, axis=-1))), score_new)
        weight_win = jnp.where(valid_mask[None, :], jnp.exp(score_win - top[:, None]), 0.0)
        weight_sink = jnp.exp(score_sink - top[:, None])
        weight_new = jnp.exp(score_new - top)
        total = lax.optimization_barrier(jnp.sum(weight_win, axis=-1)) + lax.optimization_barrier(jnp.sum(weight_sink, axis=-1)) + weight_new
        mixture = jnp.einsum('hs,hds->hd', undo_round(weight_win), vwin)
        mixture = mixture + jnp.einsum('hs,hds->hd', undo_round(weight_sink), vsink)
        mixture = mixture + undo_round(weight_new)[:, None] * single_value.astype(jnp.float32)
        return (mixture / total[:, None]).astype(jnp.bfloat16).reshape(ATTENTION_HEADS * HEAD_SIZE)
    attended = lax.map(one_request, (queries, keys_new, values_new, key_cache, value_cache, sink_keys, sink_values, live))
    resid = (floats + jnp.dot(attended, w_out, preferred_element_type=jnp.float32)).astype(jnp.bfloat16)
    resid_f = resid.astype(jnp.float32)
    normed2 = rms_norm(resid_f, mlp_gain)
    gate_up = jnp.dot(normed2, w_gate_up.reshape(D, 2 * FF), preferred_element_type=jnp.float32)
    hidden = (jax.nn.silu(gate_up[:, :FF]) * gate_up[:, FF:]).astype(jnp.bfloat16)
    out_states = (resid_f + jnp.dot(hidden, w_down, preferred_element_type=jnp.float32)).astype(jnp.bfloat16)
    return (out_states, keys_new.reshape(REQ, ATTENTION_HEADS * HEAD_SIZE), values_new.reshape(REQ, ATTENTION_HEADS * HEAD_SIZE))
```

```python
import functools

import jax
import jax.numpy as jnp
from jax import lax
from jax.experimental import pallas as pl
from jax.experimental.pallas import tpu as pltpu
from jax.sharding import PartitionSpec as P

HEAD_SIZE = 64
WINDOW = 4096
NEG = -1e30
LANE = 128
HEADS_BLOCK = 8
MIB = 2**20

VMEM_SPEC = pl.BlockSpec(memory_space=pltpu.VMEM)
SMEM_SPEC = pl.BlockSpec(memory_space=pltpu.SMEM)
F32 = jnp.float32
BF16 = jnp.bfloat16


def normed_rows(values, gain):
    meansq = jnp.mean(values * values, axis=-1, keepdims=True)
    return (values * lax.rsqrt(meansq + 1e-05) * gain).astype(BF16)


def swap_halves(tensor):
    width = tensor.shape[1]
    half = HEAD_SIZE // 2
    if width == HEAD_SIZE:
        return jnp.concatenate([tensor[:, half:], tensor[:, :half]], axis=1)
    lane = lax.broadcasted_iota(jnp.int32, tensor.shape, 1)
    upper = pltpu.roll(tensor, width - half, 1)
    lower = pltpu.roll(tensor, half, 1)
    return jnp.where(lane % HEAD_SIZE < half, upper, lower)


def wire_row(rows, lane_chunk, row):
    return lane_chunk * rows + row


def qkv_kernel(rows, x_ref, gain_ref, w_ref, cos_ref, sin_ref, q_ref, k_ref, v_ref, new_ref):
    lanes = w_ref.shape[2]
    normed = normed_rows(x_ref[...].astype(F32), gain_ref[...].astype(F32))
    cosine = cos_ref[...]
    sine = sin_ref[...]

    def project(part):
        return jnp.dot(normed, w_ref[part], preferred_element_type=F32)

    def turned(t):
        return (t * cosine + swap_halves(t) * sine).astype(BF16)

    queries = turned(project(0))
    keys = turned(project(1))
    values = project(2).astype(BF16)
    k_ref[...] = keys
    v_ref[...] = values
    queries = queries.astype(F32)
    head_in = lax.broadcasted_iota(jnp.int32, (lanes, lanes), 0) // HEAD_SIZE
    head_out = lax.broadcasted_iota(jnp.int32, (lanes, lanes), 1) // HEAD_SIZE
    same_head = (head_in == head_out).astype(F32)
    score = jnp.dot(
        queries * keys.astype(F32),
        same_head,
        preferred_element_type=F32,
        precision=lax.Precision.HIGHEST,
    ) * (HEAD_SIZE**-0.5)
    values = values.astype(F32)
    groups, half, chunk = q_ref.shape[0], q_ref.shape[1] // 2, q_ref.shape[2]
    q_ref[...] = jnp.zeros_like(q_ref)
    for group in range(groups):
        mine = slice(group * rows, (group + 1) * rows)
        for c in range(lanes // chunk):
            at = slice(c * chunk, (c + 1) * chunk)
            row = wire_row(rows, c, 0)
            q_ref[group, row : row + rows, :] = queries[mine, at]
            new_ref[group, row : row + rows, :] = values[mine, at]
            new_ref[group, half + row : half + row + rows, :] = score[mine, at]


def attention_kernel(
    lanes,
    len_ref,
    pos_ref,
    q_ref,
    k_ref,
    v_ref,
    sink_k_ref,
    sink_v_ref,
    mask_ref,
    slot_pos_ref,
    out_ref,
):
    rows, features, slots = k_ref.shape
    sinks = sink_k_ref.shape[1]
    copies = out_ref.shape[0]
    half, chunk = out_ref.shape[2] // 2, out_ref.shape[3]
    block = HEADS_BLOCK * HEAD_SIZE
    seq_index = lax.axis_index("seq")
    first_row = lax.axis_index("tensor") * rows
    head = lax.broadcasted_iota(jnp.int32, (HEADS_BLOCK, block), 0)
    own = head == lax.broadcasted_iota(jnp.int32, (HEADS_BLOCK, block), 1) // HEAD_SIZE
    slot = seq_index * slots + lax.broadcasted_iota(jnp.int32, (1, slots), 1)
    scale = HEAD_SIZE**-0.5
    for r in range(rows):
        own_len = len_ref[first_row + r]
        own_pos = pos_ref[first_row + r]
        slot_at = slot_pos_ref[r : r + 1, :]
        live = (slot < own_len) & (mask_ref[r : r + 1, :] == 1)
        live = live & (slot_at < own_pos) & (own_pos - slot_at < WINDOW)
        live = jnp.broadcast_to(live.astype(jnp.int32), (HEADS_BLOCK, slots)) == 1
        sink_keys = sink_k_ref[r].astype(F32)
        sink_values = sink_v_ref[r].astype(F32)
        for b in range(features // block):
            here = slice(b * block, (b + 1) * block)
            chunks = [divmod(b * (block // chunk) + f, lanes // chunk) for f in range(block // chunk)]
            query = jnp.concatenate(
                [
                    q_ref[t, wire_row(rows, c, r) : wire_row(rows, c, r) + 1, :]
                    for t, c in chunks
                ],
                axis=1,
            )
            query = jnp.where(own, jnp.broadcast_to(query, (HEADS_BLOCK, block)), 0.0)
            score = (
                jnp.dot(query.astype(BF16), k_ref[r, here, :], preferred_element_type=F32) * scale
            )
            score = jnp.where(live, score, NEG)
            top = jnp.max(score, axis=1, keepdims=True)
            sink_score = []
            for i in range(sinks):
                one = jnp.sum(query * sink_keys[i : i + 1, here], axis=1, keepdims=True) * scale
                one = jnp.where(seq_index == 0, one, NEG)
                sink_score.append(one)
                top = jnp.maximum(top, one)
            weight = jnp.where(live, jnp.exp(score - top), 0.0)
            total = jnp.sum(weight, axis=1, keepdims=True)
            mixture = lax.dot_general(
                weight.astype(BF16),
                v_ref[r, here, :],
                (((1,), (1,)), ((), ())),
                preferred_element_type=F32,
            )
            for i in range(sinks):
                one = jnp.where(seq_index == 0, jnp.exp(sink_score[i] - top), 0.0)
                total = total + one
                mixture = mixture + one.astype(BF16).astype(F32) * sink_values[i : i + 1, here]
            some = total > 0.0
            level = jnp.where(some, top + jnp.log(jnp.where(some, total, 1.0)), NEG)
            mixture = mixture / jnp.where(some, total, 1.0)
            mixture = jnp.sum(jnp.where(own, mixture, 0.0), axis=0, keepdims=True)
            level = jnp.sum(jnp.where(own, level, 0.0), axis=0, keepdims=True)
            for f, (t, c) in enumerate(chunks):
                row = wire_row(rows, c, r)
                at = slice(f * chunk, (f + 1) * chunk)
                for copy in range(copies):
                    out_ref[copy, t, row : row + 1, :] = mixture[:, at]
                    out_ref[copy, t, half + row : half + row + 1, :] = level[:, at]


def merge_kernel(rows, part_ref, new_ref, w_ref, mine_ref, other_ref, rows_ref, full_ref):
    copies, groups, wire_rows, chunk = part_ref.shape
    half = wire_rows // 2
    lanes = w_ref.shape[0]
    flat = groups * wire_rows
    parts = [part_ref[s].reshape(flat, chunk) for s in range(copies)]
    parts.append(new_ref[...].reshape(flat, chunk))
    levels = [pltpu.roll(part, flat - half, 0) for part in parts]
    top = functools.reduce(jnp.maximum, levels)
    mixture = jnp.zeros((flat, chunk), F32)
    total = jnp.zeros((flat, chunk), F32)
    for part, level in zip(parts, levels):
        share = jnp.exp(level - top)
        mixture = mixture + share * part
        total = total + share
    rows_ref[...] = mixture / total
    attended = []
    for c in range(lanes // chunk):
        start = wire_row(rows, c, 0)
        attended.append(
            jnp.concatenate(
                [
                    rows_ref[g * wire_rows + start : g * wire_rows + start + rows, :]
                    for g in range(groups)
                ],
                axis=0,
            )
        )
    attended = jnp.concatenate(attended, axis=1).astype(BF16)
    full_ref[...] = jnp.dot(attended, w_ref[...], preferred_element_type=F32)
    width = mine_ref.shape[1]
    core = lax.axis_index("tensor") % 2
    mine_ref[...] = full_ref[:, pl.ds(pl.multiple_of(core * width, LANE), width)]
    other_ref[...] = full_ref[:, pl.ds(pl.multiple_of((1 - core) * width, LANE), width)]


def mlp_kernel(mine_ref, other_ref, gain_ref, gate_up_ref, down_ref, out_ref, resid_ref, wide_ref):
    batch, width = mine_ref.shape
    units = gate_up_ref.shape[2]
    core = lax.axis_index("tensor") % 2
    first = jnp.where(core == 0, mine_ref[...].astype(F32), other_ref[...].astype(F32))
    second = jnp.where(core == 0, other_ref[...].astype(F32), mine_ref[...].astype(F32))
    resid = jnp.concatenate([first, second], axis=1)
    resid_ref[...] = resid.astype(BF16)
    normed = normed_rows(resid, gain_ref[...].astype(F32))
    step = 2 * LANE
    feature = lax.broadcasted_iota(jnp.int32, (step, 4 * step), 0)
    lane = lax.broadcasted_iota(jnp.int32, (step, 4 * step), 1)
    lane = jnp.where(lane < 2 * step, lane, lane - 2 * step - 1)
    spread = (2 * feature == lane).astype(F32).astype(BF16)
    pieces = 2 * width // step
    stacked = jnp.concatenate([normed[:, j * step : (j + 1) * step] for j in range(pieces)], axis=0)
    wide = jnp.dot(stacked, spread, preferred_element_type=F32).astype(BF16)
    for j in range(pieces):
        part = wide[j * batch : (j + 1) * batch, :]
        at = slice(j * 2 * step, (j + 1) * 2 * step)
        wide_ref[:batch, at] = part[:, : 2 * step]
        wide_ref[batch:, at] = part[:, 2 * step :]
    weights = gate_up_ref.reshape(4 * width, units)
    gate_up = jnp.dot(wide_ref[...], weights[...], preferred_element_type=F32)
    gate = gate_up[:batch]
    hidden = (gate * jax.nn.sigmoid(gate) * gate_up[batch:]).astype(BF16)
    out_ref[...] = jnp.dot(hidden, down_ref[...], preferred_element_type=F32).astype(BF16)


def call(kernel, out, inputs, specs=None, scratch=(), limit=16, name=None, flops=0):
    return pl.pallas_call(
        kernel,
        out_shape=out,
        in_specs=specs or [VMEM_SPEC] * len(inputs),
        out_specs=jax.tree.map(lambda _: VMEM_SPEC, out),
        scratch_shapes=scratch,
        compiler_params=pltpu.CompilerParams(vmem_limit_bytes=limit * MIB),
        name=name,
        cost_estimate=pl.CostEstimate(
            flops=flops,
            bytes_accessed=sum(a.size * a.dtype.itemsize for a in inputs),
            transcendentals=0,
        ),
    )(*inputs)


def per_device(
    shards,
    groups,
    states,
    attn_gain,
    w_qkv,
    w_out,
    mlp_gain,
    w_gate_up,
    w_down,
    key_cache,
    value_cache,
    sink_keys,
    sink_values,
    cache_len,
    slot_mask,
    slot_pos,
    new_pos,
):
    rows, width = states.shape
    batch = rows * groups
    lanes = w_qkv.shape[2]
    tensor = lax.axis_index("tensor")
    sds = jax.ShapeDtypeStruct
    chunk = min(lanes, LANE)
    wire_rows = max(8, 2 * rows * lanes // chunk)

    half = HEAD_SIZE // 2
    inverse = jnp.exp(-jnp.log(F32(130000.0)) * jnp.arange(half, dtype=F32) * (2.0 / HEAD_SIZE))
    angle = new_pos.astype(F32)[:, None] * inverse[None, :]
    cosine = jnp.cos(angle)
    sine = jnp.sin(angle)
    heads_here = lanes // HEAD_SIZE
    cosine = jnp.tile(cosine, (1, 2 * heads_here))
    sine = jnp.tile(jnp.concatenate([-sine, sine], axis=1), (1, heads_here))

    everyone = lax.all_to_all(
        jnp.broadcast_to(states[None], (groups, rows, width)), "tensor", 0, 0, tiled=True
    ).reshape(batch, width)
    wire = sds((groups, wire_rows, chunk), F32)
    flat = sds((batch, lanes), BF16)
    queries, new_keys, new_values, new_part = call(
        functools.partial(qkv_kernel, rows),
        (wire, flat, flat, wire),
        (everyone, attn_gain[None], jnp.transpose(w_qkv, (1, 0, 2)), cosine, sine),
        name="qkv",
        flops=2 * batch * width * 3 * lanes,
    )
    queries = lax.all_to_all(queries, "tensor", 0, 0, tiled=True)
    part = call(
        functools.partial(attention_kernel, lanes),
        sds((shards, groups, wire_rows, chunk), F32),
        (
            cache_len,
            new_pos,
            queries,
            key_cache,
            value_cache,
            jnp.transpose(sink_keys, (0, 2, 1)),
            jnp.transpose(sink_values, (0, 2, 1)),
            slot_mask,
            slot_pos,
        ),
        specs=[SMEM_SPEC] * 2 + [VMEM_SPEC] * 7,
        limit=28,
        name="attention",
        flops=4 * HEADS_BLOCK * key_cache.size,
    )
    part = lax.all_to_all(
        part.reshape(shards * groups, wire_rows, chunk), ("seq", "tensor"), 0, 0, tiled=True
    ).reshape(shards, groups, wire_rows, chunk)
    side = sds((batch, width // 2), F32)
    mine, other = call(
        functools.partial(merge_kernel, rows),
        (side, side),
        (part, new_part, w_out),
        scratch=[pltpu.VMEM((groups * wire_rows, chunk), F32), pltpu.VMEM((batch, width), F32)],
        name="merge",
        flops=2 * batch * lanes * width,
    )
    across = [(i, i ^ 1) for i in range(groups)]
    chip = (mine + lax.ppermute(other, "tensor", across)).astype(BF16)
    total = chip.astype(F32)
    for step in range(2, groups, 2):
        hop = [(i, (i + step) % groups) for i in range(groups)]
        total = total + lax.ppermute(chip, "tensor", hop).astype(F32)
    own_side = lax.dynamic_slice_in_dim(everyone, (tensor % 2) * (width // 2), width // 2, 1)
    side_resid = (own_side.astype(F32) + total).astype(BF16)
    other_resid = lax.ppermute(side_resid, "tensor", across)
    partial, resid = call(
        mlp_kernel,
        (sds((batch, width), BF16), sds((batch, width), BF16)),
        (side_resid, other_resid, mlp_gain[None], w_gate_up, w_down),
        scratch=[pltpu.VMEM((2 * batch, 2 * width), BF16)],
        limit=24,
        name="mlp",
        flops=6 * batch * width * w_gate_up.shape[2],
    )
    partial = lax.all_to_all(partial.reshape(groups, rows, width), "tensor", 0, 0, tiled=True)
    own_resid = lax.dynamic_slice_in_dim(resid, tensor * rows, rows, 0)
    out_states = (own_resid.astype(F32) + jnp.sum(partial.astype(F32), axis=0)).astype(BF16)
    return out_states, new_keys, new_values


def solution(mesh):
    in_specs = (
        P("tensor", None),
        P(),
        P(None, None, "tensor"),
        P("tensor", None),
        P(),
        P(None, None, "tensor"),
        P("tensor", None),
        P("tensor", None, "seq"),
        P("tensor", None, "seq"),
        P("tensor", None, None),
        P("tensor", None, None),
        P(),
        P("tensor", "seq"),
        P("tensor", "seq"),
        P(),
    )
    out_specs = (P("tensor", None), P(None, "tensor"), P(None, "tensor"))
    body = functools.partial(per_device, mesh.shape["seq"], mesh.shape["tensor"])
    return jax.shard_map(
        body, mesh=mesh, in_specs=in_specs, out_specs=out_specs, check_vma=False
    )
```

```python
import functools

import jax
import jax.numpy as jnp
import numpy as np
from jax import lax
from jax.experimental import pallas as pl
from jax.experimental.pallas import tpu as pltpu
from jax.sharding import PartitionSpec as P

HEAD_SIZE = 64
WINDOW = 4096
NEG = -1e30
LANE = 128
HEADS_BLOCK = 8
MIB = 2**20
PREP_FLOPS = 20_000_000_000
QKV_FLOPS = 20_000_000_000
ATT_FLOPS = 10_000_000_000
MERGE_FLOPS = 10_000_000_000

VMEM_SPEC = pl.BlockSpec(memory_space=pltpu.VMEM)
SMEM_SPEC = pl.BlockSpec(memory_space=pltpu.SMEM)
F32 = jnp.float32
BF16 = jnp.bfloat16


def normed_rows(values, gain):
    meansq = jnp.mean(values * values, axis=-1, keepdims=True)
    return (values * lax.rsqrt(meansq + 1e-05) * gain).astype(BF16)


def swap_halves(tensor):
    width = tensor.shape[1]
    half = HEAD_SIZE // 2
    if width == HEAD_SIZE:
        return jnp.concatenate([tensor[:, half:], tensor[:, :half]], axis=1)
    lane = lax.broadcasted_iota(jnp.int32, tensor.shape, 1)
    upper = pltpu.roll(tensor, width - half, 1)
    lower = pltpu.roll(tensor, half, 1)
    return jnp.where(lane % HEAD_SIZE < half, upper, lower)


def wire_row(rows, lane_chunk, row):
    return lane_chunk * rows + row


def qkv_kernel(
    rows,
    same_ref,
    peer_ref,
    gain_ref,
    w_ref,
    cos_ref,
    sin_ref,
    q_ref,
    k_ref,
    v_ref,
    new_ref,
    side_ref,
    by_ref,
    flat_ref,
):
    lanes = w_ref.shape[2]
    core = lax.axis_index("tensor") % 2
    chip = lax.axis_index("tensor") // 2
    chips = same_ref.shape[0]
    for step in range(chips):
        source = 2 * lax.rem(chip + chips - step, chips)
        by_ref[source + core, :rows, :] = same_ref[step].astype(F32)
        by_ref[source + 1 - core, :rows, :] = peer_ref[step].astype(F32)
    for group in range(2 * chips):
        flat_ref[group * rows : (group + 1) * rows, :] = by_ref[group, :rows, :]
    values = flat_ref[...]
    width = side_ref.shape[1]
    side_ref[...] = flat_ref[:, pl.ds(pl.multiple_of(core * width, LANE), width)]
    normed = normed_rows(values, gain_ref[...].astype(F32))
    cosine = cos_ref[...]
    sine = sin_ref[...]

    def project(part):
        return jnp.dot(normed, w_ref[part], preferred_element_type=F32)

    def turned(t):
        return (t * cosine + swap_halves(t) * sine).astype(BF16)

    queries = turned(project(0))
    keys = turned(project(1))
    values = project(2).astype(BF16)
    k_ref[...] = keys
    v_ref[...] = values
    queries = queries.astype(F32)
    head_in = lax.broadcasted_iota(jnp.int32, (lanes, lanes), 0) // HEAD_SIZE
    head_out = lax.broadcasted_iota(jnp.int32, (lanes, lanes), 1) // HEAD_SIZE
    same_head = (head_in == head_out).astype(F32)
    score = jnp.dot(
        queries * keys.astype(F32),
        same_head,
        preferred_element_type=F32,
        precision=lax.Precision.HIGHEST,
    ) * (HEAD_SIZE**-0.5)
    values = values.astype(F32)
    groups, half, chunk = q_ref.shape[0], q_ref.shape[1] // 2, q_ref.shape[2]
    q_ref[...] = jnp.zeros_like(q_ref)
    for group in range(groups):
        mine = slice(group * rows, (group + 1) * rows)
        for c in range(lanes // chunk):
            at = slice(c * chunk, (c + 1) * chunk)
            row = wire_row(rows, c, 0)
            q_ref[group, row : row + rows, :] = queries[mine, at]
            new_ref[group, row : row + rows, :] = values[mine, at]
            new_ref[group, half + row : half + row + rows, :] = score[mine, at]


def attention_kernel(
    lanes,
    q_ref,
    k_ref,
    v_ref,
    sink_k_ref,
    sink_v_ref,
    live_ref,
    out_ref,
):
    rows, features, slots = k_ref.shape
    sinks = sink_k_ref.shape[1]
    copies = out_ref.shape[0]
    half, chunk = out_ref.shape[2] // 2, out_ref.shape[3]
    block = HEADS_BLOCK * HEAD_SIZE
    seq_index = lax.axis_index("seq")
    head = lax.broadcasted_iota(jnp.int32, (HEADS_BLOCK, block), 0)
    own = head == lax.broadcasted_iota(jnp.int32, (HEADS_BLOCK, block), 1) // HEAD_SIZE
    scale = HEAD_SIZE**-0.5
    for r in range(rows):
        live = jnp.broadcast_to(live_ref[r : r + 1, :], (HEADS_BLOCK, slots)) == 1
        sink_keys = sink_k_ref[r].astype(F32)
        sink_values = sink_v_ref[r].astype(F32)
        for b in range(features // block):
            here = slice(b * block, (b + 1) * block)
            chunks = [divmod(b * (block // chunk) + f, lanes // chunk) for f in range(block // chunk)]
            query = jnp.concatenate(
                [
                    q_ref[t, wire_row(rows, c, r) : wire_row(rows, c, r) + 1, :]
                    for t, c in chunks
                ],
                axis=1,
            )
            query = jnp.where(own, jnp.broadcast_to(query, (HEADS_BLOCK, block)), 0.0)
            score = (
                jnp.dot(query.astype(BF16), k_ref[r, here, :], preferred_element_type=F32) * scale
            )
            score = jnp.where(live, score, NEG)
            top = jnp.max(score, axis=1, keepdims=True)
            sink_score = []
            for i in range(sinks):
                one = jnp.sum(query * sink_keys[i : i + 1, here], axis=1, keepdims=True) * scale
                one = jnp.where(seq_index == 0, one, NEG)
                sink_score.append(one)
                top = jnp.maximum(top, one)
            weight = jnp.where(live, jnp.exp(score - top), 0.0)
            total = jnp.sum(weight, axis=1, keepdims=True)
            mixture = lax.dot_general(
                weight.astype(BF16),
                v_ref[r, here, :],
                (((1,), (1,)), ((), ())),
                preferred_element_type=F32,
            )
            for i in range(sinks):
                one = jnp.where(seq_index == 0, jnp.exp(sink_score[i] - top), 0.0)
                total = total + one
                mixture = mixture + one.astype(BF16).astype(F32) * sink_values[i : i + 1, here]
            some = total > 0.0
            level = jnp.where(some, top + jnp.log(jnp.where(some, total, 1.0)), NEG)
            mixture = mixture / jnp.where(some, total, 1.0)
            mixture = jnp.sum(jnp.where(own, mixture, 0.0), axis=0, keepdims=True)
            level = jnp.sum(jnp.where(own, level, 0.0), axis=0, keepdims=True)
            for f, (t, c) in enumerate(chunks):
                row = wire_row(rows, c, r)
                at = slice(f * chunk, (f + 1) * chunk)
                for copy in range(copies):
                    out_ref[copy, t, row : row + 1, :] = mixture[:, at]
                    out_ref[copy, t, half + row : half + row + 1, :] = level[:, at]


def merge_kernel(rows, part_ref, new_ref, w_ref, mine_ref, other_ref, rows_ref, full_ref):
    copies, groups, wire_rows, chunk = part_ref.shape
    half = wire_rows // 2
    lanes = w_ref.shape[0]
    flat = groups * wire_rows
    parts = [part_ref[s].reshape(flat, chunk) for s in range(copies)]
    parts.append(new_ref[...].reshape(flat, chunk))
    levels = [pltpu.roll(part, flat - half, 0) for part in parts]
    top = functools.reduce(jnp.maximum, levels)
    mixture = jnp.zeros((flat, chunk), F32)
    total = jnp.zeros((flat, chunk), F32)
    for part, level in zip(parts, levels):
        share = jnp.exp(level - top)
        mixture = mixture + share * part
        total = total + share
    rows_ref[...] = mixture / total
    attended = []
    for c in range(lanes // chunk):
        start = wire_row(rows, c, 0)
        attended.append(
            jnp.concatenate(
                [
                    rows_ref[g * wire_rows + start : g * wire_rows + start + rows, :]
                    for g in range(groups)
                ],
                axis=0,
            )
        )
    attended = jnp.concatenate(attended, axis=1).astype(BF16)
    full_ref[...] = jnp.dot(attended, w_ref[...], preferred_element_type=F32)
    width = mine_ref.shape[1]
    core = lax.axis_index("tensor") % 2
    mine_ref[...] = full_ref[:, pl.ds(pl.multiple_of(core * width, LANE), width)]
    other_ref[...] = full_ref[:, pl.ds(pl.multiple_of((1 - core) * width, LANE), width)]


def mlp_kernel(
    rows, mine_ref, other_ref, gain_ref, gate_up_ref, down_ref, out_ref, resid_ref, wide_ref, by_ref
):
    batch, width = mine_ref.shape
    units = gate_up_ref.shape[2]
    core = lax.axis_index("tensor") % 2
    first = jnp.where(core == 0, mine_ref[...].astype(F32), other_ref[...].astype(F32))
    second = jnp.where(core == 0, other_ref[...].astype(F32), mine_ref[...].astype(F32))
    resid = jnp.concatenate([first, second], axis=1)
    groups = out_ref.shape[0]
    for group in range(groups):
        by_ref[group, :rows, :] = resid[group * rows : (group + 1) * rows, :]
    resid_ref[...] = by_ref[lax.axis_index("tensor"), :rows, :]
    normed = normed_rows(resid, gain_ref[...].astype(F32))
    step = 2 * LANE
    feature = lax.broadcasted_iota(jnp.int32, (step, 4 * step), 0)
    lane = lax.broadcasted_iota(jnp.int32, (step, 4 * step), 1)
    lane = jnp.where(lane < 2 * step, lane, lane - 2 * step - 1)
    spread = (2 * feature == lane).astype(F32).astype(BF16)
    pieces = 2 * width // step
    stacked = jnp.concatenate([normed[:, j * step : (j + 1) * step] for j in range(pieces)], axis=0)
    wide = jnp.dot(stacked, spread, preferred_element_type=F32).astype(BF16)
    for j in range(pieces):
        part = wide[j * batch : (j + 1) * batch, :]
        at = slice(j * 2 * step, (j + 1) * 2 * step)
        wide_ref[:batch, at] = part[:, : 2 * step]
        wide_ref[batch:, at] = part[:, 2 * step :]
    weights = gate_up_ref.reshape(4 * width, units)
    gate_up = jnp.dot(wide_ref[...], weights[...], preferred_element_type=F32)
    gate = gate_up[:batch]
    hidden = (gate * jax.nn.sigmoid(gate) * gate_up[batch:]).astype(BF16)
    out = jnp.dot(hidden, down_ref[...], preferred_element_type=F32)
    for group in range(groups):
        out_ref[group] = out[group * rows : (group + 1) * rows, :].astype(BF16)


def prepare_kernel(
    len_ref, pos_ref, inverse_ref, mask_ref, slot_pos_ref, cos_ref, sin_ref, live_ref
):
    batch, width = cos_ref.shape
    wide = inverse_ref.shape[1]
    row = lax.broadcasted_iota(jnp.int32, (batch, wide), 0)
    position = jnp.zeros((batch, wide), F32)
    for i in range(batch):
        position = jnp.where(row == i, pos_ref[i].astype(F32), position)
    angle = position * inverse_ref[...]
    cosine = jnp.cos(angle)
    sine = jnp.sin(angle)
    lane = lax.broadcasted_iota(jnp.int32, (batch, wide), 1)
    sine = jnp.where(lane % HEAD_SIZE < HEAD_SIZE // 2, -sine, sine)
    for start in range(0, width, wide):
        cos_ref[:, start : start + wide] = cosine
        sin_ref[:, start : start + wide] = sine
    rows, slots = mask_ref.shape
    slot = lax.axis_index("seq") * slots + lax.broadcasted_iota(jnp.int32, (1, slots), 1)
    first_row = lax.axis_index("tensor") * rows
    for r in range(rows):
        own_len = len_ref[first_row + r]
        own_pos = pos_ref[first_row + r]
        slot_at = slot_pos_ref[r : r + 1, :]
        live = (slot < own_len) & (mask_ref[r : r + 1, :] == 1)
        live = live & (slot_at < own_pos) & (own_pos - slot_at < WINDOW)
        live_ref[r : r + 1, :] = live.astype(jnp.int32)


def call(kernel, out, inputs, specs=None, scratch=(), limit=6, name=None, flops=0):
    return pl.pallas_call(
        kernel,
        out_shape=out,
        in_specs=specs or [VMEM_SPEC] * len(inputs),
        out_specs=jax.tree.map(lambda _: VMEM_SPEC, out),
        scratch_shapes=scratch,
        compiler_params=pltpu.CompilerParams(vmem_limit_bytes=limit * MIB),
        name=name,
        cost_estimate=pl.CostEstimate(
            flops=flops,
            bytes_accessed=sum(a.size * a.dtype.itemsize for a in inputs),
            transcendentals=0,
        ),
    )(*inputs)


def per_device(
    shards,
    groups,
    states,
    attn_gain,
    w_qkv,
    w_out,
    mlp_gain,
    w_gate_up,
    w_down,
    key_cache,
    value_cache,
    sink_keys,
    sink_values,
    cache_len,
    slot_mask,
    slot_pos,
    new_pos,
):
    rows, width = states.shape
    batch = rows * groups
    lanes = w_qkv.shape[2]
    sds = jax.ShapeDtypeStruct
    chunk = min(lanes, LANE)
    wire_rows = max(8, 2 * rows * lanes // chunk)

    half = HEAD_SIZE // 2
    inverse = np.exp(-np.log(130000.0) * np.arange(half) * (2.0 / HEAD_SIZE))
    inverse = jnp.asarray(np.tile(inverse, 2 * chunk // HEAD_SIZE)[None], F32)
    turn = sds((batch, lanes), F32)
    cosine, sine, live = call(
        prepare_kernel,
        (turn, turn, sds(slot_mask.shape, jnp.int32)),
        (cache_len, new_pos, inverse, slot_mask, slot_pos),
        specs=[SMEM_SPEC] * 2 + [VMEM_SPEC] * 3,
        name="prepare",
        flops=PREP_FLOPS,
    )
    across = [(i, i ^ 1) for i in range(groups)]
    hops = [[(i, (i + step) % groups) for i in range(groups)] for step in range(2, groups, 2)]
    same = jnp.stack([states] + [lax.ppermute(states, "tensor", hop) for hop in hops])
    peer = lax.ppermute(same, "tensor", across)
    w_qkv = jnp.transpose(w_qkv, (1, 0, 2))
    side = sds((batch, width // 2), F32)
    wire = sds((groups, wire_rows, chunk), F32)
    flat = sds((batch, lanes), BF16)
    queries, new_keys, new_values, new_part, own_side = call(
        functools.partial(qkv_kernel, rows),
        (wire, flat, flat, wire, side),
        (same, peer, attn_gain[None], w_qkv, cosine, sine),
        scratch=[pltpu.VMEM((groups, 8, width), F32), pltpu.VMEM((batch, width), F32)],
        name="qkv",
        flops=QKV_FLOPS,
    )
    queries = lax.all_to_all(queries, "tensor", 0, 0, tiled=True)
    sink_keys = jnp.transpose(sink_keys, (0, 2, 1))
    sink_values = jnp.transpose(sink_values, (0, 2, 1))
    part = call(
        functools.partial(attention_kernel, lanes),
        sds((shards, groups, wire_rows, chunk), F32),
        (queries, key_cache, value_cache, sink_keys, sink_values, live),
        limit=8,
        name="attention",
        flops=ATT_FLOPS,
    )
    part = lax.all_to_all(
        part.reshape(shards * groups, wire_rows, chunk), ("seq", "tensor"), 0, 0, tiled=True
    ).reshape(shards, groups, wire_rows, chunk)
    mine, other = call(
        functools.partial(merge_kernel, rows),
        (side, side),
        (part, new_part, w_out),
        scratch=[pltpu.VMEM((groups * wire_rows, chunk), F32), pltpu.VMEM((batch, width), F32)],
        name="merge",
        flops=MERGE_FLOPS,
    )
    chip = (mine + lax.ppermute(other, "tensor", across)).astype(BF16)
    total = chip.astype(F32)
    for hop in hops:
        total = total + lax.ppermute(chip, "tensor", hop).astype(F32)
    side_resid = (own_side + total).astype(BF16)
    other_resid = lax.ppermute(side_resid, "tensor", across)
    partial, own_resid = call(
        functools.partial(mlp_kernel, rows),
        (sds((groups, rows, width), BF16), sds((rows, width), F32)),
        (side_resid, other_resid, mlp_gain[None], w_gate_up, w_down),
        scratch=[pltpu.VMEM((2 * batch, 2 * width), BF16), pltpu.VMEM((groups, 8, width), F32)],
        limit=8,
        name="mlp",
        flops=6 * batch * width * w_gate_up.shape[2],
    )
    partial = lax.all_to_all(partial, "tensor", 0, 0, tiled=True)
    out_states = (own_resid + jnp.sum(partial.astype(F32), axis=0)).astype(BF16)
    return out_states, new_keys, new_values


def solution(mesh):
    in_specs = (
        P("tensor", None),
        P(),
        P(None, None, "tensor"),
        P("tensor", None),
        P(),
        P(None, None, "tensor"),
        P("tensor", None),
        P("tensor", None, "seq"),
        P("tensor", None, "seq"),
        P("tensor", None, None),
        P("tensor", None, None),
        P(),
        P("tensor", "seq"),
        P("tensor", "seq"),
        P(),
    )
    out_specs = (P("tensor", None), P(None, "tensor"), P(None, "tensor"))
    body = functools.partial(per_device, mesh.shape["seq"], mesh.shape["tensor"])
    return jax.shard_map(
        body, mesh=mesh, in_specs=in_specs, out_specs=out_specs, check_vma=False
    )
```

```python
import functools

import jax
import jax.numpy as jnp
import numpy as np
from jax import lax
from jax.experimental import pallas as pl
from jax.experimental.pallas import tpu as pltpu
from jax.sharding import PartitionSpec as P

HEAD_SIZE = 64
WINDOW = 4096
ROTARY_BASE = 130000.0
NEG = -1e30
LANE = 128
MIB = 2**20
PREP_FLOPS = 20_000_000_000
QKV_FLOPS = 2_000_000_000
ATT_FLOPS = 10_000_000_000
MERGE_FLOPS = 10_000_000_000

VMEM_SPEC = pl.BlockSpec(memory_space=pltpu.VMEM)
SMEM_SPEC = pl.BlockSpec(memory_space=pltpu.SMEM)
F32 = jnp.float32
BF16 = jnp.bfloat16


def normed_rows(values, gain):
    meansq = jnp.mean(values * values, axis=-1, keepdims=True)
    return (values * lax.rsqrt(meansq + 1e-05) * gain).astype(BF16)


def swap_halves(tensor):
    width = tensor.shape[1]
    half = HEAD_SIZE // 2
    if width == HEAD_SIZE:
        return jnp.concatenate([tensor[:, half:], tensor[:, :half]], axis=1)
    lane = lax.broadcasted_iota(jnp.int32, tensor.shape, 1)
    upper = pltpu.roll(tensor, width - half, 1)
    lower = pltpu.roll(tensor, half, 1)
    return jnp.where(lane % HEAD_SIZE < half, upper, lower)


def wire_row(rows, lane_chunk, row):
    return lane_chunk * rows + row


def query_kernel(rows, chips, *refs):
    states, refs = refs[:chips], refs[chips:]
    gain_ref, own_ref, peer_ref, cos_ref, sin_ref = refs[:5]
    outs = refs[5:]
    core = lax.axis_index("tensor") % 2
    values = jnp.concatenate([ref[...].astype(F32) for ref in states], axis=0)
    normed = normed_rows(values, gain_ref[...].astype(F32))
    own = jnp.dot(normed, own_ref[...], preferred_element_type=F32)
    peer = jnp.dot(normed, peer_ref[...], preferred_element_type=F32)
    queries = jnp.concatenate(
        [jnp.where(core == 0, own, peer), jnp.where(core == 0, peer, own)], axis=1
    )
    repeat = queries.shape[1] // cos_ref.shape[1]
    cosine = jnp.concatenate([cos_ref[...]] * repeat, axis=1)
    sine = jnp.concatenate([sin_ref[...]] * repeat, axis=1)
    queries = (queries * cosine + swap_halves(queries) * sine).astype(BF16).astype(F32)
    for step in range(chips):
        first = (chips - step) % chips * rows
        out = outs[step]
        if rows * queries.shape[1] // LANE < out.shape[0]:
            out[...] = jnp.zeros_like(out)
        for c in range(queries.shape[1] // LANE):
            at = slice(c * LANE, (c + 1) * LANE)
            row = wire_row(rows, c, 0)
            out[row : row + rows, :] = queries[first : first + rows, at]


def new_token_kernel(
    rows,
    len_ref,
    pos_ref,
    mask_ref,
    slot_pos_ref,
    same_ref,
    peer_ref,
    gain_ref,
    w_ref,
    cos_ref,
    sin_ref,
    k_ref,
    v_ref,
    new_ref,
    side_ref,
    live_ref,
    by_ref,
    flat_ref,
):
    mark_live(len_ref, pos_ref, mask_ref, slot_pos_ref, live_ref)
    lanes = w_ref.shape[2]
    core = lax.axis_index("tensor") % 2
    chip = lax.axis_index("tensor") // 2
    chips = same_ref.shape[0]
    for step in range(chips):
        source = 2 * lax.rem(chip + chips - step, chips)
        by_ref[source + core, :rows, :] = same_ref[step].astype(F32)
        by_ref[source + 1 - core, :rows, :] = peer_ref[step].astype(F32)
    for group in range(2 * chips):
        flat_ref[group * rows : (group + 1) * rows, :] = by_ref[group, :rows, :]
    values = flat_ref[...]
    width = side_ref.shape[1]
    side_ref[...] = flat_ref[:, pl.ds(pl.multiple_of(core * width, LANE), width)]
    normed = normed_rows(values, gain_ref[...].astype(F32))
    repeat = lanes // cos_ref.shape[1]
    cosine = jnp.concatenate([cos_ref[...]] * repeat, axis=1)
    sine = jnp.concatenate([sin_ref[...]] * repeat, axis=1)

    def project(part):
        return jnp.dot(normed, w_ref[part], preferred_element_type=F32)

    def turned(t):
        return (t * cosine + swap_halves(t) * sine).astype(BF16)

    queries = turned(project(0))
    keys = turned(project(1))
    values = project(2).astype(BF16)
    k_ref[...] = keys
    v_ref[...] = values
    queries = queries.astype(F32)
    head_in = lax.broadcasted_iota(jnp.int32, (lanes, lanes), 0) // HEAD_SIZE
    head_out = lax.broadcasted_iota(jnp.int32, (lanes, lanes), 1) // HEAD_SIZE
    same_head = (head_in == head_out).astype(F32)
    score = jnp.dot(
        queries * keys.astype(F32),
        same_head,
        preferred_element_type=F32,
        precision=lax.Precision.HIGHEST,
    ) * (HEAD_SIZE**-0.5)
    values = values.astype(F32)
    groups, half, chunk = new_ref.shape[0], new_ref.shape[1] // 2, new_ref.shape[2]
    for group in range(groups):
        mine = slice(group * rows, (group + 1) * rows)
        for c in range(lanes // chunk):
            at = slice(c * chunk, (c + 1) * chunk)
            row = wire_row(rows, c, 0)
            new_ref[group, row : row + rows, :] = values[mine, at]
            new_ref[group, half + row : half + row + rows, :] = score[mine, at]


def attention_kernel(lanes, chips, *refs):
    queries, refs = refs[:chips], refs[chips:]
    k_ref, v_ref, sink_k_ref, sink_v_ref, live_ref, out_ref = refs
    rows, features, slots = k_ref.shape
    sinks = sink_k_ref.shape[1]
    copies = out_ref.shape[0]
    half, chunk = out_ref.shape[2] // 2, out_ref.shape[3]
    block = 2 * lanes
    heads = max(8, block // HEAD_SIZE)
    seq_index = lax.axis_index("seq")
    chip = lax.axis_index("tensor") // 2
    head = lax.broadcasted_iota(jnp.int32, (heads, block), 0)
    own = head == lax.broadcasted_iota(jnp.int32, (heads, block), 1) // HEAD_SIZE
    scale = HEAD_SIZE**-0.5
    for r in range(rows):
        live = jnp.broadcast_to(live_ref[r : r + 1, :], (heads, slots)) == 1
        for step in range(chips):
            source = lax.rem(chip + chips - step, chips)
            here = pl.ds(pl.multiple_of(source * block, block), block)
            sink_keys = sink_k_ref[r, :, here].astype(F32)
            sink_values = sink_v_ref[r, :, here].astype(F32)
            query = jnp.concatenate(
                [
                    queries[step][wire_row(rows, c, r) : wire_row(rows, c, r) + 1, :]
                    for c in range(block // LANE)
                ],
                axis=1,
            )
            query = jnp.where(own, jnp.broadcast_to(query, (heads, block)), 0.0)
            score = (
                jnp.dot(query.astype(BF16), k_ref[r, here, :], preferred_element_type=F32) * scale
            )
            score = jnp.where(live, score, NEG)
            top = jnp.max(score, axis=1, keepdims=True)
            sink_score = []
            for i in range(sinks):
                one = jnp.sum(query * sink_keys[i : i + 1, :], axis=1, keepdims=True) * scale
                one = jnp.where(seq_index == 0, one, NEG)
                sink_score.append(one)
                top = jnp.maximum(top, one)
            weight = jnp.where(live, jnp.exp(score - top), 0.0)
            total = jnp.sum(weight, axis=1, keepdims=True)
            mixture = lax.dot_general(
                weight.astype(BF16),
                v_ref[r, here, :],
                (((1,), (1,)), ((), ())),
                preferred_element_type=F32,
            )
            for i in range(sinks):
                one = jnp.where(seq_index == 0, jnp.exp(sink_score[i] - top), 0.0)
                total = total + one
                mixture = mixture + one.astype(BF16).astype(F32) * sink_values[i : i + 1, :]
            some = total > 0.0
            level = jnp.where(some, top + jnp.log(jnp.where(some, total, 1.0)), NEG)
            mixture = mixture / jnp.where(some, total, 1.0)
            mixture = jnp.sum(jnp.where(own, mixture, 0.0), axis=0, keepdims=True)
            level = jnp.sum(jnp.where(own, level, 0.0), axis=0, keepdims=True)
            for f in range(block // chunk):
                t, c = divmod(f, lanes // chunk)
                row = wire_row(rows, c, r)
                at = slice(f * chunk, (f + 1) * chunk)
                for copy in range(copies):
                    out_ref[copy, 2 * source + t, row : row + 1, :] = mixture[:, at]
                    out_ref[copy, 2 * source + t, half + row : half + row + 1, :] = level[:, at]


def merge_kernel(rows, part_ref, new_ref, w_ref, mine_ref, other_ref, rows_ref, full_ref):
    copies, groups, wire_rows, chunk = part_ref.shape
    half = wire_rows // 2
    lanes = w_ref.shape[0]
    flat = groups * wire_rows
    parts = [part_ref[s].reshape(flat, chunk) for s in range(copies)]
    parts.append(new_ref[...].reshape(flat, chunk))
    levels = [pltpu.roll(part, flat - half, 0) for part in parts]
    top = functools.reduce(jnp.maximum, levels)
    mixture = jnp.zeros((flat, chunk), F32)
    total = jnp.zeros((flat, chunk), F32)
    for part, level in zip(parts, levels):
        share = jnp.exp(level - top)
        mixture = mixture + share * part
        total = total + share
    rows_ref[...] = mixture / total
    attended = []
    for c in range(lanes // chunk):
        start = wire_row(rows, c, 0)
        attended.append(
            jnp.concatenate(
                [
                    rows_ref[g * wire_rows + start : g * wire_rows + start + rows, :]
                    for g in range(groups)
                ],
                axis=0,
            )
        )
    attended = jnp.concatenate(attended, axis=1).astype(BF16)
    full_ref[...] = jnp.dot(attended, w_ref[...], preferred_element_type=F32)
    width = mine_ref.shape[1]
    core = lax.axis_index("tensor") % 2
    mine_ref[...] = full_ref[:, pl.ds(pl.multiple_of(core * width, LANE), width)]
    other_ref[...] = full_ref[:, pl.ds(pl.multiple_of((1 - core) * width, LANE), width)]


def mlp_kernel(
    rows, mine_ref, other_ref, gain_ref, gate_up_ref, down_ref, out_ref, resid_ref, wide_ref, by_ref
):
    batch, width = mine_ref.shape
    units = gate_up_ref.shape[2]
    core = lax.axis_index("tensor") % 2
    first = jnp.where(core == 0, mine_ref[...].astype(F32), other_ref[...].astype(F32))
    second = jnp.where(core == 0, other_ref[...].astype(F32), mine_ref[...].astype(F32))
    resid = jnp.concatenate([first, second], axis=1)
    groups = out_ref.shape[0]
    for group in range(groups):
        by_ref[group, :rows, :] = resid[group * rows : (group + 1) * rows, :]
    resid_ref[...] = by_ref[lax.axis_index("tensor"), :rows, :]
    normed = normed_rows(resid, gain_ref[...].astype(F32))
    step = 2 * LANE
    feature = lax.broadcasted_iota(jnp.int32, (step, 4 * step), 0)
    lane = lax.broadcasted_iota(jnp.int32, (step, 4 * step), 1)
    lane = jnp.where(lane < 2 * step, lane, lane - 2 * step - 1)
    spread = (2 * feature == lane).astype(F32).astype(BF16)
    pieces = 2 * width // step
    stacked = jnp.concatenate([normed[:, j * step : (j + 1) * step] for j in range(pieces)], axis=0)
    wide = jnp.dot(stacked, spread, preferred_element_type=F32).astype(BF16)
    for j in range(pieces):
        part = wide[j * batch : (j + 1) * batch, :]
        at = slice(j * 2 * step, (j + 1) * 2 * step)
        wide_ref[:batch, at] = part[:, : 2 * step]
        wide_ref[batch:, at] = part[:, 2 * step :]
    weights = gate_up_ref.reshape(4 * width, units)
    gate_up = jnp.dot(wide_ref[...], weights[...], preferred_element_type=F32)
    gate = gate_up[:batch]
    hidden = (gate * jax.nn.sigmoid(gate) * gate_up[batch:]).astype(BF16)
    out = jnp.dot(hidden, down_ref[...], preferred_element_type=F32)
    for group in range(groups):
        out_ref[group] = out[group * rows : (group + 1) * rows, :].astype(BF16)


def prepare_kernel(rows, pos_ref, cos_ref, sin_ref, query_cos_ref, query_sin_ref):
    core = lax.axis_index("tensor") % 2
    chip = lax.axis_index("tensor") // 2
    chips = query_cos_ref.shape[0] // rows
    wide = cos_ref.shape[1]
    half = HEAD_SIZE // 2
    pair = lax.broadcasted_iota(jnp.int32, (1, wide), 1) % half
    inverse = jnp.zeros((1, wide), F32)
    for i in range(half):
        inverse = jnp.where(pair == i, np.float32(ROTARY_BASE ** (-2 * i / HEAD_SIZE)), inverse)

    def turn(positions, to_cos, to_sin):
        shape = to_cos.shape
        row = lax.broadcasted_iota(jnp.int32, shape, 0)
        position = jnp.zeros(shape, F32)
        for i, one in enumerate(positions):
            position = jnp.where(row == i, one.astype(F32), position)
        angle = position * inverse
        sine = jnp.sin(angle)
        lane = lax.broadcasted_iota(jnp.int32, shape, 1)
        to_cos[...] = jnp.cos(angle)
        to_sin[...] = jnp.where(lane % HEAD_SIZE < half, -sine, sine)

    turn([pos_ref[i] for i in range(cos_ref.shape[0])], cos_ref, sin_ref)
    sources = [2 * lax.rem(chip + chips - step, chips) + core for step in range(chips)]
    turn(
        [pos_ref[source * rows + r] for source in sources for r in range(rows)],
        query_cos_ref,
        query_sin_ref,
    )


def mark_live(len_ref, pos_ref, mask_ref, slot_pos_ref, live_ref):
    rows, slots = mask_ref.shape
    slot = lax.axis_index("seq") * slots + lax.broadcasted_iota(jnp.int32, (1, slots), 1)
    first_row = lax.axis_index("tensor") * rows
    for r in range(rows):
        own_len = len_ref[first_row + r]
        own_pos = pos_ref[first_row + r]
        slot_at = slot_pos_ref[r : r + 1, :]
        live = (slot < own_len) & (mask_ref[r : r + 1, :] == 1)
        live = live & (slot_at < own_pos) & (own_pos - slot_at < WINDOW)
        live_ref[r : r + 1, :] = live.astype(jnp.int32)


def call(kernel, out, inputs, specs=None, scratch=(), limit=6, name=None, flops=0):
    return pl.pallas_call(
        kernel,
        out_shape=out,
        in_specs=specs or [VMEM_SPEC] * len(inputs),
        out_specs=jax.tree.map(lambda _: VMEM_SPEC, out),
        scratch_shapes=scratch,
        compiler_params=pltpu.CompilerParams(vmem_limit_bytes=limit * MIB),
        name=name,
        cost_estimate=pl.CostEstimate(
            flops=flops,
            bytes_accessed=sum(a.size * a.dtype.itemsize for a in inputs),
            transcendentals=0,
        ),
    )(*inputs)


def per_device(
    shards,
    groups,
    states,
    attn_gain,
    w_qkv,
    w_out,
    mlp_gain,
    w_gate_up,
    w_down,
    key_cache,
    value_cache,
    sink_keys,
    sink_values,
    cache_len,
    slot_mask,
    slot_pos,
    new_pos,
):
    rows, width = states.shape
    batch = rows * groups
    lanes = w_qkv.shape[2]
    sds = jax.ShapeDtypeStruct
    chunk = min(lanes, LANE)
    wire_rows = max(8, 2 * rows * lanes // chunk)

    chips = groups // 2
    turn = sds((batch, chunk), F32)
    query_turn = sds((batch // 2, chunk), F32)
    cosine, sine, query_cos, query_sin = call(
        functools.partial(prepare_kernel, rows),
        (turn, turn, query_turn, query_turn),
        (new_pos,),
        specs=[SMEM_SPEC],
        name="prepare",
        flops=PREP_FLOPS,
    )
    across = [(i, i ^ 1) for i in range(groups)]
    hops = [[(i, (i + step) % groups) for i in range(groups)] for step in range(2, groups, 2)]
    column = [states] + [lax.ppermute(states, "tensor", hop) for hop in hops]
    w_qkv = jnp.transpose(w_qkv, (1, 0, 2))
    w_query = w_qkv[0]
    w_query_peer = lax.ppermute(w_query, "tensor", across)
    query_wire = sds((max(8, 2 * rows * lanes // LANE), LANE), F32)
    queries = call(
        functools.partial(query_kernel, rows, chips),
        (query_wire,) * chips,
        (*column, attn_gain[None], w_query, w_query_peer, query_cos, query_sin),
        name="query",
        flops=QKV_FLOPS,
    )
    queries = [queries[0]] + [
        lax.ppermute(query, "tensor", hop) for query, hop in zip(queries[1:], hops)
    ]
    same = jnp.stack(column)
    peer = lax.ppermute(same, "tensor", across)
    side = sds((batch, width // 2), F32)
    wire = sds((groups, wire_rows, chunk), F32)
    flat = sds((batch, lanes), BF16)
    new_keys, new_values, new_part, own_side, live = call(
        functools.partial(new_token_kernel, rows),
        (flat, flat, wire, side, sds(slot_mask.shape, jnp.int32)),
        (cache_len, new_pos, slot_mask, slot_pos, same, peer, attn_gain[None], w_qkv, cosine, sine),
        specs=[SMEM_SPEC] * 2 + [VMEM_SPEC] * 8,
        scratch=[pltpu.VMEM((groups, 8, width), F32), pltpu.VMEM((batch, width), F32)],
        name="new_token",
        flops=QKV_FLOPS,
    )
    queries, new_part = lax.optimization_barrier((queries, new_part))
    sink_keys = jnp.transpose(sink_keys, (0, 2, 1))
    sink_values = jnp.transpose(sink_values, (0, 2, 1))
    part = call(
        functools.partial(attention_kernel, lanes, chips),
        sds((shards, groups, wire_rows, chunk), F32),
        (*queries, key_cache, value_cache, sink_keys, sink_values, live),
        limit=8,
        name="attention",
        flops=ATT_FLOPS,
    )
    part = lax.all_to_all(
        part.reshape(shards * groups, wire_rows, chunk), ("seq", "tensor"), 0, 0, tiled=True
    ).reshape(shards, groups, wire_rows, chunk)
    mine, other = call(
        functools.partial(merge_kernel, rows),
        (side, side),
        (part, new_part, w_out),
        scratch=[pltpu.VMEM((groups * wire_rows, chunk), F32), pltpu.VMEM((batch, width), F32)],
        name="merge",
        flops=MERGE_FLOPS,
    )
    chip = (mine + lax.ppermute(other, "tensor", across)).astype(BF16)
    total = chip.astype(F32)
    for hop in hops:
        total = total + lax.ppermute(chip, "tensor", hop).astype(F32)
    side_resid = (own_side + total).astype(BF16)
    other_resid = lax.ppermute(side_resid, "tensor", across)
    partial, own_resid = call(
        functools.partial(mlp_kernel, rows),
        (sds((groups, rows, width), BF16), sds((rows, width), F32)),
        (side_resid, other_resid, mlp_gain[None], w_gate_up, w_down),
        scratch=[pltpu.VMEM((2 * batch, 2 * width), BF16), pltpu.VMEM((groups, 8, width), F32)],
        limit=8,
        name="mlp",
        flops=6 * batch * width * w_gate_up.shape[2],
    )
    partial = lax.all_to_all(partial, "tensor", 0, 0, tiled=True)
    out_states = (own_resid + jnp.sum(partial.astype(F32), axis=0)).astype(BF16)
    return out_states, new_keys, new_values


def solution(mesh):
    in_specs = (
        P("tensor", None),
        P(),
        P(None, None, "tensor"),
        P("tensor", None),
        P(),
        P(None, None, "tensor"),
        P("tensor", None),
        P("tensor", None, "seq"),
        P("tensor", None, "seq"),
        P("tensor", None, None),
        P("tensor", None, None),
        P(),
        P("tensor", "seq"),
        P("tensor", "seq"),
        P(),
    )
    out_specs = (P("tensor", None), P(None, "tensor"), P(None, "tensor"))
    body = functools.partial(per_device, mesh.shape["seq"], mesh.shape["tensor"])
    return jax.shard_map(
        body, mesh=mesh, in_specs=in_specs, out_specs=out_specs, check_vma=False
    )
```

```python
import functools

import jax
import jax.numpy as jnp
import numpy as np
from jax import lax
from jax.experimental import pallas as pl
from jax.experimental.pallas import tpu as pltpu
from jax.sharding import PartitionSpec as P

HEAD_SIZE = 64
WINDOW = 4096
ROTARY_BASE = 130000.0
NEG = -1e30
LANE = 128
MIB = 2**20
AHEAD = 1
PREP_FLOPS = 20_000_000_000
QKV_FLOPS = 2_000_000_000
ATT_FLOPS = 10_000_000_000
MERGE_FLOPS = 10_000_000_000

VMEM_SPEC = pl.BlockSpec(memory_space=pltpu.VMEM)
SMEM_SPEC = pl.BlockSpec(memory_space=pltpu.SMEM)
F32 = jnp.float32
BF16 = jnp.bfloat16


def normed_rows(values, gain):
    meansq = jnp.mean(values * values, axis=-1, keepdims=True)
    return (values * lax.rsqrt(meansq + 1e-05) * gain).astype(BF16)


def swap_halves(tensor):
    width = tensor.shape[1]
    half = HEAD_SIZE // 2
    if width == HEAD_SIZE:
        return jnp.concatenate([tensor[:, half:], tensor[:, :half]], axis=1)
    lane = lax.broadcasted_iota(jnp.int32, tensor.shape, 1)
    upper = pltpu.roll(tensor, width - half, 1)
    lower = pltpu.roll(tensor, half, 1)
    return jnp.where(lane % HEAD_SIZE < half, upper, lower)


def wire_row(rows, lane_chunk, row):
    return lane_chunk * rows + row


def query_kernel(rows, chips, *refs):
    states, refs = refs[:chips], refs[chips:]
    gain_ref, own_ref, peer_ref, cos_ref, sin_ref = refs[:5]
    outs = refs[5:]
    core = lax.axis_index("tensor") % 2
    values = jnp.concatenate([ref[...].astype(F32) for ref in states], axis=0)
    normed = normed_rows(values, gain_ref[...].astype(F32).reshape(1, -1))
    own = jnp.dot(normed, own_ref[0], preferred_element_type=F32)
    peer = jnp.dot(normed, peer_ref[0], preferred_element_type=F32)
    queries = jnp.concatenate(
        [jnp.where(core == 0, own, peer), jnp.where(core == 0, peer, own)], axis=1
    )
    repeat = queries.shape[1] // cos_ref.shape[1]
    cosine = jnp.concatenate([cos_ref[...]] * repeat, axis=1)
    sine = jnp.concatenate([sin_ref[...]] * repeat, axis=1)
    queries = (queries * cosine + swap_halves(queries) * sine).astype(BF16).astype(F32)
    for step in range(chips):
        first = (chips - step) % chips * rows
        out = outs[step]
        if rows * queries.shape[1] // LANE < out.shape[0]:
            out[...] = jnp.zeros_like(out)
        for c in range(queries.shape[1] // LANE):
            at = slice(c * LANE, (c + 1) * LANE)
            row = wire_row(rows, c, 0)
            out[row : row + rows, :] = queries[first : first + rows, at]


def new_token_kernel(
    rows,
    len_ref,
    pos_ref,
    mask_ref,
    slot_pos_ref,
    same_ref,
    peer_ref,
    gain_ref,
    w_ref,
    cos_ref,
    sin_ref,
    k_ref,
    v_ref,
    new_ref,
    side_ref,
    live_ref,
    by_ref,
    flat_ref,
):
    mark_live(len_ref, pos_ref, mask_ref, slot_pos_ref, live_ref)
    lanes = w_ref.shape[2]
    core = lax.axis_index("tensor") % 2
    chip = lax.axis_index("tensor") // 2
    chips = same_ref.shape[0]
    for step in range(chips):
        source = 2 * lax.rem(chip + chips - step, chips)
        by_ref[source + core, :rows, :] = same_ref[step].astype(F32)
        by_ref[source + 1 - core, :rows, :] = peer_ref[step].astype(F32)
    for group in range(2 * chips):
        flat_ref[group * rows : (group + 1) * rows, :] = by_ref[group, :rows, :]
    values = flat_ref[...]
    width = side_ref.shape[1]
    side_ref[...] = flat_ref[:, pl.ds(pl.multiple_of(core * width, LANE), width)]
    normed = normed_rows(values, gain_ref[...].astype(F32).reshape(1, -1))
    repeat = lanes // cos_ref.shape[1]
    cosine = jnp.concatenate([cos_ref[...]] * repeat, axis=1)
    sine = jnp.concatenate([sin_ref[...]] * repeat, axis=1)

    def project(part):
        return jnp.dot(normed, w_ref[part], preferred_element_type=F32)

    def turned(t):
        return (t * cosine + swap_halves(t) * sine).astype(BF16)

    queries = turned(project(0))
    keys = turned(project(1))
    values = project(2).astype(BF16)
    k_ref[...] = keys
    v_ref[...] = values
    queries = queries.astype(F32)
    head_in = lax.broadcasted_iota(jnp.int32, (lanes, lanes), 0) // HEAD_SIZE
    head_out = lax.broadcasted_iota(jnp.int32, (lanes, lanes), 1) // HEAD_SIZE
    same_head = (head_in == head_out).astype(F32)
    score = jnp.dot(
        queries * keys.astype(F32),
        same_head,
        preferred_element_type=F32,
        precision=lax.Precision.HIGHEST,
    ) * (HEAD_SIZE**-0.5)
    values = values.astype(F32)
    groups, half, chunk = new_ref.shape[0], new_ref.shape[1] // 2, new_ref.shape[2]
    for group in range(groups):
        mine = slice(group * rows, (group + 1) * rows)
        for c in range(lanes // chunk):
            at = slice(c * chunk, (c + 1) * chunk)
            row = wire_row(rows, c, 0)
            new_ref[group, row : row + rows, :] = values[mine, at]
            new_ref[group, half + row : half + row + rows, :] = score[mine, at]


def attention_kernel(lanes, chips, *refs):
    queries, refs = refs[:chips], refs[chips:]
    k_ref, v_ref, sink_k_ref, sink_v_ref, live_ref, out_ref = refs
    rows, features, slots = k_ref.shape
    sinks = sink_k_ref.shape[1]
    copies = out_ref.shape[0]
    half, chunk = out_ref.shape[2] // 2, out_ref.shape[3]
    block = 2 * lanes
    heads = max(8, block // HEAD_SIZE)
    seq_index = lax.axis_index("seq")
    chip = lax.axis_index("tensor") // 2
    head = lax.broadcasted_iota(jnp.int32, (heads, block), 0)
    own = head == lax.broadcasted_iota(jnp.int32, (heads, block), 1) // HEAD_SIZE
    scale = HEAD_SIZE**-0.5
    lives = [
        jnp.broadcast_to(live_ref[r : r + 1, :], (heads, slots)) == 1 for r in range(rows)
    ]
    first_shard = seq_index == 0

    def place(step):
        source = lax.rem(chip + chips - step, chips)
        return source, pl.ds(pl.multiple_of(source * block, block), block)

    def scores(r, step):
        _, here = place(step)
        query = jnp.concatenate(
            [
                queries[step][wire_row(rows, c, r) : wire_row(rows, c, r) + 1, :]
                for c in range(block // LANE)
            ],
            axis=1,
        )
        query = jnp.where(own, jnp.broadcast_to(query, (heads, block)), 0.0)
        score = jnp.dot(query.astype(BF16), k_ref[r, here, :], preferred_element_type=F32)
        return query, score

    def mix(r, step, query, score):
        source, here = place(step)
        sink_keys = sink_k_ref[r, :, here].astype(F32)
        sink_values = sink_v_ref[r, :, here].astype(F32)
        score = jnp.where(lives[r], score * scale, NEG)
        top = jnp.max(score, axis=1, keepdims=True)
        sink_score = []
        for i in range(sinks):
            one = jnp.sum(query * sink_keys[i : i + 1, :], axis=1, keepdims=True) * scale
            one = jnp.where(first_shard, one, NEG)
            sink_score.append(one)
            top = jnp.maximum(top, one)
        weight = jnp.where(lives[r], jnp.exp(score - top), 0.0)
        mixture = lax.dot_general(
            weight.astype(BF16),
            v_ref[r, here, :],
            (((1,), (1,)), ((), ())),
            preferred_element_type=F32,
        )
        total = jnp.sum(weight, axis=1, keepdims=True)
        for i in range(sinks):
            one = jnp.where(first_shard, jnp.exp(sink_score[i] - top), 0.0)
            total = total + one
            mixture = mixture + one.astype(BF16).astype(F32) * sink_values[i : i + 1, :]
        some = total > 0.0
        level = jnp.where(some, top + jnp.log(jnp.where(some, total, 1.0)), NEG)
        mixture = mixture / jnp.where(some, total, 1.0)
        mixture = jnp.sum(jnp.where(own, mixture, 0.0), axis=0, keepdims=True)
        level = jnp.sum(jnp.where(own, level, 0.0), axis=0, keepdims=True)
        for f in range(block // chunk):
            t, c = divmod(f, lanes // chunk)
            row = wire_row(rows, c, r)
            at = slice(f * chunk, (f + 1) * chunk)
            for copy in range(copies):
                out_ref[copy, 2 * source + t, row : row + 1, :] = mixture[:, at]
                out_ref[copy, 2 * source + t, half + row : half + row + 1, :] = level[:, at]

    todo = [(r, step) for r in range(rows) for step in range(chips)]
    ahead = [scores(*one) for one in todo[:AHEAD]]
    for i, one in enumerate(todo):
        if i + AHEAD < len(todo):
            ahead.append(scores(*todo[i + AHEAD]))
        mix(*one, *ahead[i])


def merge_kernel(rows, part_ref, new_ref, w_ref, mine_ref, other_ref, rows_ref, full_ref):
    copies, groups, wire_rows, chunk = part_ref.shape
    half = wire_rows // 2
    lanes = w_ref.shape[0]
    flat = groups * wire_rows
    parts = [part_ref[s].reshape(flat, chunk) for s in range(copies)]
    parts.append(new_ref[...].reshape(flat, chunk))
    levels = [pltpu.roll(part, flat - half, 0) for part in parts]
    top = functools.reduce(jnp.maximum, levels)
    mixture = jnp.zeros((flat, chunk), F32)
    total = jnp.zeros((flat, chunk), F32)
    for part, level in zip(parts, levels):
        share = jnp.exp(level - top)
        mixture = mixture + share * part
        total = total + share
    rows_ref[...] = mixture / total
    attended = []
    for c in range(lanes // chunk):
        start = wire_row(rows, c, 0)
        attended.append(
            jnp.concatenate(
                [
                    rows_ref[g * wire_rows + start : g * wire_rows + start + rows, :]
                    for g in range(groups)
                ],
                axis=0,
            )
        )
    attended = jnp.concatenate(attended, axis=1).astype(BF16)
    full_ref[...] = jnp.dot(attended, w_ref[...], preferred_element_type=F32)
    width = mine_ref.shape[1]
    core = lax.axis_index("tensor") % 2
    mine_ref[...] = full_ref[:, pl.ds(pl.multiple_of(core * width, LANE), width)]
    other_ref[...] = full_ref[:, pl.ds(pl.multiple_of((1 - core) * width, LANE), width)]


def spread_rows(values, wide_ref):
    batch, width = values.shape
    step = 2 * LANE
    feature = lax.broadcasted_iota(jnp.int32, (step, 4 * step), 0)
    lane = lax.broadcasted_iota(jnp.int32, (step, 4 * step), 1)
    lane = jnp.where(lane < 2 * step, lane, lane - 2 * step - 1)
    spread = (2 * feature == lane).astype(F32).astype(BF16)
    pieces = width // step
    stacked = jnp.concatenate([values[:, j * step : (j + 1) * step] for j in range(pieces)], axis=0)
    wide = jnp.dot(stacked, spread, preferred_element_type=F32).astype(BF16)
    for j in range(pieces):
        part = wide[j * batch : (j + 1) * batch, :]
        at = slice(j * 2 * step, (j + 1) * 2 * step)
        wide_ref[:batch, at] = part[:, : 2 * step]
        wide_ref[batch:, at] = part[:, 2 * step :]


def half_gate_up(side, half, gain_ref, gate_up_ref, wide_ref):
    width = side.shape[1]
    units = gate_up_ref.shape[2]
    gain = gain_ref[...].astype(F32).reshape(1, -1)
    gain = jnp.where(half == 0, gain[:, :width], gain[:, width:])
    spread_rows((side * gain).astype(BF16), wide_ref)
    weights = gate_up_ref.reshape(4 * width, units)
    weights = weights[pl.ds(pl.multiple_of(half * 2 * width, 2 * width), 2 * width), :]
    gate_up = jnp.dot(wide_ref[...], weights, preferred_element_type=F32)
    return gate_up, jnp.sum(side * side, axis=1, keepdims=True)


def first_half_kernel(side_ref, gain_ref, gate_up_ref, out_ref, square_ref, wide_ref):
    core = lax.axis_index("tensor") % 2
    side = side_ref[...].astype(F32)
    out_ref[...], square = half_gate_up(side, core, gain_ref, gate_up_ref, wide_ref)
    square_ref[...] = jnp.broadcast_to(square, square_ref.shape)


def mlp_kernel(
    rows,
    mine_ref,
    other_ref,
    gain_ref,
    gate_up_ref,
    down_ref,
    first_ref,
    square_ref,
    out_ref,
    resid_ref,
    wide_ref,
    by_ref,
):
    batch, width = mine_ref.shape
    core = lax.axis_index("tensor") % 2
    mine = mine_ref[...].astype(F32)
    other = other_ref[...].astype(F32)
    gate_up, square = half_gate_up(other, 1 - core, gain_ref, gate_up_ref, wide_ref)
    meansq = (square + square_ref[:, :1]) / (2 * width)
    scale = lax.rsqrt(meansq + 1e-05)
    gate_up = gate_up + first_ref[...]
    gate = gate_up[:batch] * scale
    hidden = (gate * jax.nn.sigmoid(gate) * (gate_up[batch:] * scale)).astype(BF16)
    out = jnp.dot(hidden, down_ref[...], preferred_element_type=F32)
    resid = jnp.concatenate(
        [jnp.where(core == 0, mine, other), jnp.where(core == 0, other, mine)], axis=1
    )
    groups = out_ref.shape[0]
    for group in range(groups):
        by_ref[group, :rows, :] = resid[group * rows : (group + 1) * rows, :]
        out_ref[group] = out[group * rows : (group + 1) * rows, :].astype(BF16)
    resid_ref[...] = by_ref[lax.axis_index("tensor"), :rows, :]


def prepare_kernel(rows, pos_ref, cos_ref, sin_ref, query_cos_ref, query_sin_ref):
    core = lax.axis_index("tensor") % 2
    chip = lax.axis_index("tensor") // 2
    chips = query_cos_ref.shape[0] // rows
    wide = cos_ref.shape[1]
    half = HEAD_SIZE // 2
    pair = lax.broadcasted_iota(jnp.int32, (1, wide), 1) % half
    inverse = jnp.zeros((1, wide), F32)
    for i in range(half):
        inverse = jnp.where(pair == i, np.float32(ROTARY_BASE ** (-2 * i / HEAD_SIZE)), inverse)

    def turn(positions, to_cos, to_sin):
        shape = to_cos.shape
        row = lax.broadcasted_iota(jnp.int32, shape, 0)
        position = jnp.zeros(shape, F32)
        for i, one in enumerate(positions):
            position = jnp.where(row == i, one.astype(F32), position)
        angle = position * inverse
        sine = jnp.sin(angle)
        lane = lax.broadcasted_iota(jnp.int32, shape, 1)
        to_cos[...] = jnp.cos(angle)
        to_sin[...] = jnp.where(lane % HEAD_SIZE < half, -sine, sine)

    turn([pos_ref[i] for i in range(cos_ref.shape[0])], cos_ref, sin_ref)
    sources = [2 * lax.rem(chip + chips - step, chips) + core for step in range(chips)]
    turn(
        [pos_ref[source * rows + r] for source in sources for r in range(rows)],
        query_cos_ref,
        query_sin_ref,
    )


def mark_live(len_ref, pos_ref, mask_ref, slot_pos_ref, live_ref):
    rows, slots = mask_ref.shape
    slot = lax.axis_index("seq") * slots + lax.broadcasted_iota(jnp.int32, (1, slots), 1)
    first_row = lax.axis_index("tensor") * rows
    for r in range(rows):
        own_len = len_ref[first_row + r]
        own_pos = pos_ref[first_row + r]
        slot_at = slot_pos_ref[r : r + 1, :]
        live = (slot < own_len) & (mask_ref[r : r + 1, :] == 1)
        live = live & (slot_at < own_pos) & (own_pos - slot_at < WINDOW)
        live_ref[r : r + 1, :] = live.astype(jnp.int32)


def call(kernel, out, inputs, specs=None, scratch=(), limit=6, name=None, flops=0):
    return pl.pallas_call(
        kernel,
        out_shape=out,
        in_specs=specs or [VMEM_SPEC] * len(inputs),
        out_specs=jax.tree.map(lambda _: VMEM_SPEC, out),
        scratch_shapes=scratch,
        compiler_params=pltpu.CompilerParams(vmem_limit_bytes=limit * MIB),
        name=name,
        cost_estimate=pl.CostEstimate(
            flops=flops,
            bytes_accessed=sum(a.size * a.dtype.itemsize for a in inputs),
            transcendentals=0,
        ),
    )(*inputs)


def per_device(
    shards,
    groups,
    states,
    attn_gain,
    w_qkv,
    w_out,
    mlp_gain,
    w_gate_up,
    w_down,
    key_cache,
    value_cache,
    sink_keys,
    sink_values,
    cache_len,
    slot_mask,
    slot_pos,
    new_pos,
):
    rows, width = states.shape
    batch = rows * groups
    lanes = w_qkv.shape[2]
    sds = jax.ShapeDtypeStruct
    chunk = min(lanes, LANE)
    wire_rows = max(8, 2 * rows * lanes // chunk)

    chips = groups // 2
    turn = sds((batch, chunk), F32)
    query_turn = sds((batch // 2, chunk), F32)
    cosine, sine, query_cos, query_sin = call(
        functools.partial(prepare_kernel, rows),
        (turn, turn, query_turn, query_turn),
        (new_pos,),
        specs=[SMEM_SPEC],
        name="prepare",
        flops=PREP_FLOPS,
    )
    across = [(i, i ^ 1) for i in range(groups)]
    hops = [[(i, (i + step) % groups) for i in range(groups)] for step in range(2, groups, 2)]
    column = [states] + [lax.ppermute(states, "tensor", hop) for hop in hops]
    w_qkv = jnp.transpose(w_qkv, (1, 0, 2))
    w_peer = lax.ppermute(w_qkv, "tensor", across)
    query_wire = sds((max(8, 2 * rows * lanes // LANE), LANE), F32)
    queries = call(
        functools.partial(query_kernel, rows, chips),
        (query_wire,) * chips,
        (*column, attn_gain, w_qkv, w_peer, query_cos, query_sin),
        name="query",
        flops=QKV_FLOPS,
    )
    queries = [queries[0]] + [
        lax.ppermute(query, "tensor", hop) for query, hop in zip(queries[1:], hops)
    ]
    same = jnp.stack(column)
    peer = lax.ppermute(same, "tensor", across)
    side = sds((batch, width // 2), F32)
    wire = sds((groups, wire_rows, chunk), F32)
    flat = sds((batch, lanes), BF16)
    new_keys, new_values, new_part, own_side, live = call(
        functools.partial(new_token_kernel, rows),
        (flat, flat, wire, side, sds(slot_mask.shape, jnp.int32)),
        (cache_len, new_pos, slot_mask, slot_pos, same, peer, attn_gain, w_qkv, cosine, sine),
        specs=[SMEM_SPEC] * 2 + [VMEM_SPEC] * 8,
        scratch=[pltpu.VMEM((groups, 8, width), F32), pltpu.VMEM((batch, width), F32)],
        name="new_token",
        flops=QKV_FLOPS,
    )
    queries, new_part = lax.optimization_barrier((queries, new_part))
    sink_keys = jnp.transpose(sink_keys, (0, 2, 1))
    sink_values = jnp.transpose(sink_values, (0, 2, 1))
    part = call(
        functools.partial(attention_kernel, lanes, chips),
        sds((shards, groups, wire_rows, chunk), F32),
        (*queries, key_cache, value_cache, sink_keys, sink_values, live),
        limit=8,
        name="attention",
        flops=ATT_FLOPS,
    )
    part = lax.all_to_all(
        part.reshape(shards * groups, wire_rows, chunk), ("seq", "tensor"), 0, 0, tiled=True
    ).reshape(shards, groups, wire_rows, chunk)
    mine, other = call(
        functools.partial(merge_kernel, rows),
        (side, side),
        (part, new_part, w_out),
        scratch=[pltpu.VMEM((groups * wire_rows, chunk), F32), pltpu.VMEM((batch, width), F32)],
        name="merge",
        flops=MERGE_FLOPS,
    )
    chip = (mine + lax.ppermute(other, "tensor", across)).astype(BF16)
    total = chip.astype(F32)
    for hop in hops:
        total = total + lax.ppermute(chip, "tensor", hop).astype(F32)
    side_resid = (own_side + total).astype(BF16)
    other_resid = lax.ppermute(side_resid, "tensor", across)
    units = w_gate_up.shape[2]
    first_half, square = call(
        first_half_kernel,
        (sds((2 * batch, units), F32), sds((batch, LANE), F32)),
        (side_resid, mlp_gain, w_gate_up),
        scratch=[pltpu.VMEM((2 * batch, width), BF16)],
        limit=8,
        name="first_half",
        flops=2 * batch * width * units,
    )
    partial, own_resid = call(
        functools.partial(mlp_kernel, rows),
        (sds((groups, rows, width), BF16), sds((rows, width), F32)),
        (side_resid, other_resid, mlp_gain, w_gate_up, w_down, first_half, square),
        scratch=[pltpu.VMEM((2 * batch, width), BF16), pltpu.VMEM((groups, 8, width), F32)],
        limit=8,
        name="mlp",
        flops=4 * batch * width * units,
    )
    partial = lax.all_to_all(partial, "tensor", 0, 0, tiled=True)
    out_states = (own_resid + jnp.sum(partial.astype(F32), axis=0)).astype(BF16)
    return out_states, new_keys, new_values


def solution(mesh):
    in_specs = (
        P("tensor", None),
        P(),
        P(None, None, "tensor"),
        P("tensor", None),
        P(),
        P(None, None, "tensor"),
        P("tensor", None),
        P("tensor", None, "seq"),
        P("tensor", None, "seq"),
        P("tensor", None, None),
        P("tensor", None, None),
        P(),
        P("tensor", "seq"),
        P("tensor", "seq"),
        P(),
    )
    out_specs = (P("tensor", None), P(None, "tensor"), P(None, "tensor"))
    body = functools.partial(per_device, mesh.shape["seq"], mesh.shape["tensor"])
    return jax.shard_map(
        body, mesh=mesh, in_specs=in_specs, out_specs=out_specs, check_vma=False
    )
```

```python
import functools

import jax
import jax.numpy as jnp
import numpy as np
from jax import lax
from jax.experimental import pallas as pl
from jax.experimental.pallas import tpu as pltpu
from jax.sharding import PartitionSpec as P

HEAD_SIZE = 64
WINDOW = 4096
ROTARY_BASE = 130000.0
NEG = -1e30
LANE = 128
MIB = 2**20
AHEAD = 1
PREP_FLOPS = 20_000_000_000
QKV_FLOPS = 2_000_000_000
ATT_FLOPS = 10_000_000_000
MERGE_FLOPS = 10_000_000_000

VMEM_SPEC = pl.BlockSpec(memory_space=pltpu.VMEM)
SMEM_SPEC = pl.BlockSpec(memory_space=pltpu.SMEM)
F32 = jnp.float32
BF16 = jnp.bfloat16


def normed_rows(values, gain):
    meansq = jnp.mean(values * values, axis=-1, keepdims=True)
    return (values * lax.rsqrt(meansq + 1e-05) * gain).astype(BF16)


def swap_halves(tensor):
    width = tensor.shape[1]
    half = HEAD_SIZE // 2
    if width == HEAD_SIZE:
        return jnp.concatenate([tensor[:, half:], tensor[:, :half]], axis=1)
    lane = lax.broadcasted_iota(jnp.int32, tensor.shape, 1)
    upper = pltpu.roll(tensor, width - half, 1)
    lower = pltpu.roll(tensor, half, 1)
    return jnp.where(lane % HEAD_SIZE < half, upper, lower)


def wire_row(rows, lane_chunk, row):
    return lane_chunk * rows + row


def query_kernel(rows, chips, *refs):
    states, refs = refs[:chips], refs[chips:]
    gain_ref, own_ref, peer_ref, cos_ref, sin_ref = refs[:5]
    outs = refs[5:]
    core = lax.axis_index("tensor") % 2
    values = jnp.concatenate([ref[...].astype(F32) for ref in states], axis=0)
    normed = normed_rows(values, gain_ref[...].astype(F32).reshape(1, -1))
    own = jnp.dot(normed, own_ref[0], preferred_element_type=F32)
    peer = jnp.dot(normed, peer_ref[0], preferred_element_type=F32)
    queries = jnp.concatenate(
        [jnp.where(core == 0, own, peer), jnp.where(core == 0, peer, own)], axis=1
    )
    count, repeat = queries.shape[0], queries.shape[1] // cos_ref.shape[1]
    cosine = jnp.concatenate([cos_ref[:count, :]] * repeat, axis=1)
    sine = jnp.concatenate([sin_ref[:count, :]] * repeat, axis=1)
    queries = (queries * cosine + swap_halves(queries) * sine).astype(BF16).astype(F32)
    for step in range(chips):
        first = (chips - step) % chips * rows
        out = outs[step]
        if rows * queries.shape[1] // LANE < out.shape[0]:
            out[...] = jnp.zeros_like(out)
        for c in range(queries.shape[1] // LANE):
            at = slice(c * LANE, (c + 1) * LANE)
            row = wire_row(rows, c, 0)
            out[row : row + rows, :] = queries[first : first + rows, at]


def chip_away(step, chips):
    return lax.rem(lax.axis_index("tensor") // 2 + chips - step, chips)


def new_token_kernel(
    rows,
    len_ref,
    pos_ref,
    mask_ref,
    slot_pos_ref,
    same_ref,
    peer_ref,
    gain_ref,
    w_ref,
    cos_ref,
    sin_ref,
    new_ref,
    key_ref,
    live_ref,
):
    mark_live(len_ref, pos_ref, mask_ref, slot_pos_ref, live_ref)
    lanes = w_ref.shape[2]
    core = lax.axis_index("tensor") % 2
    chips = same_ref.shape[0]
    values = jnp.concatenate(
        [ref[step].astype(F32) for ref in (same_ref, peer_ref) for step in range(chips)], axis=0
    )
    normed = normed_rows(values, gain_ref[...].astype(F32).reshape(1, -1))
    repeat = lanes // cos_ref.shape[1]
    cosine = jnp.concatenate([cos_ref[...]] * repeat, axis=1)
    sine = jnp.concatenate([sin_ref[...]] * repeat, axis=1)

    def project(part):
        return jnp.dot(normed, w_ref[part], preferred_element_type=F32)

    def turned(t):
        return (t * cosine + swap_halves(t) * sine).astype(BF16).astype(F32)

    queries = turned(project(0))
    keys = turned(project(1))
    values = project(2).astype(BF16).astype(F32)
    head_in = lax.broadcasted_iota(jnp.int32, (lanes, lanes), 0) // HEAD_SIZE
    head_out = lax.broadcasted_iota(jnp.int32, (lanes, lanes), 1) // HEAD_SIZE
    same_head = (head_in == head_out).astype(F32)
    score = jnp.dot(
        queries * keys,
        same_head,
        preferred_element_type=F32,
        precision=lax.Precision.HIGHEST,
    ) * (HEAD_SIZE**-0.5)
    half, chunk = new_ref.shape[1] // 2, new_ref.shape[2]
    for i in range(2 * chips):
        group = 2 * chip_away(i % chips, chips) + (core if i < chips else 1 - core)
        mine = slice(i * rows, (i + 1) * rows)
        for c in range(lanes // chunk):
            at = slice(c * chunk, (c + 1) * chunk)
            row = wire_row(rows, c, 0)
            new_ref[group, row : row + rows, :] = values[mine, at]
            new_ref[group, half + row : half + row + rows, :] = score[mine, at]
            key_ref[group, row : row + rows, :] = keys[mine, at]


def outputs_kernel(same_ref, peer_ref, new_ref, key_ref, k_ref, v_ref, side_ref, by_ref, flat_ref):
    chips, rows, _ = same_ref.shape
    core = lax.axis_index("tensor") % 2
    for step in range(chips):
        source = 2 * chip_away(step, chips)
        by_ref[source + core, :rows, :] = same_ref[step].astype(F32)
        by_ref[source + 1 - core, :rows, :] = peer_ref[step].astype(F32)
    for group in range(2 * chips):
        flat_ref[group * rows : (group + 1) * rows, :] = by_ref[group, :rows, :]
    width = side_ref.shape[1]
    side_ref[...] = flat_ref[:, pl.ds(pl.multiple_of(core * width, LANE), width)]
    lanes, chunk = k_ref.shape[1], new_ref.shape[2]
    for from_ref, to_ref in ((key_ref, k_ref), (new_ref, v_ref)):
        parts = []
        for c in range(lanes // chunk):
            row = wire_row(rows, c, 0)
            parts.append(
                jnp.concatenate(
                    [from_ref[group, row : row + rows, :] for group in range(2 * chips)], axis=0
                )
            )
        to_ref[...] = jnp.concatenate(parts, axis=1).astype(BF16)


def attention_kernel(lanes, chips, steps, *refs):
    queries, refs = dict(zip(steps, refs)), refs[len(steps) :]
    k_ref, v_ref, sink_k_ref, sink_v_ref, live_ref = refs[:5]
    out_ref = refs[-1]
    rows, features, slots = k_ref.shape
    sinks = sink_k_ref.shape[1]
    copies = out_ref.shape[0]
    half, chunk = out_ref.shape[2] // 2, out_ref.shape[3]
    block = 2 * lanes
    heads = max(8, block // HEAD_SIZE)
    seq_index = lax.axis_index("seq")
    chip = lax.axis_index("tensor") // 2
    head = lax.broadcasted_iota(jnp.int32, (heads, block), 0)
    own = head == lax.broadcasted_iota(jnp.int32, (heads, block), 1) // HEAD_SIZE
    scale = HEAD_SIZE**-0.5
    lives = [
        jnp.broadcast_to(live_ref[r : r + 1, :], (heads, slots)) == 1 for r in range(rows)
    ]
    first_shard = seq_index == 0

    def place(step):
        source = lax.rem(chip + chips - step, chips)
        return source, pl.ds(pl.multiple_of(source * block, block), block)

    def scores(r, step):
        _, here = place(step)
        query = jnp.concatenate(
            [
                queries[step][wire_row(rows, c, r) : wire_row(rows, c, r) + 1, :]
                for c in range(block // LANE)
            ],
            axis=1,
        )
        query = jnp.where(own, jnp.broadcast_to(query, (heads, block)), 0.0)
        score = jnp.dot(query.astype(BF16), k_ref[r, here, :], preferred_element_type=F32)
        return query, score

    def mix(r, step, query, score):
        source, here = place(step)
        sink_keys = sink_k_ref[r, :, here].astype(F32)
        sink_values = sink_v_ref[r, :, here].astype(F32)
        score = jnp.where(lives[r], score * scale, NEG)
        top = jnp.max(score, axis=1, keepdims=True)
        sink_score = []
        for i in range(sinks):
            one = jnp.sum(query * sink_keys[i : i + 1, :], axis=1, keepdims=True) * scale
            one = jnp.where(first_shard, one, NEG)
            sink_score.append(one)
            top = jnp.maximum(top, one)
        weight = jnp.where(lives[r], jnp.exp(score - top), 0.0)
        mixture = lax.dot_general(
            weight.astype(BF16),
            v_ref[r, here, :],
            (((1,), (1,)), ((), ())),
            preferred_element_type=F32,
        )
        total = jnp.sum(weight, axis=1, keepdims=True)
        for i in range(sinks):
            one = jnp.where(first_shard, jnp.exp(sink_score[i] - top), 0.0)
            total = total + one
            mixture = mixture + one.astype(BF16).astype(F32) * sink_values[i : i + 1, :]
        some = total > 0.0
        level = jnp.where(some, top + jnp.log(jnp.where(some, total, 1.0)), NEG)
        mixture = mixture / jnp.where(some, total, 1.0)
        mixture = jnp.sum(jnp.where(own, mixture, 0.0), axis=0, keepdims=True)
        level = jnp.sum(jnp.where(own, level, 0.0), axis=0, keepdims=True)
        for f in range(block // chunk):
            t, c = divmod(f, lanes // chunk)
            row = wire_row(rows, c, r)
            at = slice(f * chunk, (f + 1) * chunk)
            for copy in range(copies):
                out_ref[copy, 2 * source + t, row : row + 1, :] = mixture[:, at]
                out_ref[copy, 2 * source + t, half + row : half + row + 1, :] = level[:, at]

    todo = [(r, step) for step in steps for r in range(rows)]
    ahead = [scores(*one) for one in todo[:AHEAD]]
    for i, one in enumerate(todo):
        if i + AHEAD < len(todo):
            ahead.append(scores(*todo[i + AHEAD]))
        mix(*one, *ahead[i])


def merge_kernel(rows, part_ref, new_ref, w_ref, mine_ref, other_ref, rows_ref, full_ref):
    copies, groups, wire_rows, chunk = part_ref.shape
    half = wire_rows // 2
    lanes = w_ref.shape[0]
    flat = groups * wire_rows
    parts = [part_ref[s].reshape(flat, chunk) for s in range(copies)]
    parts.append(new_ref[...].reshape(flat, chunk))
    levels = [pltpu.roll(part, flat - half, 0) for part in parts]
    top = functools.reduce(jnp.maximum, levels)
    mixture = jnp.zeros((flat, chunk), F32)
    total = jnp.zeros((flat, chunk), F32)
    for part, level in zip(parts, levels):
        share = jnp.exp(level - top)
        mixture = mixture + share * part
        total = total + share
    rows_ref[...] = mixture / total
    attended = []
    for c in range(lanes // chunk):
        start = wire_row(rows, c, 0)
        attended.append(
            jnp.concatenate(
                [
                    rows_ref[g * wire_rows + start : g * wire_rows + start + rows, :]
                    for g in range(groups)
                ],
                axis=0,
            )
        )
    attended = jnp.concatenate(attended, axis=1).astype(BF16)
    full_ref[...] = jnp.dot(attended, w_ref[...], preferred_element_type=F32)
    width = mine_ref.shape[1]
    core = lax.axis_index("tensor") % 2
    mine_ref[...] = full_ref[:, pl.ds(pl.multiple_of(core * width, LANE), width)]
    other_ref[...] = full_ref[:, pl.ds(pl.multiple_of((1 - core) * width, LANE), width)]


def spread_rows(values, wide_ref):
    batch, width = values.shape
    step = 2 * LANE
    feature = lax.broadcasted_iota(jnp.int32, (step, 4 * step), 0)
    lane = lax.broadcasted_iota(jnp.int32, (step, 4 * step), 1)
    lane = jnp.where(lane < 2 * step, lane, lane - 2 * step - 1)
    spread = (2 * feature == lane).astype(F32).astype(BF16)
    pieces = width // step
    stacked = jnp.concatenate([values[:, j * step : (j + 1) * step] for j in range(pieces)], axis=0)
    wide = jnp.dot(stacked, spread, preferred_element_type=F32).astype(BF16)
    for j in range(pieces):
        part = wide[j * batch : (j + 1) * batch, :]
        at = slice(j * 2 * step, (j + 1) * 2 * step)
        wide_ref[:batch, at] = part[:, : 2 * step]
        wide_ref[batch:, at] = part[:, 2 * step :]


def half_gate_up(side, half, gain_ref, gate_up_ref, wide_ref):
    width = side.shape[1]
    units = gate_up_ref.shape[2]
    gain = gain_ref[...].astype(F32).reshape(1, -1)
    gain = jnp.where(half == 0, gain[:, :width], gain[:, width:])
    spread_rows((side * gain).astype(BF16), wide_ref)
    weights = gate_up_ref.reshape(4 * width, units)
    weights = weights[pl.ds(pl.multiple_of(half * 2 * width, 2 * width), 2 * width), :]
    gate_up = jnp.dot(wide_ref[...], weights, preferred_element_type=F32)
    return gate_up, jnp.sum(side * side, axis=1, keepdims=True)


def first_half_kernel(side_ref, gain_ref, gate_up_ref, out_ref, square_ref, wide_ref):
    core = lax.axis_index("tensor") % 2
    side = side_ref[...].astype(F32)
    out_ref[...], square = half_gate_up(side, core, gain_ref, gate_up_ref, wide_ref)
    square_ref[...] = jnp.broadcast_to(square, square_ref.shape)


def mlp_kernel(
    rows,
    mine_ref,
    other_ref,
    gain_ref,
    gate_up_ref,
    down_ref,
    first_ref,
    square_ref,
    out_ref,
    resid_ref,
    wide_ref,
    by_ref,
):
    batch, width = mine_ref.shape
    core = lax.axis_index("tensor") % 2
    mine = mine_ref[...].astype(F32)
    other = other_ref[...].astype(F32)
    gate_up, square = half_gate_up(other, 1 - core, gain_ref, gate_up_ref, wide_ref)
    meansq = (square + square_ref[:, :1]) / (2 * width)
    scale = lax.rsqrt(meansq + 1e-05)
    gate_up = gate_up + first_ref[...]
    gate = gate_up[:batch] * scale
    hidden = (gate * jax.nn.sigmoid(gate) * (gate_up[batch:] * scale)).astype(BF16)
    out = jnp.dot(hidden, down_ref[...], preferred_element_type=F32)
    resid = jnp.concatenate(
        [jnp.where(core == 0, mine, other), jnp.where(core == 0, other, mine)], axis=1
    )
    groups = out_ref.shape[0]
    for group in range(groups):
        by_ref[group, :rows, :] = resid[group * rows : (group + 1) * rows, :]
        out_ref[group] = out[group * rows : (group + 1) * rows, :].astype(BF16)
    resid_ref[...] = by_ref[lax.axis_index("tensor"), :rows, :]


def prepare_kernel(rows, pos_ref, cos_ref, sin_ref):
    core = lax.axis_index("tensor") % 2
    chips = cos_ref.shape[0] // (2 * rows)
    wide = cos_ref.shape[1]
    half = HEAD_SIZE // 2
    pair = lax.broadcasted_iota(jnp.int32, (1, wide), 1) % half
    inverse = jnp.zeros((1, wide), F32)
    for i in range(half):
        inverse = jnp.where(pair == i, np.float32(ROTARY_BASE ** (-2 * i / HEAD_SIZE)), inverse)

    shape = cos_ref.shape
    row = lax.broadcasted_iota(jnp.int32, shape, 0)
    position = jnp.zeros(shape, F32)
    for i in range(shape[0]):
        group, r = divmod(i, rows)
        parity = core if group < chips else 1 - core
        request = (2 * chip_away(group % chips, chips) + parity) * rows + r
        position = jnp.where(row == i, pos_ref[request].astype(F32), position)
    angle = position * inverse
    sine = jnp.sin(angle)
    lane = lax.broadcasted_iota(jnp.int32, shape, 1)
    cos_ref[...] = jnp.cos(angle)
    sin_ref[...] = jnp.where(lane % HEAD_SIZE < half, -sine, sine)


def mark_live(len_ref, pos_ref, mask_ref, slot_pos_ref, live_ref):
    rows, slots = mask_ref.shape
    slot = lax.axis_index("seq") * slots + lax.broadcasted_iota(jnp.int32, (1, slots), 1)
    first_row = lax.axis_index("tensor") * rows
    for r in range(rows):
        own_len = len_ref[first_row + r]
        own_pos = pos_ref[first_row + r]
        slot_at = slot_pos_ref[r : r + 1, :]
        live = (slot < own_len) & (mask_ref[r : r + 1, :] == 1)
        live = live & (slot_at < own_pos) & (own_pos - slot_at < WINDOW)
        live_ref[r : r + 1, :] = live.astype(jnp.int32)


def call(kernel, out, inputs, specs=None, scratch=(), limit=6, name=None, flops=0, aliases={}):
    return pl.pallas_call(
        kernel,
        out_shape=out,
        in_specs=specs or [VMEM_SPEC] * len(inputs),
        out_specs=jax.tree.map(lambda _: VMEM_SPEC, out),
        scratch_shapes=scratch,
        input_output_aliases=aliases,
        compiler_params=pltpu.CompilerParams(vmem_limit_bytes=limit * MIB),
        name=name,
        cost_estimate=pl.CostEstimate(
            flops=flops,
            bytes_accessed=sum(a.size * a.dtype.itemsize for a in inputs),
            transcendentals=0,
        ),
    )(*inputs)


def per_device(
    shards,
    groups,
    states,
    attn_gain,
    w_qkv,
    w_out,
    mlp_gain,
    w_gate_up,
    w_down,
    key_cache,
    value_cache,
    sink_keys,
    sink_values,
    cache_len,
    slot_mask,
    slot_pos,
    new_pos,
):
    rows, width = states.shape
    batch = rows * groups
    lanes = w_qkv.shape[2]
    sds = jax.ShapeDtypeStruct
    chunk = min(lanes, LANE)
    wire_rows = max(8, 2 * rows * lanes // chunk)

    chips = groups // 2
    turn = sds((batch, chunk), F32)
    cosine, sine = call(
        functools.partial(prepare_kernel, rows),
        (turn, turn),
        (new_pos,),
        specs=[SMEM_SPEC],
        name="prepare",
        flops=PREP_FLOPS,
    )
    across = [(i, i ^ 1) for i in range(groups)]
    hops = [[(i, (i + step) % groups) for i in range(groups)] for step in range(2, groups, 2)]
    column = [states] + [lax.ppermute(states, "tensor", hop) for hop in hops]
    w_qkv = jnp.transpose(w_qkv, (1, 0, 2))
    w_peer = lax.ppermute(w_qkv, "tensor", across)
    query_wire = sds((max(8, 2 * rows * lanes // LANE), LANE), F32)
    queries = call(
        functools.partial(query_kernel, rows, chips),
        (query_wire,) * chips,
        (*column, attn_gain, w_qkv, w_peer, cosine, sine),
        name="query",
        flops=QKV_FLOPS,
    )
    same = jnp.stack(column)
    peer = lax.ppermute(same, "tensor", across)
    same, *queries = lax.optimization_barrier((same, *queries))
    queries = [queries[0]] + [
        lax.ppermute(query, "tensor", hop) for query, hop in zip(queries[1:], hops)
    ]
    wire = sds((groups, wire_rows, chunk), F32)
    new_part, key_part, live = call(
        functools.partial(new_token_kernel, rows),
        (wire, wire, sds(slot_mask.shape, jnp.int32)),
        (cache_len, new_pos, slot_mask, slot_pos, same, peer, attn_gain, w_qkv, cosine, sine),
        specs=[SMEM_SPEC] * 2 + [VMEM_SPEC] * 8,
        name="new_token",
        flops=QKV_FLOPS,
    )
    sink_keys = jnp.transpose(sink_keys, (0, 2, 1))
    sink_values = jnp.transpose(sink_values, (0, 2, 1))

    def attention(steps, arrays, aliases, name):
        return call(
            functools.partial(attention_kernel, lanes, chips, steps),
            sds((shards, groups, wire_rows, chunk), F32),
            arrays,
            limit=8,
            name=name,
            flops=ATT_FLOPS,
            aliases=aliases,
        )

    cache = (key_cache, value_cache, sink_keys, sink_values, live)
    part = attention((0,), (queries[0], *cache), {}, "own_heads")
    queries, new_part, part = lax.optimization_barrier((queries, new_part, part))
    part = attention(
        tuple(range(1, chips)), (*queries[1:], *cache, part), {chips + 4: 0}, "other_heads"
    )
    part = lax.all_to_all(
        part.reshape(shards * groups, wire_rows, chunk), ("seq", "tensor"), 0, 0, tiled=True
    ).reshape(shards, groups, wire_rows, chunk)
    side = sds((batch, width // 2), F32)
    mine, other = call(
        functools.partial(merge_kernel, rows),
        (side, side),
        (part, new_part, w_out),
        scratch=[pltpu.VMEM((groups * wire_rows, chunk), F32), pltpu.VMEM((batch, width), F32)],
        name="merge",
        flops=MERGE_FLOPS,
    )
    chip = (mine + lax.ppermute(other, "tensor", across)).astype(BF16)
    flat = sds((batch, lanes), BF16)
    chip, same, peer, new_part, key_part = lax.optimization_barrier(
        (chip, same, peer, new_part, key_part)
    )
    new_keys, new_values, own_side = call(
        outputs_kernel,
        (flat, flat, side),
        (same, peer, new_part, key_part),
        scratch=[pltpu.VMEM((groups, 8, width), F32), pltpu.VMEM((batch, width), F32)],
        name="outputs",
    )
    total = chip.astype(F32)
    for hop in hops:
        total = total + lax.ppermute(chip, "tensor", hop).astype(F32)
    side_resid = (own_side + total).astype(BF16)
    other_resid = lax.ppermute(side_resid, "tensor", across)
    units = w_gate_up.shape[2]
    first_half, square = call(
        first_half_kernel,
        (sds((2 * batch, units), F32), sds((batch, LANE), F32)),
        (side_resid, mlp_gain, w_gate_up),
        scratch=[pltpu.VMEM((2 * batch, width), BF16)],
        limit=8,
        name="first_half",
        flops=2 * batch * width * units,
    )
    partial, own_resid = call(
        functools.partial(mlp_kernel, rows),
        (sds((groups, rows, width), BF16), sds((rows, width), F32)),
        (side_resid, other_resid, mlp_gain, w_gate_up, w_down, first_half, square),
        scratch=[pltpu.VMEM((2 * batch, width), BF16), pltpu.VMEM((groups, 8, width), F32)],
        limit=8,
        name="mlp",
        flops=4 * batch * width * units,
    )
    partial = lax.all_to_all(partial, "tensor", 0, 0, tiled=True)
    out_states = (own_resid + jnp.sum(partial.astype(F32), axis=0)).astype(BF16)
    return out_states, new_keys, new_values


def solution(mesh):
    in_specs = (
        P("tensor", None),
        P(),
        P(None, None, "tensor"),
        P("tensor", None),
        P(),
        P(None, None, "tensor"),
        P("tensor", None),
        P("tensor", None, "seq"),
        P("tensor", None, "seq"),
        P("tensor", None, None),
        P("tensor", None, None),
        P(),
        P("tensor", "seq"),
        P("tensor", "seq"),
        P(),
    )
    out_specs = (P("tensor", None), P(None, "tensor"), P(None, "tensor"))
    body = functools.partial(per_device, mesh.shape["seq"], mesh.shape["tensor"])
    return jax.shard_map(
        body, mesh=mesh, in_specs=in_specs, out_specs=out_specs, check_vma=False
    )
```

```python
import functools

import jax
import jax.numpy as jnp
import numpy as np
from jax import lax
from jax.experimental import pallas as pl
from jax.experimental.pallas import tpu as pltpu
from jax.sharding import PartitionSpec as P

HEAD_SIZE = 64
WINDOW = 4096
ROTARY_BASE = 130000.0
NEG = -1e30
LANE = 128
MIB = 2**20
AHEAD = 1
PREP_FLOPS = 20_000_000_000
QKV_FLOPS = 2_000_000_000
ATT_FLOPS = 10_000_000_000
MERGE_FLOPS = 10_000_000_000

VMEM_SPEC = pl.BlockSpec(memory_space=pltpu.VMEM)
SMEM_SPEC = pl.BlockSpec(memory_space=pltpu.SMEM)
F32 = jnp.float32
BF16 = jnp.bfloat16


def normed_rows(values, gain):
    meansq = jnp.mean(values * values, axis=-1, keepdims=True)
    return (values * lax.rsqrt(meansq + 1e-05) * gain).astype(BF16)


def swap_halves(tensor):
    width = tensor.shape[1]
    half = HEAD_SIZE // 2
    if width == HEAD_SIZE:
        return jnp.concatenate([tensor[:, half:], tensor[:, :half]], axis=1)
    lane = lax.broadcasted_iota(jnp.int32, tensor.shape, 1)
    upper = pltpu.roll(tensor, width - half, 1)
    lower = pltpu.roll(tensor, half, 1)
    return jnp.where(lane % HEAD_SIZE < half, upper, lower)


def wire_row(rows, lane_chunk, row):
    return lane_chunk * rows + row


def query_kernel(rows, chips, *refs):
    states, refs = refs[:chips], refs[chips:]
    gain_ref, own_ref, peer_ref, cos_ref, sin_ref = refs[:5]
    outs = refs[5:]
    core = lax.axis_index("tensor") % 2
    values = jnp.concatenate([ref[...].astype(F32) for ref in states], axis=0)
    normed = normed_rows(values, gain_ref[...].astype(F32).reshape(1, -1))
    own = jnp.dot(normed, own_ref[0], preferred_element_type=F32)
    peer = jnp.dot(normed, peer_ref[0], preferred_element_type=F32)
    queries = jnp.concatenate(
        [jnp.where(core == 0, own, peer), jnp.where(core == 0, peer, own)], axis=1
    )
    count, repeat = queries.shape[0], queries.shape[1] // cos_ref.shape[1]
    cosine = jnp.concatenate([cos_ref[:count, :]] * repeat, axis=1)
    sine = jnp.concatenate([sin_ref[:count, :]] * repeat, axis=1)
    queries = (queries * cosine + swap_halves(queries) * sine).astype(BF16).astype(F32)
    for step in range(chips):
        first = (chips - step) % chips * rows
        out = outs[step]
        if rows * queries.shape[1] // LANE < out.shape[0]:
            out[...] = jnp.zeros_like(out)
        for c in range(queries.shape[1] // LANE):
            at = slice(c * LANE, (c + 1) * LANE)
            row = wire_row(rows, c, 0)
            out[row : row + rows, :] = queries[first : first + rows, at]


def chip_away(step, chips):
    return lax.rem(lax.axis_index("tensor") // 2 + chips - step, chips)


def new_token_kernel(
    rows,
    len_ref,
    pos_ref,
    mask_ref,
    slot_pos_ref,
    same_ref,
    peer_ref,
    gain_ref,
    w_ref,
    cos_ref,
    sin_ref,
    new_ref,
    key_ref,
    live_ref,
):
    mark_live(len_ref, pos_ref, mask_ref, slot_pos_ref, live_ref)
    lanes = w_ref.shape[2]
    core = lax.axis_index("tensor") % 2
    chips = same_ref.shape[0]
    values = jnp.concatenate(
        [ref[step].astype(F32) for ref in (same_ref, peer_ref) for step in range(chips)], axis=0
    )
    normed = normed_rows(values, gain_ref[...].astype(F32).reshape(1, -1))
    repeat = lanes // cos_ref.shape[1]
    cosine = jnp.concatenate([cos_ref[...]] * repeat, axis=1)
    sine = jnp.concatenate([sin_ref[...]] * repeat, axis=1)

    def project(part):
        return jnp.dot(normed, w_ref[part], preferred_element_type=F32)

    def turned(t):
        return (t * cosine + swap_halves(t) * sine).astype(BF16).astype(F32)

    queries = turned(project(0))
    keys = turned(project(1))
    values = project(2).astype(BF16).astype(F32)
    head_in = lax.broadcasted_iota(jnp.int32, (lanes, lanes), 0) // HEAD_SIZE
    head_out = lax.broadcasted_iota(jnp.int32, (lanes, lanes), 1) // HEAD_SIZE
    same_head = (head_in == head_out).astype(F32)
    score = jnp.dot(
        queries * keys,
        same_head,
        preferred_element_type=F32,
        precision=lax.Precision.HIGHEST,
    ) * (HEAD_SIZE**-0.5)
    half, chunk = new_ref.shape[1] // 2, new_ref.shape[2]
    for i in range(2 * chips):
        group = 2 * chip_away(i % chips, chips) + (core if i < chips else 1 - core)
        mine = slice(i * rows, (i + 1) * rows)
        for c in range(lanes // chunk):
            at = slice(c * chunk, (c + 1) * chunk)
            row = wire_row(rows, c, 0)
            new_ref[group, row : row + rows, :] = values[mine, at]
            new_ref[group, half + row : half + row + rows, :] = score[mine, at]
            key_ref[group, row : row + rows, :] = keys[mine, at]


def outputs_kernel(same_ref, peer_ref, new_ref, key_ref, k_ref, v_ref, side_ref, by_ref, flat_ref):
    chips, rows, _ = same_ref.shape
    core = lax.axis_index("tensor") % 2
    for step in range(chips):
        source = 2 * chip_away(step, chips)
        by_ref[source + core, :rows, :] = same_ref[step].astype(F32)
        by_ref[source + 1 - core, :rows, :] = peer_ref[step].astype(F32)
    for group in range(2 * chips):
        flat_ref[group * rows : (group + 1) * rows, :] = by_ref[group, :rows, :]
    width = side_ref.shape[1]
    side_ref[...] = flat_ref[:, pl.ds(pl.multiple_of(core * width, LANE), width)]
    lanes, chunk = k_ref.shape[1], new_ref.shape[2]
    for from_ref, to_ref in ((key_ref, k_ref), (new_ref, v_ref)):
        parts = []
        for c in range(lanes // chunk):
            row = wire_row(rows, c, 0)
            parts.append(
                jnp.concatenate(
                    [from_ref[group, row : row + rows, :] for group in range(2 * chips)], axis=0
                )
            )
        to_ref[...] = jnp.concatenate(parts, axis=1).astype(BF16)


def attention_kernel(lanes, chips, steps, *refs):
    queries, refs = dict(zip(steps, refs)), refs[len(steps) :]
    k_ref, v_ref, sink_k_ref, sink_v_ref, live_ref = refs[:5]
    out_ref = refs[-1]
    rows, features, slots = k_ref.shape
    sinks = sink_k_ref.shape[1]
    copies = out_ref.shape[0]
    half, chunk = out_ref.shape[2] // 2, out_ref.shape[3]
    block = 2 * lanes
    heads = max(8, block // HEAD_SIZE)
    seq_index = lax.axis_index("seq")
    chip = lax.axis_index("tensor") // 2
    head = lax.broadcasted_iota(jnp.int32, (heads, block), 0)
    own = head == lax.broadcasted_iota(jnp.int32, (heads, block), 1) // HEAD_SIZE
    scale = HEAD_SIZE**-0.5
    lives = [
        jnp.broadcast_to(live_ref[r : r + 1, :], (heads, slots)) == 1 for r in range(rows)
    ]
    first_shard = seq_index == 0

    def place(step):
        source = lax.rem(chip + chips - step, chips)
        return source, pl.ds(pl.multiple_of(source * block, block), block)

    def scores(r, step):
        _, here = place(step)
        query = jnp.concatenate(
            [
                queries[step][wire_row(rows, c, r) : wire_row(rows, c, r) + 1, :]
                for c in range(block // LANE)
            ],
            axis=1,
        )
        query = jnp.where(own, jnp.broadcast_to(query, (heads, block)), 0.0)
        score = jnp.dot(query.astype(BF16), k_ref[r, here, :], preferred_element_type=F32)
        return query, score

    def mix(r, step, query, score):
        source, here = place(step)
        sink_keys = sink_k_ref[r, :, here].astype(F32)
        sink_values = sink_v_ref[r, :, here].astype(F32)
        score = jnp.where(lives[r], score * scale, NEG)
        top = jnp.max(score, axis=1, keepdims=True)
        sink_score = []
        for i in range(sinks):
            one = jnp.sum(query * sink_keys[i : i + 1, :], axis=1, keepdims=True) * scale
            one = jnp.where(first_shard, one, NEG)
            sink_score.append(one)
            top = jnp.maximum(top, one)
        weight = jnp.where(lives[r], jnp.exp(score - top), 0.0)
        mixture = lax.dot_general(
            weight.astype(BF16),
            v_ref[r, here, :],
            (((1,), (1,)), ((), ())),
            preferred_element_type=F32,
        )
        total = jnp.sum(weight, axis=1, keepdims=True)
        for i in range(sinks):
            one = jnp.where(first_shard, jnp.exp(sink_score[i] - top), 0.0)
            total = total + one
            mixture = mixture + one.astype(BF16).astype(F32) * sink_values[i : i + 1, :]
        some = total > 0.0
        level = jnp.where(some, top + jnp.log(jnp.where(some, total, 1.0)), NEG)
        mixture = mixture / jnp.where(some, total, 1.0)
        mixture = jnp.sum(jnp.where(own, mixture, 0.0), axis=0, keepdims=True)
        level = jnp.sum(jnp.where(own, level, 0.0), axis=0, keepdims=True)
        for f in range(block // chunk):
            t, c = divmod(f, lanes // chunk)
            row = wire_row(rows, c, r)
            at = slice(f * chunk, (f + 1) * chunk)
            for copy in range(copies):
                out_ref[copy, 2 * source + t, row : row + 1, :] = mixture[:, at]
                out_ref[copy, 2 * source + t, half + row : half + row + 1, :] = level[:, at]

    todo = [(r, step) for step in steps for r in range(rows)]
    ahead = [scores(*one) for one in todo[:AHEAD]]
    for i, one in enumerate(todo):
        if i + AHEAD < len(todo):
            ahead.append(scores(*todo[i + AHEAD]))
        mix(*one, *ahead[i])


def merge_kernel(rows, part_ref, new_ref, w_ref, mine_ref, other_ref, rows_ref, full_ref):
    copies, groups, wire_rows, chunk = part_ref.shape
    half = wire_rows // 2
    lanes = w_ref.shape[0]
    flat = groups * wire_rows
    parts = [part_ref[s].reshape(flat, chunk) for s in range(copies)]
    parts.append(new_ref[...].reshape(flat, chunk))
    levels = [pltpu.roll(part, flat - half, 0) for part in parts]
    top = functools.reduce(jnp.maximum, levels)
    mixture = jnp.zeros((flat, chunk), F32)
    total = jnp.zeros((flat, chunk), F32)
    for part, level in zip(parts, levels):
        share = jnp.exp(level - top)
        mixture = mixture + share * part
        total = total + share
    rows_ref[...] = mixture / total
    attended = []
    for c in range(lanes // chunk):
        start = wire_row(rows, c, 0)
        attended.append(
            jnp.concatenate(
                [
                    rows_ref[g * wire_rows + start : g * wire_rows + start + rows, :]
                    for g in range(groups)
                ],
                axis=0,
            )
        )
    attended = jnp.concatenate(attended, axis=1).astype(BF16)
    full_ref[...] = jnp.dot(attended, w_ref[...], preferred_element_type=F32)
    width = mine_ref.shape[1]
    core = lax.axis_index("tensor") % 2
    mine_ref[...] = full_ref[:, pl.ds(pl.multiple_of(core * width, LANE), width)]
    other_ref[...] = full_ref[:, pl.ds(pl.multiple_of((1 - core) * width, LANE), width)]


def spread_rows(values, wide_ref):
    batch, width = values.shape
    step = 2 * LANE
    feature = lax.broadcasted_iota(jnp.int32, (step, 4 * step), 0)
    lane = lax.broadcasted_iota(jnp.int32, (step, 4 * step), 1)
    lane = jnp.where(lane < 2 * step, lane, lane - 2 * step - 1)
    spread = (2 * feature == lane).astype(F32).astype(BF16)
    pieces = width // step
    stacked = jnp.concatenate([values[:, j * step : (j + 1) * step] for j in range(pieces)], axis=0)
    wide = jnp.dot(stacked, spread, preferred_element_type=F32).astype(BF16)
    for j in range(pieces):
        part = wide[j * batch : (j + 1) * batch, :]
        at = slice(j * 2 * step, (j + 1) * 2 * step)
        wide_ref[:batch, at] = part[:, : 2 * step]
        wide_ref[batch:, at] = part[:, 2 * step :]


def half_gate_up(side, half, gain_ref, gate_up_ref, wide_ref):
    width = side.shape[1]
    units = gate_up_ref.shape[2]
    gain = gain_ref[...].astype(F32).reshape(1, -1)
    gain = jnp.where(half == 0, gain[:, :width], gain[:, width:])
    spread_rows((side * gain).astype(BF16), wide_ref)
    weights = gate_up_ref.reshape(4 * width, units)
    weights = weights[pl.ds(pl.multiple_of(half * 2 * width, 2 * width), 2 * width), :]
    gate_up = jnp.dot(wide_ref[...], weights, preferred_element_type=F32)
    return gate_up, jnp.sum(side * side, axis=1, keepdims=True)


def first_half_kernel(side_ref, gain_ref, gate_up_ref, out_ref, square_ref, wide_ref):
    core = lax.axis_index("tensor") % 2
    side = side_ref[...].astype(F32)
    out_ref[...], square = half_gate_up(side, core, gain_ref, gate_up_ref, wide_ref)
    square_ref[...] = jnp.broadcast_to(square, square_ref.shape)


def mlp_kernel(
    rows,
    mine_ref,
    other_ref,
    gain_ref,
    gate_up_ref,
    down_ref,
    first_ref,
    square_ref,
    out_ref,
    resid_ref,
    wide_ref,
    by_ref,
):
    batch, width = mine_ref.shape
    core = lax.axis_index("tensor") % 2
    mine = mine_ref[...].astype(F32)
    other = other_ref[...].astype(F32)
    gate_up, square = half_gate_up(other, 1 - core, gain_ref, gate_up_ref, wide_ref)
    meansq = (square + square_ref[:, :1]) / (2 * width)
    scale = lax.rsqrt(meansq + 1e-05)
    gate_up = gate_up + first_ref[...]
    gate = gate_up[:batch] * scale
    hidden = (gate * jax.nn.sigmoid(gate) * (gate_up[batch:] * scale)).astype(BF16)
    out = jnp.dot(hidden, down_ref[...], preferred_element_type=F32)
    resid = jnp.concatenate(
        [jnp.where(core == 0, mine, other), jnp.where(core == 0, other, mine)], axis=1
    )
    groups = out_ref.shape[0]
    for group in range(groups):
        by_ref[group, :rows, :] = resid[group * rows : (group + 1) * rows, :]
        out_ref[group] = out[group * rows : (group + 1) * rows, :].astype(BF16)
    resid_ref[...] = by_ref[lax.axis_index("tensor"), :rows, :]


def prepare_kernel(rows, pos_ref, cos_ref, sin_ref):
    core = lax.axis_index("tensor") % 2
    chips = cos_ref.shape[0] // (2 * rows)
    wide = cos_ref.shape[1]
    half = HEAD_SIZE // 2
    pair = lax.broadcasted_iota(jnp.int32, (1, wide), 1) % half
    inverse = jnp.zeros((1, wide), F32)
    for i in range(half):
        inverse = jnp.where(pair == i, np.float32(ROTARY_BASE ** (-2 * i / HEAD_SIZE)), inverse)

    shape = cos_ref.shape
    row = lax.broadcasted_iota(jnp.int32, shape, 0)
    position = jnp.zeros(shape, F32)
    for i in range(shape[0]):
        group, r = divmod(i, rows)
        parity = core if group < chips else 1 - core
        request = (2 * chip_away(group % chips, chips) + parity) * rows + r
        position = jnp.where(row == i, pos_ref[request].astype(F32), position)
    angle = position * inverse
    sine = jnp.sin(angle)
    lane = lax.broadcasted_iota(jnp.int32, shape, 1)
    cos_ref[...] = jnp.cos(angle)
    sin_ref[...] = jnp.where(lane % HEAD_SIZE < half, -sine, sine)


def mark_live(len_ref, pos_ref, mask_ref, slot_pos_ref, live_ref):
    rows, slots = mask_ref.shape
    slot = lax.axis_index("seq") * slots + lax.broadcasted_iota(jnp.int32, (1, slots), 1)
    first_row = lax.axis_index("tensor") * rows
    for r in range(rows):
        own_len = len_ref[first_row + r]
        own_pos = pos_ref[first_row + r]
        slot_at = slot_pos_ref[r : r + 1, :]
        live = (slot < own_len) & (mask_ref[r : r + 1, :] == 1)
        live = live & (slot_at < own_pos) & (own_pos - slot_at < WINDOW)
        live_ref[r : r + 1, :] = live.astype(jnp.int32)


def call(kernel, out, inputs, specs=None, scratch=(), limit=6, name=None, flops=0, aliases={}):
    return pl.pallas_call(
        kernel,
        out_shape=out,
        in_specs=specs or [VMEM_SPEC] * len(inputs),
        out_specs=jax.tree.map(lambda _: VMEM_SPEC, out),
        scratch_shapes=scratch,
        input_output_aliases=aliases,
        compiler_params=pltpu.CompilerParams(vmem_limit_bytes=limit * MIB),
        name=name,
        cost_estimate=pl.CostEstimate(
            flops=flops,
            bytes_accessed=sum(a.size * a.dtype.itemsize for a in inputs),
            transcendentals=0,
        ),
    )(*inputs)


def per_device(
    shards,
    groups,
    states,
    attn_gain,
    w_qkv,
    w_out,
    mlp_gain,
    w_gate_up,
    w_down,
    key_cache,
    value_cache,
    sink_keys,
    sink_values,
    cache_len,
    slot_mask,
    slot_pos,
    new_pos,
):
    rows, width = states.shape
    batch = rows * groups
    lanes = w_qkv.shape[2]
    sds = jax.ShapeDtypeStruct
    chunk = min(lanes, LANE)
    wire_rows = max(8, 2 * rows * lanes // chunk)

    chips = groups // 2
    turn = sds((batch, chunk), F32)
    cosine, sine = call(
        functools.partial(prepare_kernel, rows),
        (turn, turn),
        (new_pos,),
        specs=[SMEM_SPEC],
        name="prepare",
        flops=PREP_FLOPS,
    )
    across = [(i, i ^ 1) for i in range(groups)]
    hops = [[(i, (i + step) % groups) for i in range(groups)] for step in range(2, groups, 2)]
    column = [states] + [lax.ppermute(states, "tensor", hop) for hop in hops]
    w_qkv = jnp.transpose(w_qkv, (1, 0, 2))
    w_peer = lax.ppermute(w_qkv, "tensor", across)
    query_wire = sds((max(8, 2 * rows * lanes // LANE), LANE), F32)
    queries = call(
        functools.partial(query_kernel, rows, chips),
        (query_wire,) * chips,
        (*column, attn_gain, w_qkv, w_peer, cosine, sine),
        name="query",
        flops=QKV_FLOPS,
    )
    same = jnp.stack(column)
    peer = lax.ppermute(same, "tensor", across)
    same, *queries = lax.optimization_barrier((same, *queries))
    queries = [queries[0]] + [
        lax.ppermute(query, "tensor", hop) for query, hop in zip(queries[1:], hops)
    ]
    wire = sds((groups, wire_rows, chunk), F32)
    new_part, key_part, live = call(
        functools.partial(new_token_kernel, rows),
        (wire, wire, sds(slot_mask.shape, jnp.int32)),
        (cache_len, new_pos, slot_mask, slot_pos, same, peer, attn_gain, w_qkv, cosine, sine),
        specs=[SMEM_SPEC] * 2 + [VMEM_SPEC] * 8,
        name="new_token",
        flops=QKV_FLOPS,
    )
    sink_keys = jnp.transpose(sink_keys, (0, 2, 1))
    sink_values = jnp.transpose(sink_values, (0, 2, 1))

    def attention(steps, arrays, aliases, name):
        return call(
            functools.partial(attention_kernel, lanes, chips, steps),
            sds((shards, groups, wire_rows, chunk), F32),
            arrays,
            limit=8,
            name=name,
            flops=ATT_FLOPS,
            aliases=aliases,
        )

    cache = (key_cache, value_cache, sink_keys, sink_values, live)
    part = attention((0,), (queries[0], *cache), {}, "own_heads")
    queries, new_part, part = lax.optimization_barrier((queries, new_part, part))
    part = attention(
        tuple(range(1, chips)), (*queries[1:], *cache, part), {chips + 4: 0}, "other_heads"
    )
    part = lax.all_to_all(
        part.reshape(shards * groups, wire_rows, chunk), ("seq", "tensor"), 0, 0, tiled=True
    ).reshape(shards, groups, wire_rows, chunk)
    side = sds((batch, width // 2), F32)
    mine, other = call(
        functools.partial(merge_kernel, rows),
        (side, side),
        (part, new_part, w_out),
        scratch=[pltpu.VMEM((groups * wire_rows, chunk), F32), pltpu.VMEM((batch, width), F32)],
        name="merge",
        flops=MERGE_FLOPS,
    )
    chip = (mine + lax.ppermute(other, "tensor", across)).astype(BF16)
    flat = sds((batch, lanes), BF16)
    chip, same, peer, new_part, key_part = lax.optimization_barrier(
        (chip, same, peer, new_part, key_part)
    )
    new_keys, new_values, own_side = call(
        outputs_kernel,
        (flat, flat, side),
        (same, peer, new_part, key_part),
        scratch=[pltpu.VMEM((groups, 8, width), F32), pltpu.VMEM((batch, width), F32)],
        name="outputs",
    )
    total = chip.astype(F32)
    for which in range(0, -len(hops), -1):
        total = total + lax.ppermute(chip, "tensor", hops[which]).astype(F32)
    side_resid = (own_side + total).astype(BF16)
    other_resid = lax.ppermute(side_resid, "tensor", across)
    units = w_gate_up.shape[2]
    first_half, square = call(
        first_half_kernel,
        (sds((2 * batch, units), F32), sds((batch, LANE), F32)),
        (side_resid, mlp_gain, w_gate_up),
        scratch=[pltpu.VMEM((2 * batch, width), BF16)],
        limit=8,
        name="first_half",
        flops=2 * batch * width * units,
    )
    partial, own_resid = call(
        functools.partial(mlp_kernel, rows),
        (sds((groups, rows, width), BF16), sds((rows, width), F32)),
        (side_resid, other_resid, mlp_gain, w_gate_up, w_down, first_half, square),
        scratch=[pltpu.VMEM((2 * batch, width), BF16), pltpu.VMEM((groups, 8, width), F32)],
        limit=8,
        name="mlp",
        flops=4 * batch * width * units,
    )
    partial = lax.all_to_all(partial, "tensor", 0, 0, tiled=True)
    out_states = (own_resid + jnp.sum(partial.astype(F32), axis=0)).astype(BF16)
    return out_states, new_keys, new_values


def solution(mesh):
    in_specs = (
        P("tensor", None),
        P(),
        P(None, None, "tensor"),
        P("tensor", None),
        P(),
        P(None, None, "tensor"),
        P("tensor", None),
        P("tensor", None, "seq"),
        P("tensor", None, "seq"),
        P("tensor", None, None),
        P("tensor", None, None),
        P(),
        P("tensor", "seq"),
        P("tensor", "seq"),
        P(),
    )
    out_specs = (P("tensor", None), P(None, "tensor"), P(None, "tensor"))
    body = functools.partial(per_device, mesh.shape["seq"], mesh.shape["tensor"])
    return jax.shard_map(
        body, mesh=mesh, in_specs=in_specs, out_specs=out_specs, check_vma=False
    )
```

```python
import functools

import jax
import jax.numpy as jnp
import numpy as np
from jax import lax
from jax.experimental import pallas as pl
from jax.experimental.pallas import tpu as pltpu
from jax.sharding import PartitionSpec as P

HEAD_SIZE = 64
WINDOW = 4096
ROTARY_BASE = 130000.0
NEG = -1e30
LANE = 128
MIB = 2**20
AHEAD = 1
LEVEL_ROW = 4
PREP_FLOPS = 20_000_000_000
QKV_FLOPS = 2_000_000_000
ATT_FLOPS = 10_000_000_000
MERGE_FLOPS = 10_000_000_000

VMEM_SPEC = pl.BlockSpec(memory_space=pltpu.VMEM)
SMEM_SPEC = pl.BlockSpec(memory_space=pltpu.SMEM)
F32 = jnp.float32
BF16 = jnp.bfloat16


def normed_rows(values, gain):
    meansq = jnp.mean(values * values, axis=-1, keepdims=True)
    return (values * lax.rsqrt(meansq + 1e-05) * gain).astype(BF16)


def swap_halves(tensor):
    width = tensor.shape[1]
    half = HEAD_SIZE // 2
    if width == HEAD_SIZE:
        return jnp.concatenate([tensor[:, half:], tensor[:, :half]], axis=1)
    lane = lax.broadcasted_iota(jnp.int32, tensor.shape, 1)
    upper = pltpu.roll(tensor, width - half, 1)
    lower = pltpu.roll(tensor, half, 1)
    return jnp.where(lane % HEAD_SIZE < half, upper, lower)


def wire_row(rows, lane_chunk, row):
    return lane_chunk * rows + row


def query_kernel(rows, chips, *refs):
    states, refs = refs[:chips], refs[chips:]
    gain_ref, own_ref, peer_ref, cos_ref, sin_ref = refs[:5]
    outs = refs[5:]
    core = lax.axis_index("tensor") % 2
    values = jnp.concatenate([ref[...].astype(F32) for ref in states], axis=0)
    normed = normed_rows(values, gain_ref[...].astype(F32).reshape(1, -1))
    own = jnp.dot(normed, own_ref[0], preferred_element_type=F32)
    peer = jnp.dot(normed, peer_ref[0], preferred_element_type=F32)
    queries = jnp.concatenate(
        [jnp.where(core == 0, own, peer), jnp.where(core == 0, peer, own)], axis=1
    )
    count, repeat = queries.shape[0], queries.shape[1] // cos_ref.shape[1]
    cosine = jnp.concatenate([cos_ref[:count, :]] * repeat, axis=1)
    sine = jnp.concatenate([sin_ref[:count, :]] * repeat, axis=1)
    queries = (queries * cosine + swap_halves(queries) * sine).astype(BF16).astype(F32)
    for step in range(chips):
        first = (chips - step) % chips * rows
        out = outs[step]
        if rows * queries.shape[1] // LANE < out.shape[0]:
            out[...] = jnp.zeros_like(out)
        for c in range(queries.shape[1] // LANE):
            at = slice(c * LANE, (c + 1) * LANE)
            row = wire_row(rows, c, 0)
            out[row : row + rows, :] = queries[first : first + rows, at]


def chip_away(step, chips):
    return lax.rem(lax.axis_index("tensor") // 2 + chips - step, chips)


def new_token_kernel(
    rows,
    len_ref,
    pos_ref,
    mask_ref,
    slot_pos_ref,
    same_ref,
    peer_ref,
    gain_ref,
    w_ref,
    cos_ref,
    sin_ref,
    new_ref,
    key_ref,
    live_ref,
):
    mark_live(len_ref, pos_ref, mask_ref, slot_pos_ref, live_ref)
    lanes = w_ref.shape[2]
    core = lax.axis_index("tensor") % 2
    chips = same_ref.shape[0]
    values = jnp.concatenate(
        [ref[step].astype(F32) for ref in (same_ref, peer_ref) for step in range(chips)], axis=0
    )
    normed = normed_rows(values, gain_ref[...].astype(F32).reshape(1, -1))
    repeat = lanes // cos_ref.shape[1]
    cosine = jnp.concatenate([cos_ref[...]] * repeat, axis=1)
    sine = jnp.concatenate([sin_ref[...]] * repeat, axis=1)

    def project(part):
        return jnp.dot(normed, w_ref[part], preferred_element_type=F32)

    def turned(t):
        return (t * cosine + swap_halves(t) * sine).astype(BF16).astype(F32)

    queries = turned(project(0))
    keys = turned(project(1))
    values = project(2).astype(BF16).astype(F32)
    head_in = lax.broadcasted_iota(jnp.int32, (lanes, lanes), 0) // HEAD_SIZE
    head_out = lax.broadcasted_iota(jnp.int32, (lanes, lanes), 1) // HEAD_SIZE
    same_head = (head_in == head_out).astype(F32)
    score = jnp.dot(
        queries * keys,
        same_head,
        preferred_element_type=F32,
        precision=lax.Precision.HIGHEST,
    ) * (HEAD_SIZE**-0.5)
    half, chunk = new_ref.shape[1] // 2, new_ref.shape[2]
    for i in range(2 * chips):
        group = 2 * chip_away(i % chips, chips) + (core if i < chips else 1 - core)
        mine = slice(i * rows, (i + 1) * rows)
        for c in range(lanes // chunk):
            at = slice(c * chunk, (c + 1) * chunk)
            row = wire_row(rows, c, 0)
            new_ref[group, row : row + rows, :] = values[mine, at]
            new_ref[group, half + row : half + row + rows, :] = score[mine, at]
            key_ref[group, row : row + rows, :] = keys[mine, at]


def outputs_kernel(same_ref, peer_ref, new_ref, key_ref, k_ref, v_ref, side_ref, by_ref, flat_ref):
    chips, rows, _ = same_ref.shape
    core = lax.axis_index("tensor") % 2
    for step in range(chips):
        source = 2 * chip_away(step, chips)
        by_ref[source + core, :rows, :] = same_ref[step].astype(F32)
        by_ref[source + 1 - core, :rows, :] = peer_ref[step].astype(F32)
    for group in range(2 * chips):
        flat_ref[group * rows : (group + 1) * rows, :] = by_ref[group, :rows, :]
    width = side_ref.shape[1]
    side_ref[...] = flat_ref[:, pl.ds(pl.multiple_of(core * width, LANE), width)]
    lanes, chunk = k_ref.shape[1], new_ref.shape[2]
    for from_ref, to_ref in ((key_ref, k_ref), (new_ref, v_ref)):
        parts = []
        for c in range(lanes // chunk):
            row = wire_row(rows, c, 0)
            parts.append(
                jnp.concatenate(
                    [from_ref[group, row : row + rows, :] for group in range(2 * chips)], axis=0
                )
            )
        to_ref[...] = jnp.concatenate(parts, axis=1).astype(BF16)


def attention_kernel(lanes, chips, steps, *refs):
    queries, refs = dict(zip(steps, refs)), refs[len(steps) :]
    k_ref, v_ref, sink_k_ref, sink_v_ref, live_ref = refs[:5]
    out_ref, tile_ref = refs[-2:]
    rows, features, slots = k_ref.shape
    sinks = sink_k_ref.shape[1]
    copies = out_ref.shape[0]
    chunk = out_ref.shape[3]
    block = 2 * lanes
    group_heads = lanes // HEAD_SIZE
    repeat = chunk // (rows * group_heads)
    heads = max(8, block // HEAD_SIZE)
    seq_index = lax.axis_index("seq")
    chip = lax.axis_index("tensor") // 2
    head = lax.broadcasted_iota(jnp.int32, (heads, block), 0)
    own = head == lax.broadcasted_iota(jnp.int32, (heads, block), 1) // HEAD_SIZE
    scale = HEAD_SIZE**-0.5
    lives = [
        jnp.broadcast_to(live_ref[r : r + 1, :], (heads, slots)) == 1 for r in range(rows)
    ]
    first_shard = seq_index == 0

    def place(step):
        source = lax.rem(chip + chips - step, chips)
        return source, pl.ds(pl.multiple_of(source * block, block), block)

    def scores(r, step):
        _, here = place(step)
        query = jnp.concatenate(
            [
                queries[step][wire_row(rows, c, r) : wire_row(rows, c, r) + 1, :]
                for c in range(block // LANE)
            ],
            axis=1,
        )
        query = jnp.where(own, jnp.broadcast_to(query, (heads, block)), 0.0)
        score = jnp.dot(query.astype(BF16), k_ref[r, here, :], preferred_element_type=F32)
        return query, score

    def mix(r, step, query, score):
        source, here = place(step)
        sink_keys = sink_k_ref[r, :, here].astype(F32)
        sink_values = sink_v_ref[r, :, here].astype(F32)
        score = jnp.where(lives[r], score * scale, NEG)
        top = jnp.max(score, axis=1, keepdims=True)
        sink_score = []
        for i in range(sinks):
            one = jnp.sum(query * sink_keys[i : i + 1, :], axis=1, keepdims=True) * scale
            one = jnp.where(first_shard, one, NEG)
            sink_score.append(one)
            top = jnp.maximum(top, one)
        weight = jnp.where(lives[r], jnp.exp(score - top), 0.0)
        mixture = lax.dot_general(
            weight.astype(BF16),
            v_ref[r, here, :],
            (((1,), (1,)), ((), ())),
            preferred_element_type=F32,
        )
        total = jnp.sum(weight, axis=1, keepdims=True)
        for i in range(sinks):
            one = jnp.where(first_shard, jnp.exp(sink_score[i] - top), 0.0)
            total = total + one
            mixture = mixture + one.astype(BF16).astype(F32) * sink_values[i : i + 1, :]
        some = total > 0.0
        level = jnp.where(some, top + jnp.log(jnp.where(some, total, 1.0)), NEG)
        mixture = mixture / jnp.where(some, total, 1.0)
        mixture = jnp.sum(jnp.where(own, mixture, 0.0), axis=0, keepdims=True)
        for t in range(2):
            tile = steps.index(step) * 2 + t
            for c in range(lanes // chunk):
                row = wire_row(rows, c, r)
                start = t * lanes + c * chunk
                tile_ref[tile, row : row + 1, :] = mixture[:, start : start + chunk]
            here = head_row == head_lane + (t - r) * group_heads
            here = here & (head_row // group_heads == t)
            one = jnp.sum(jnp.where(here, level, 0.0), axis=0, keepdims=True)
            if r > 0:
                one = one + tile_ref[tile, LEVEL_ROW : LEVEL_ROW + 1, :]
            if r < rows - 1:
                tile_ref[tile, LEVEL_ROW : LEVEL_ROW + 1, :] = one
                continue
            for term in range(3):
                rounded = one.astype(BF16).astype(F32)
                tile_ref[tile, LEVEL_ROW + term : LEVEL_ROW + term + 1, :] = rounded
                one = one - rounded
            parts = tile_ref[tile].astype(BF16)
            for copy in range(copies):
                out_ref[copy, 2 * source + t] = parts

    tile_ref[...] = jnp.zeros_like(tile_ref)
    head_row = lax.broadcasted_iota(jnp.int32, (heads, chunk), 0)
    head_lane = lax.broadcasted_iota(jnp.int32, (heads, chunk), 1) // repeat
    todo = [(r, step) for step in steps for r in range(rows)]
    ahead = [scores(*one) for one in todo[:AHEAD]]
    for i, one in enumerate(todo):
        if i + AHEAD < len(todo):
            ahead.append(scores(*todo[i + AHEAD]))
        mix(*one, *ahead[i])


def merge_kernel(
    rows, part_ref, new_ref, w_ref, mine_ref, other_ref, rows_ref, attended_ref, full_ref
):
    copies, groups, wire_rows, chunk = part_ref.shape
    lanes = w_ref.shape[0]
    flat = groups * wire_rows
    for s in range(copies):
        rows_ref[s * flat : (s + 1) * flat, :] = part_ref[s].astype(F32).reshape(flat, chunk)
    rows_ref[copies * flat :, :] = new_ref[...].reshape(flat, chunk)

    def every(row, first, count):
        return rows_ref[pl.ds(first * flat + row, count * groups, stride=wire_rows), :]

    count = rows * lanes // chunk
    terms = jnp.concatenate([every(LEVEL_ROW + term, 0, copies) for term in range(3)], axis=0)
    shape = (chunk, count * chunk)
    to = lax.broadcasted_iota(jnp.int32, shape, 1)
    to_head = (to // (rows * chunk) * chunk + to % chunk) // HEAD_SIZE
    group_heads = lanes // HEAD_SIZE
    at = (to // chunk % rows * group_heads + to_head) * (chunk // (rows * group_heads))
    spread = (lax.broadcasted_iota(jnp.int32, shape, 0) == at).astype(F32).astype(BF16)
    terms = jnp.dot(terms.astype(BF16), spread, preferred_element_type=F32)
    size = copies * groups
    levels = terms[:size] + terms[size : 2 * size] + terms[2 * size :]
    for i in range(count):
        c, r = divmod(i, rows)
        mine = every(i, 0, copies)
        parts = [mine[s * groups : (s + 1) * groups] for s in range(copies)]
        parts.append(every(i, copies, 1))
        level = [
            levels[s * groups : (s + 1) * groups, i * chunk : (i + 1) * chunk]
            for s in range(copies)
        ]
        level.append(every(wire_rows // 2 + i, copies, 1))
        top = functools.reduce(jnp.maximum, level)
        shares = [jnp.exp(one - top) for one in level]
        mixture = functools.reduce(jnp.add, [share * part for share, part in zip(shares, parts)])
        total = functools.reduce(jnp.add, shares)
        attended_ref[c, pl.ds(r, groups, stride=rows), :] = mixture / total
    attended = [attended_ref[c] for c in range(lanes // chunk)]
    attended = jnp.concatenate(attended, axis=1).astype(BF16)
    full_ref[...] = jnp.dot(attended, w_ref[...], preferred_element_type=F32)
    width = mine_ref.shape[1]
    core = lax.axis_index("tensor") % 2
    mine_ref[...] = full_ref[:, pl.ds(pl.multiple_of(core * width, LANE), width)]
    other_ref[...] = full_ref[:, pl.ds(pl.multiple_of((1 - core) * width, LANE), width)]


def spread_rows(values, wide_ref):
    batch, width = values.shape
    step = 2 * LANE
    feature = lax.broadcasted_iota(jnp.int32, (step, 4 * step), 0)
    lane = lax.broadcasted_iota(jnp.int32, (step, 4 * step), 1)
    lane = jnp.where(lane < 2 * step, lane, lane - 2 * step - 1)
    spread = (2 * feature == lane).astype(F32).astype(BF16)
    pieces = width // step
    stacked = jnp.concatenate([values[:, j * step : (j + 1) * step] for j in range(pieces)], axis=0)
    wide = jnp.dot(stacked, spread, preferred_element_type=F32).astype(BF16)
    for j in range(pieces):
        part = wide[j * batch : (j + 1) * batch, :]
        at = slice(j * 2 * step, (j + 1) * 2 * step)
        wide_ref[:batch, at] = part[:, : 2 * step]
        wide_ref[batch:, at] = part[:, 2 * step :]


def half_gate_up(side, half, gain_ref, gate_up_ref, wide_ref):
    width = side.shape[1]
    units = gate_up_ref.shape[2]
    gain = gain_ref[...].astype(F32).reshape(1, -1)
    gain = jnp.where(half == 0, gain[:, :width], gain[:, width:])
    spread_rows((side * gain).astype(BF16), wide_ref)
    weights = gate_up_ref.reshape(4 * width, units)
    weights = weights[pl.ds(pl.multiple_of(half * 2 * width, 2 * width), 2 * width), :]
    gate_up = jnp.dot(wide_ref[...], weights, preferred_element_type=F32)
    return gate_up, jnp.sum(side * side, axis=1, keepdims=True)


def first_half_kernel(side_ref, gain_ref, gate_up_ref, out_ref, square_ref, wide_ref):
    core = lax.axis_index("tensor") % 2
    side = side_ref[...].astype(F32)
    out_ref[...], square = half_gate_up(side, core, gain_ref, gate_up_ref, wide_ref)
    square_ref[...] = jnp.broadcast_to(square, square_ref.shape)


def mlp_kernel(
    rows,
    mine_ref,
    other_ref,
    gain_ref,
    gate_up_ref,
    down_ref,
    first_ref,
    square_ref,
    out_ref,
    resid_ref,
    wide_ref,
    by_ref,
):
    batch, width = mine_ref.shape
    core = lax.axis_index("tensor") % 2
    mine = mine_ref[...].astype(F32)
    other = other_ref[...].astype(F32)
    gate_up, square = half_gate_up(other, 1 - core, gain_ref, gate_up_ref, wide_ref)
    meansq = (square + square_ref[:, :1]) / (2 * width)
    scale = lax.rsqrt(meansq + 1e-05)
    gate_up = gate_up + first_ref[...]
    gate = gate_up[:batch] * scale
    hidden = (gate * jax.nn.sigmoid(gate) * (gate_up[batch:] * scale)).astype(BF16)
    out = jnp.dot(hidden, down_ref[...], preferred_element_type=F32)
    resid = jnp.concatenate(
        [jnp.where(core == 0, mine, other), jnp.where(core == 0, other, mine)], axis=1
    )
    groups = out_ref.shape[0]
    for group in range(groups):
        by_ref[group, :rows, :] = resid[group * rows : (group + 1) * rows, :]
        out_ref[group] = out[group * rows : (group + 1) * rows, :].astype(BF16)
    resid_ref[...] = by_ref[lax.axis_index("tensor"), :rows, :]


def prepare_kernel(rows, pos_ref, cos_ref, sin_ref):
    core = lax.axis_index("tensor") % 2
    chips = cos_ref.shape[0] // (2 * rows)
    wide = cos_ref.shape[1]
    half = HEAD_SIZE // 2
    pair = lax.broadcasted_iota(jnp.int32, (1, wide), 1) % half
    inverse = jnp.zeros((1, wide), F32)
    for i in range(half):
        inverse = jnp.where(pair == i, np.float32(ROTARY_BASE ** (-2 * i / HEAD_SIZE)), inverse)

    shape = cos_ref.shape
    row = lax.broadcasted_iota(jnp.int32, shape, 0)
    position = jnp.zeros(shape, F32)
    for i in range(shape[0]):
        group, r = divmod(i, rows)
        parity = core if group < chips else 1 - core
        request = (2 * chip_away(group % chips, chips) + parity) * rows + r
        position = jnp.where(row == i, pos_ref[request].astype(F32), position)
    angle = position * inverse
    sine = jnp.sin(angle)
    lane = lax.broadcasted_iota(jnp.int32, shape, 1)
    cos_ref[...] = jnp.cos(angle)
    sin_ref[...] = jnp.where(lane % HEAD_SIZE < half, -sine, sine)


def mark_live(len_ref, pos_ref, mask_ref, slot_pos_ref, live_ref):
    rows, slots = mask_ref.shape
    slot = lax.axis_index("seq") * slots + lax.broadcasted_iota(jnp.int32, (1, slots), 1)
    first_row = lax.axis_index("tensor") * rows
    for r in range(rows):
        own_len = len_ref[first_row + r]
        own_pos = pos_ref[first_row + r]
        slot_at = slot_pos_ref[r : r + 1, :]
        live = (slot < own_len) & (mask_ref[r : r + 1, :] == 1)
        live = live & (slot_at < own_pos) & (own_pos - slot_at < WINDOW)
        live_ref[r : r + 1, :] = live.astype(jnp.int32)


def call(kernel, out, inputs, specs=None, scratch=(), limit=6, name=None, flops=0, aliases={}):
    return pl.pallas_call(
        kernel,
        out_shape=out,
        in_specs=specs or [VMEM_SPEC] * len(inputs),
        out_specs=jax.tree.map(lambda _: VMEM_SPEC, out),
        scratch_shapes=scratch,
        input_output_aliases=aliases,
        compiler_params=pltpu.CompilerParams(vmem_limit_bytes=limit * MIB),
        name=name,
        cost_estimate=pl.CostEstimate(
            flops=flops,
            bytes_accessed=sum(a.size * a.dtype.itemsize for a in inputs),
            transcendentals=0,
        ),
    )(*inputs)


def per_device(
    shards,
    groups,
    states,
    attn_gain,
    w_qkv,
    w_out,
    mlp_gain,
    w_gate_up,
    w_down,
    key_cache,
    value_cache,
    sink_keys,
    sink_values,
    cache_len,
    slot_mask,
    slot_pos,
    new_pos,
):
    rows, width = states.shape
    batch = rows * groups
    lanes = w_qkv.shape[2]
    sds = jax.ShapeDtypeStruct
    chunk = min(lanes, LANE)
    wire_rows = max(8, 2 * rows * lanes // chunk)

    chips = groups // 2
    turn = sds((batch, chunk), F32)
    cosine, sine = call(
        functools.partial(prepare_kernel, rows),
        (turn, turn),
        (new_pos,),
        specs=[SMEM_SPEC],
        name="prepare",
        flops=PREP_FLOPS,
    )
    across = [(i, i ^ 1) for i in range(groups)]
    hops = [[(i, (i + step) % groups) for i in range(groups)] for step in range(2, groups, 2)]
    column = [states] + [lax.ppermute(states, "tensor", hop) for hop in hops]
    w_qkv = jnp.transpose(w_qkv, (1, 0, 2))
    w_peer = lax.ppermute(w_qkv, "tensor", across)
    query_wire = sds((max(8, 2 * rows * lanes // LANE), LANE), F32)
    queries = call(
        functools.partial(query_kernel, rows, chips),
        (query_wire,) * chips,
        (*column, attn_gain, w_qkv, w_peer, cosine, sine),
        name="query",
        flops=QKV_FLOPS,
    )
    same = jnp.stack(column)
    peer = lax.ppermute(same, "tensor", across)
    same, *queries = lax.optimization_barrier((same, *queries))
    queries = [queries[0]] + [
        lax.ppermute(query, "tensor", hop) for query, hop in zip(queries[1:], hops)
    ]
    wire = sds((groups, wire_rows, chunk), F32)
    new_part, key_part, live = call(
        functools.partial(new_token_kernel, rows),
        (wire, wire, sds(slot_mask.shape, jnp.int32)),
        (cache_len, new_pos, slot_mask, slot_pos, same, peer, attn_gain, w_qkv, cosine, sine),
        specs=[SMEM_SPEC] * 2 + [VMEM_SPEC] * 8,
        name="new_token",
        flops=QKV_FLOPS,
    )
    sink_keys = jnp.transpose(sink_keys, (0, 2, 1))
    sink_values = jnp.transpose(sink_values, (0, 2, 1))

    def attention(steps, arrays, aliases, name):
        return call(
            functools.partial(attention_kernel, lanes, chips, steps),
            sds((shards, groups, 8, chunk), BF16),
            arrays,
            scratch=[pltpu.VMEM((2 * len(steps), 8, chunk), F32)],
            limit=8,
            name=name,
            flops=ATT_FLOPS,
            aliases=aliases,
        )

    cache = (key_cache, value_cache, sink_keys, sink_values, live)
    part = attention((0,), (queries[0], *cache), {}, "own_heads")
    queries, new_part, part = lax.optimization_barrier((queries, new_part, part))
    part = attention(
        tuple(range(1, chips)), (*queries[1:], *cache, part), {chips + 4: 0}, "other_heads"
    )
    part = lax.all_to_all(
        part.reshape(shards * groups, 8, chunk), ("seq", "tensor"), 0, 0, tiled=True
    ).reshape(shards, groups, 8, chunk)
    side = sds((batch, width // 2), F32)
    mine, other = call(
        functools.partial(merge_kernel, rows),
        (side, side),
        (part, new_part, w_out),
        scratch=[
            pltpu.VMEM(((shards + 1) * groups * 8, chunk), F32),
            pltpu.VMEM((lanes // chunk, batch, chunk), F32),
            pltpu.VMEM((batch, width), F32),
        ],
        name="merge",
        flops=MERGE_FLOPS,
    )
    chip = (mine + lax.ppermute(other, "tensor", across)).astype(BF16)
    flat = sds((batch, lanes), BF16)
    chip, same, peer, new_part, key_part = lax.optimization_barrier(
        (chip, same, peer, new_part, key_part)
    )
    new_keys, new_values, own_side = call(
        outputs_kernel,
        (flat, flat, side),
        (same, peer, new_part, key_part),
        scratch=[pltpu.VMEM((groups, 8, width), F32), pltpu.VMEM((batch, width), F32)],
        name="outputs",
    )
    total = chip.astype(F32)
    for which in range(0, -len(hops), -1):
        total = total + lax.ppermute(chip, "tensor", hops[which]).astype(F32)
    side_resid = (own_side + total).astype(BF16)
    other_resid = lax.ppermute(side_resid, "tensor", across)
    units = w_gate_up.shape[2]
    first_half, square = call(
        first_half_kernel,
        (sds((2 * batch, units), F32), sds((batch, LANE), F32)),
        (side_resid, mlp_gain, w_gate_up),
        scratch=[pltpu.VMEM((2 * batch, width), BF16)],
        limit=8,
        name="first_half",
        flops=2 * batch * width * units,
    )
    partial, own_resid = call(
        functools.partial(mlp_kernel, rows),
        (sds((groups, rows, width), BF16), sds((rows, width), F32)),
        (side_resid, other_resid, mlp_gain, w_gate_up, w_down, first_half, square),
        scratch=[pltpu.VMEM((2 * batch, width), BF16), pltpu.VMEM((groups, 8, width), F32)],
        limit=8,
        name="mlp",
        flops=4 * batch * width * units,
    )
    partial = lax.all_to_all(partial, "tensor", 0, 0, tiled=True)
    out_states = (own_resid + jnp.sum(partial.astype(F32), axis=0)).astype(BF16)
    return out_states, new_keys, new_values


def solution(mesh):
    in_specs = (
        P("tensor", None),
        P(),
        P(None, None, "tensor"),
        P("tensor", None),
        P(),
        P(None, None, "tensor"),
        P("tensor", None),
        P("tensor", None, "seq"),
        P("tensor", None, "seq"),
        P("tensor", None, None),
        P("tensor", None, None),
        P(),
        P("tensor", "seq"),
        P("tensor", "seq"),
        P(),
    )
    out_specs = (P("tensor", None), P(None, "tensor"), P(None, "tensor"))
    body = functools.partial(per_device, mesh.shape["seq"], mesh.shape["tensor"])
    return jax.shard_map(
        body, mesh=mesh, in_specs=in_specs, out_specs=out_specs, check_vma=False
    )
```

```python
import functools

import jax
import jax.numpy as jnp
import numpy as np
from jax import lax
from jax.experimental import pallas as pl
from jax.experimental.pallas import tpu as pltpu
from jax.sharding import PartitionSpec as P

HEAD_SIZE = 64
WINDOW = 4096
ROTARY_BASE = 130000.0
NEG = -1e30
LANE = 128
MIB = 2**20
AHEAD = 1
LEVEL_ROW = 4
PREP_FLOPS = 20_000_000_000
QKV_FLOPS = 2_000_000_000
ATT_FLOPS = 10_000_000_000
MERGE_FLOPS = 10_000_000_000

VMEM_SPEC = pl.BlockSpec(memory_space=pltpu.VMEM)
SMEM_SPEC = pl.BlockSpec(memory_space=pltpu.SMEM)
F32 = jnp.float32
BF16 = jnp.bfloat16


def normed_rows(values, gain):
    meansq = jnp.mean(values * values, axis=-1, keepdims=True)
    return (values * lax.rsqrt(meansq + 1e-05) * gain).astype(BF16)


def swap_halves(tensor):
    width = tensor.shape[1]
    half = HEAD_SIZE // 2
    if width == HEAD_SIZE:
        return jnp.concatenate([tensor[:, half:], tensor[:, :half]], axis=1)
    lane = lax.broadcasted_iota(jnp.int32, tensor.shape, 1)
    upper = pltpu.roll(tensor, width - half, 1)
    lower = pltpu.roll(tensor, half, 1)
    return jnp.where(lane % HEAD_SIZE < half, upper, lower)


def wire_row(rows, lane_chunk, row):
    return lane_chunk * rows + row


def query_kernel(rows, chips, *refs):
    states, refs = refs[:chips], refs[chips:]
    gain_ref, own_ref, peer_ref, cos_ref, sin_ref = refs[:5]
    outs = refs[5:]
    core = lax.axis_index("tensor") % 2
    values = jnp.concatenate([ref[...].astype(F32) for ref in states], axis=0)
    normed = normed_rows(values, gain_ref[...].astype(F32).reshape(1, -1))
    own = jnp.dot(normed, own_ref[0], preferred_element_type=F32)
    peer = jnp.dot(normed, peer_ref[0], preferred_element_type=F32)
    queries = jnp.concatenate(
        [jnp.where(core == 0, own, peer), jnp.where(core == 0, peer, own)], axis=1
    )
    count, repeat = queries.shape[0], queries.shape[1] // cos_ref.shape[1]
    cosine = jnp.concatenate([cos_ref[:count, :]] * repeat, axis=1)
    sine = jnp.concatenate([sin_ref[:count, :]] * repeat, axis=1)
    queries = (queries * cosine + swap_halves(queries) * sine).astype(BF16).astype(F32)
    for step in range(chips):
        first = (chips - step) % chips * rows
        out = outs[step]
        if rows * queries.shape[1] // LANE < out.shape[0]:
            out[...] = jnp.zeros_like(out)
        for c in range(queries.shape[1] // LANE):
            at = slice(c * LANE, (c + 1) * LANE)
            row = wire_row(rows, c, 0)
            out[row : row + rows, :] = queries[first : first + rows, at]


def chip_away(step, chips):
    return lax.rem(lax.axis_index("tensor") // 2 + chips - step, chips)


def new_token_kernel(
    rows,
    len_ref,
    pos_ref,
    mask_ref,
    slot_pos_ref,
    same_ref,
    peer_ref,
    gain_ref,
    w_ref,
    cos_ref,
    sin_ref,
    new_ref,
    key_ref,
    live_ref,
):
    mark_live(len_ref, pos_ref, mask_ref, slot_pos_ref, live_ref)
    lanes = w_ref.shape[2]
    core = lax.axis_index("tensor") % 2
    chips = same_ref.shape[0]
    values = jnp.concatenate(
        [ref[step].astype(F32) for ref in (same_ref, peer_ref) for step in range(chips)], axis=0
    )
    normed = normed_rows(values, gain_ref[...].astype(F32).reshape(1, -1))
    repeat = lanes // cos_ref.shape[1]
    cosine = jnp.concatenate([cos_ref[...]] * repeat, axis=1)
    sine = jnp.concatenate([sin_ref[...]] * repeat, axis=1)

    def project(part):
        return jnp.dot(normed, w_ref[part], preferred_element_type=F32)

    def turned(t):
        return (t * cosine + swap_halves(t) * sine).astype(BF16).astype(F32)

    queries = turned(project(0))
    keys = turned(project(1))
    values = project(2).astype(BF16).astype(F32)
    head_in = lax.broadcasted_iota(jnp.int32, (lanes, lanes), 0) // HEAD_SIZE
    head_out = lax.broadcasted_iota(jnp.int32, (lanes, lanes), 1) // HEAD_SIZE
    same_head = (head_in == head_out).astype(F32)
    score = jnp.dot(
        queries * keys,
        same_head,
        preferred_element_type=F32,
        precision=lax.Precision.HIGHEST,
    ) * (HEAD_SIZE**-0.5)
    half, chunk = new_ref.shape[1] // 2, new_ref.shape[2]
    for i in range(2 * chips):
        group = 2 * chip_away(i % chips, chips) + (core if i < chips else 1 - core)
        mine = slice(i * rows, (i + 1) * rows)
        for c in range(lanes // chunk):
            at = slice(c * chunk, (c + 1) * chunk)
            row = wire_row(rows, c, 0)
            new_ref[group, row : row + rows, :] = values[mine, at]
            new_ref[group, half + row : half + row + rows, :] = score[mine, at]
            key_ref[group, row : row + rows, :] = keys[mine, at]


def outputs_kernel(same_ref, peer_ref, new_ref, key_ref, k_ref, v_ref, side_ref, by_ref, flat_ref):
    chips, rows, _ = same_ref.shape
    core = lax.axis_index("tensor") % 2
    for step in range(chips):
        source = 2 * chip_away(step, chips)
        by_ref[source + core, :rows, :] = same_ref[step].astype(F32)
        by_ref[source + 1 - core, :rows, :] = peer_ref[step].astype(F32)
    for group in range(2 * chips):
        flat_ref[group * rows : (group + 1) * rows, :] = by_ref[group, :rows, :]
    width = side_ref.shape[1]
    side_ref[...] = flat_ref[:, pl.ds(pl.multiple_of(core * width, LANE), width)]
    lanes, chunk = k_ref.shape[1], new_ref.shape[2]
    for from_ref, to_ref in ((key_ref, k_ref), (new_ref, v_ref)):
        parts = []
        for c in range(lanes // chunk):
            row = wire_row(rows, c, 0)
            parts.append(
                jnp.concatenate(
                    [from_ref[group, row : row + rows, :] for group in range(2 * chips)], axis=0
                )
            )
        to_ref[...] = jnp.concatenate(parts, axis=1).astype(BF16)


def attention_kernel(lanes, chips, steps, *refs):
    queries, refs = dict(zip(steps, refs)), refs[len(steps) :]
    k_ref, v_ref, sink_k_ref, sink_v_ref, live_ref = refs[:5]
    out_ref, tile_ref = refs[-2:]
    rows, features, slots = k_ref.shape
    sinks = sink_k_ref.shape[1]
    copies = out_ref.shape[0]
    chunk = out_ref.shape[3]
    block = 2 * lanes
    group_heads = lanes // HEAD_SIZE
    repeat = chunk // (rows * group_heads)
    heads = max(8, block // HEAD_SIZE)
    seq_index = lax.axis_index("seq")
    chip = lax.axis_index("tensor") // 2
    head = lax.broadcasted_iota(jnp.int32, (heads, block), 0)
    own = head == lax.broadcasted_iota(jnp.int32, (heads, block), 1) // HEAD_SIZE
    scale = HEAD_SIZE**-0.5
    lives = [
        jnp.broadcast_to(live_ref[r : r + 1, :], (heads, slots)) == 1 for r in range(rows)
    ]
    first_shard = seq_index == 0

    def place(step):
        source = lax.rem(chip + chips - step, chips)
        return source, pl.ds(pl.multiple_of(source * block, block), block)

    def scores(r, step):
        _, here = place(step)
        query = jnp.concatenate(
            [
                queries[step][wire_row(rows, c, r) : wire_row(rows, c, r) + 1, :]
                for c in range(block // LANE)
            ],
            axis=1,
        )
        query = jnp.where(own, jnp.broadcast_to(query, (heads, block)), 0.0)
        score = jnp.dot(query.astype(BF16), k_ref[r, here, :], preferred_element_type=F32)
        return query, score

    def mix(r, step, query, score):
        source, here = place(step)
        sink_keys = sink_k_ref[r, :, here].astype(F32)
        sink_values = sink_v_ref[r, :, here].astype(F32)
        score = jnp.where(lives[r], score * scale, NEG)
        top = jnp.max(score, axis=1, keepdims=True)
        sink_score = []
        for i in range(sinks):
            one = jnp.sum(query * sink_keys[i : i + 1, :], axis=1, keepdims=True) * scale
            one = jnp.where(first_shard, one, NEG)
            sink_score.append(one)
            top = jnp.maximum(top, one)
        weight = jnp.where(lives[r], jnp.exp(score - top), 0.0)
        mixture = lax.dot_general(
            weight.astype(BF16),
            v_ref[r, here, :],
            (((1,), (1,)), ((), ())),
            preferred_element_type=F32,
        )
        total = jnp.sum(weight, axis=1, keepdims=True)
        for i in range(sinks):
            one = jnp.where(first_shard, jnp.exp(sink_score[i] - top), 0.0)
            total = total + one
            mixture = mixture + one.astype(BF16).astype(F32) * sink_values[i : i + 1, :]
        some = total > 0.0
        level = jnp.where(some, top + jnp.log(jnp.where(some, total, 1.0)), NEG)
        mixture = mixture / jnp.where(some, total, 1.0)
        mixture = jnp.sum(jnp.where(own, mixture, 0.0), axis=0, keepdims=True)
        for t in range(2):
            tile = steps.index(step) * 2 + t
            for c in range(lanes // chunk):
                row = wire_row(rows, c, r)
                start = t * lanes + c * chunk
                tile_ref[tile, row : row + 1, :] = mixture[:, start : start + chunk]
            here = head_row == head_lane + (t - r) * group_heads
            here = here & (head_row // group_heads == t)
            one = jnp.sum(jnp.where(here, level, 0.0), axis=0, keepdims=True)
            if r > 0:
                one = one + tile_ref[tile, LEVEL_ROW : LEVEL_ROW + 1, :]
            if r < rows - 1:
                tile_ref[tile, LEVEL_ROW : LEVEL_ROW + 1, :] = one
                continue
            for term in range(3):
                rounded = one.astype(BF16).astype(F32)
                tile_ref[tile, LEVEL_ROW + term : LEVEL_ROW + term + 1, :] = rounded
                one = one - rounded
            parts = tile_ref[tile].astype(BF16)
            for copy in range(copies):
                out_ref[copy, 2 * source + t] = parts

    tile_ref[...] = jnp.zeros_like(tile_ref)
    head_row = lax.broadcasted_iota(jnp.int32, (heads, chunk), 0)
    head_lane = lax.broadcasted_iota(jnp.int32, (heads, chunk), 1) // repeat
    todo = [(r, step) for step in steps for r in range(rows)]
    ahead = [scores(*one) for one in todo[:AHEAD]]
    for i, one in enumerate(todo):
        if i + AHEAD < len(todo):
            ahead.append(scores(*todo[i + AHEAD]))
        mix(*one, *ahead[i])


def merge_kernel(
    rows, part_ref, new_ref, w_ref, mine_ref, other_ref, rows_ref, attended_ref
):
    copies, groups, wire_rows, chunk = part_ref.shape
    lanes = w_ref.shape[0]
    flat = groups * wire_rows
    for s in range(copies):
        rows_ref[s * flat : (s + 1) * flat, :] = part_ref[s].astype(F32).reshape(flat, chunk)
    rows_ref[copies * flat :, :] = new_ref[...].reshape(flat, chunk)

    def every(row, first, count):
        return rows_ref[pl.ds(first * flat + row, count * groups, stride=wire_rows), :]

    count = rows * lanes // chunk
    terms = jnp.concatenate([every(LEVEL_ROW + term, 0, copies) for term in range(3)], axis=0)
    shape = (chunk, count * chunk)
    to = lax.broadcasted_iota(jnp.int32, shape, 1)
    to_head = (to // (rows * chunk) * chunk + to % chunk) // HEAD_SIZE
    group_heads = lanes // HEAD_SIZE
    at = (to // chunk % rows * group_heads + to_head) * (chunk // (rows * group_heads))
    spread = (lax.broadcasted_iota(jnp.int32, shape, 0) == at).astype(F32).astype(BF16)
    terms = jnp.dot(terms.astype(BF16), spread, preferred_element_type=F32)
    size = copies * groups
    levels = terms[:size] + terms[size : 2 * size] + terms[2 * size :]
    for i in range(count):
        c, r = divmod(i, rows)
        mine = every(i, 0, copies)
        parts = [mine[s * groups : (s + 1) * groups] for s in range(copies)]
        parts.append(every(i, copies, 1))
        level = [
            levels[s * groups : (s + 1) * groups, i * chunk : (i + 1) * chunk]
            for s in range(copies)
        ]
        level.append(every(wire_rows // 2 + i, copies, 1))
        top = functools.reduce(jnp.maximum, level)
        shares = [jnp.exp(one - top) for one in level]
        mixture = functools.reduce(jnp.add, [share * part for share, part in zip(shares, parts)])
        total = functools.reduce(jnp.add, shares)
        attended_ref[c, pl.ds(r, groups, stride=rows), :] = mixture / total
    attended = [attended_ref[c] for c in range(lanes // chunk)]
    attended = jnp.concatenate(attended, axis=1).astype(BF16)
    width = mine_ref.shape[1]
    core = lax.axis_index("tensor") % 2
    for half, to_ref in ((1 - core, other_ref), (core, mine_ref)):
        weights = w_ref[:, pl.ds(pl.multiple_of(half * width, LANE), width)]
        to_ref[...] = jnp.dot(attended, weights, preferred_element_type=F32)


def spread_rows(values, wide_ref):
    batch, width = values.shape
    step = 2 * LANE
    feature = lax.broadcasted_iota(jnp.int32, (step, 4 * step), 0)
    lane = lax.broadcasted_iota(jnp.int32, (step, 4 * step), 1)
    lane = jnp.where(lane < 2 * step, lane, lane - 2 * step - 1)
    spread = (2 * feature == lane).astype(F32).astype(BF16)
    pieces = width // step
    stacked = jnp.concatenate([values[:, j * step : (j + 1) * step] for j in range(pieces)], axis=0)
    wide = jnp.dot(stacked, spread, preferred_element_type=F32).astype(BF16)
    for j in range(pieces):
        part = wide[j * batch : (j + 1) * batch, :]
        at = slice(j * 2 * step, (j + 1) * 2 * step)
        wide_ref[:batch, at] = part[:, : 2 * step]
        wide_ref[batch:, at] = part[:, 2 * step :]


def half_gate_up(side, half, gain_ref, gate_up_ref, wide_ref):
    width = side.shape[1]
    units = gate_up_ref.shape[2]
    gain = gain_ref[...].astype(F32).reshape(1, -1)
    gain = jnp.where(half == 0, gain[:, :width], gain[:, width:])
    spread_rows((side * gain).astype(BF16), wide_ref)
    weights = gate_up_ref.reshape(4 * width, units)
    weights = weights[pl.ds(pl.multiple_of(half * 2 * width, 2 * width), 2 * width), :]
    gate_up = jnp.dot(wide_ref[...], weights, preferred_element_type=F32)
    return gate_up, jnp.sum(side * side, axis=1, keepdims=True)


def first_half_kernel(side_ref, gain_ref, gate_up_ref, out_ref, square_ref, wide_ref):
    core = lax.axis_index("tensor") % 2
    side = side_ref[...].astype(F32)
    out_ref[...], square = half_gate_up(side, core, gain_ref, gate_up_ref, wide_ref)
    square_ref[...] = jnp.broadcast_to(square, square_ref.shape)


def mlp_kernel(
    rows,
    mine_ref,
    other_ref,
    gain_ref,
    gate_up_ref,
    down_ref,
    first_ref,
    square_ref,
    out_ref,
    resid_ref,
    wide_ref,
    by_ref,
):
    batch, width = mine_ref.shape
    core = lax.axis_index("tensor") % 2
    mine = mine_ref[...].astype(F32)
    other = other_ref[...].astype(F32)
    gate_up, square = half_gate_up(other, 1 - core, gain_ref, gate_up_ref, wide_ref)
    meansq = (square + square_ref[:, :1]) / (2 * width)
    scale = lax.rsqrt(meansq + 1e-05)
    gate_up = gate_up + first_ref[...]
    gate = gate_up[:batch] * scale
    hidden = (gate * jax.nn.sigmoid(gate) * (gate_up[batch:] * scale)).astype(BF16)
    out = jnp.dot(hidden, down_ref[...], preferred_element_type=F32)
    resid = jnp.concatenate(
        [jnp.where(core == 0, mine, other), jnp.where(core == 0, other, mine)], axis=1
    )
    groups = out_ref.shape[0]
    for group in range(groups):
        by_ref[group, :rows, :] = resid[group * rows : (group + 1) * rows, :]
        out_ref[group] = out[group * rows : (group + 1) * rows, :].astype(BF16)
    resid_ref[...] = by_ref[lax.axis_index("tensor"), :rows, :]


def prepare_kernel(rows, pos_ref, cos_ref, sin_ref):
    core = lax.axis_index("tensor") % 2
    chips = cos_ref.shape[0] // (2 * rows)
    wide = cos_ref.shape[1]
    half = HEAD_SIZE // 2
    pair = lax.broadcasted_iota(jnp.int32, (1, wide), 1) % half
    inverse = jnp.zeros((1, wide), F32)
    for i in range(half):
        inverse = jnp.where(pair == i, np.float32(ROTARY_BASE ** (-2 * i / HEAD_SIZE)), inverse)

    shape = cos_ref.shape
    row = lax.broadcasted_iota(jnp.int32, shape, 0)
    position = jnp.zeros(shape, F32)
    for i in range(shape[0]):
        group, r = divmod(i, rows)
        parity = core if group < chips else 1 - core
        request = (2 * chip_away(group % chips, chips) + parity) * rows + r
        position = jnp.where(row == i, pos_ref[request].astype(F32), position)
    angle = position * inverse
    sine = jnp.sin(angle)
    lane = lax.broadcasted_iota(jnp.int32, shape, 1)
    cos_ref[...] = jnp.cos(angle)
    sin_ref[...] = jnp.where(lane % HEAD_SIZE < half, -sine, sine)


def mark_live(len_ref, pos_ref, mask_ref, slot_pos_ref, live_ref):
    rows, slots = mask_ref.shape
    slot = lax.axis_index("seq") * slots + lax.broadcasted_iota(jnp.int32, (1, slots), 1)
    first_row = lax.axis_index("tensor") * rows
    for r in range(rows):
        own_len = len_ref[first_row + r]
        own_pos = pos_ref[first_row + r]
        slot_at = slot_pos_ref[r : r + 1, :]
        live = (slot < own_len) & (mask_ref[r : r + 1, :] == 1)
        live = live & (slot_at < own_pos) & (own_pos - slot_at < WINDOW)
        live_ref[r : r + 1, :] = live.astype(jnp.int32)


def call(kernel, out, inputs, specs=None, scratch=(), limit=6, name=None, flops=0, aliases={}):
    return pl.pallas_call(
        kernel,
        out_shape=out,
        in_specs=specs or [VMEM_SPEC] * len(inputs),
        out_specs=jax.tree.map(lambda _: VMEM_SPEC, out),
        scratch_shapes=scratch,
        input_output_aliases=aliases,
        compiler_params=pltpu.CompilerParams(vmem_limit_bytes=limit * MIB),
        name=name,
        cost_estimate=pl.CostEstimate(
            flops=flops,
            bytes_accessed=sum(a.size * a.dtype.itemsize for a in inputs),
            transcendentals=0,
        ),
    )(*inputs)


def per_device(
    shards,
    groups,
    states,
    attn_gain,
    w_qkv,
    w_out,
    mlp_gain,
    w_gate_up,
    w_down,
    key_cache,
    value_cache,
    sink_keys,
    sink_values,
    cache_len,
    slot_mask,
    slot_pos,
    new_pos,
):
    rows, width = states.shape
    batch = rows * groups
    lanes = w_qkv.shape[2]
    sds = jax.ShapeDtypeStruct
    chunk = min(lanes, LANE)
    wire_rows = max(8, 2 * rows * lanes // chunk)

    chips = groups // 2
    turn = sds((batch, chunk), F32)
    cosine, sine = call(
        functools.partial(prepare_kernel, rows),
        (turn, turn),
        (new_pos,),
        specs=[SMEM_SPEC],
        name="prepare",
        flops=PREP_FLOPS,
    )
    across = [(i, i ^ 1) for i in range(groups)]
    hops = [[(i, (i + step) % groups) for i in range(groups)] for step in range(2, groups, 2)]
    column = [states] + [lax.ppermute(states, "tensor", hop) for hop in hops]
    w_qkv = jnp.transpose(w_qkv, (1, 0, 2))
    w_peer = lax.ppermute(w_qkv, "tensor", across)
    query_wire = sds((max(8, 2 * rows * lanes // LANE), LANE), F32)
    queries = call(
        functools.partial(query_kernel, rows, chips),
        (query_wire,) * chips,
        (*column, attn_gain, w_qkv, w_peer, cosine, sine),
        name="query",
        flops=QKV_FLOPS,
    )
    same = jnp.stack(column)
    peer = lax.ppermute(same, "tensor", across)
    same, *queries = lax.optimization_barrier((same, *queries))
    queries = [queries[0]] + [
        lax.ppermute(query, "tensor", hop) for query, hop in zip(queries[1:], hops)
    ]
    wire = sds((groups, wire_rows, chunk), F32)
    new_part, key_part, live = call(
        functools.partial(new_token_kernel, rows),
        (wire, wire, sds(slot_mask.shape, jnp.int32)),
        (cache_len, new_pos, slot_mask, slot_pos, same, peer, attn_gain, w_qkv, cosine, sine),
        specs=[SMEM_SPEC] * 2 + [VMEM_SPEC] * 8,
        name="new_token",
        flops=QKV_FLOPS,
    )
    sink_keys = jnp.transpose(sink_keys, (0, 2, 1))
    sink_values = jnp.transpose(sink_values, (0, 2, 1))

    def attention(steps, arrays, aliases, name):
        return call(
            functools.partial(attention_kernel, lanes, chips, steps),
            sds((shards, groups, 8, chunk), BF16),
            arrays,
            scratch=[pltpu.VMEM((2 * len(steps), 8, chunk), F32)],
            limit=8,
            name=name,
            flops=ATT_FLOPS,
            aliases=aliases,
        )

    cache = (key_cache, value_cache, sink_keys, sink_values, live)
    part = attention((0,), (queries[0], *cache), {}, "own_heads")
    first, new_part, part = lax.optimization_barrier((queries[1:-1], new_part, part))
    queries = [queries[0], *first, queries[-1]]
    middle = tuple(range(1, chips - 1))
    part = attention(middle, (*queries[1:-1], *cache, part), {len(middle) + 5: 0}, "middle_heads")
    last, part = lax.optimization_barrier((queries[-1], part))
    part = attention((chips - 1,), (last, *cache, part), {6: 0}, "last_heads")
    part = lax.all_to_all(
        part.reshape(shards * groups, 8, chunk), ("seq", "tensor"), 0, 0, tiled=True
    ).reshape(shards, groups, 8, chunk)
    side = sds((batch, width // 2), F32)
    mine, other = call(
        functools.partial(merge_kernel, rows),
        (side, side),
        (part, new_part, w_out),
        scratch=[
            pltpu.VMEM(((shards + 1) * groups * 8, chunk), F32),
            pltpu.VMEM((lanes // chunk, batch, chunk), F32),
        ],
        name="merge",
        flops=MERGE_FLOPS,
    )
    chip = (mine + lax.ppermute(other, "tensor", across)).astype(BF16)
    flat = sds((batch, lanes), BF16)
    chip, same, peer, new_part, key_part = lax.optimization_barrier(
        (chip, same, peer, new_part, key_part)
    )
    new_keys, new_values, own_side = call(
        outputs_kernel,
        (flat, flat, side),
        (same, peer, new_part, key_part),
        scratch=[pltpu.VMEM((groups, 8, width), F32), pltpu.VMEM((batch, width), F32)],
        name="outputs",
    )
    total = chip.astype(F32)
    for which in range(0, -len(hops), -1):
        total = total + lax.ppermute(chip, "tensor", hops[which]).astype(F32)
    side_resid = (own_side + total).astype(BF16)
    other_resid = lax.ppermute(side_resid, "tensor", across)
    units = w_gate_up.shape[2]
    first_half, square = call(
        first_half_kernel,
        (sds((2 * batch, units), F32), sds((batch, LANE), F32)),
        (side_resid, mlp_gain, w_gate_up),
        scratch=[pltpu.VMEM((2 * batch, width), BF16)],
        limit=8,
        name="first_half",
        flops=2 * batch * width * units,
    )
    partial, own_resid = call(
        functools.partial(mlp_kernel, rows),
        (sds((groups, rows, width), BF16), sds((rows, width), F32)),
        (side_resid, other_resid, mlp_gain, w_gate_up, w_down, first_half, square),
        scratch=[pltpu.VMEM((2 * batch, width), BF16), pltpu.VMEM((groups, 8, width), F32)],
        limit=8,
        name="mlp",
        flops=4 * batch * width * units,
    )
    partial = lax.all_to_all(partial, "tensor", 0, 0, tiled=True)
    out_states = (own_resid + jnp.sum(partial.astype(F32), axis=0)).astype(BF16)
    return out_states, new_keys, new_values


def solution(mesh):
    in_specs = (
        P("tensor", None),
        P(),
        P(None, None, "tensor"),
        P("tensor", None),
        P(),
        P(None, None, "tensor"),
        P("tensor", None),
        P("tensor", None, "seq"),
        P("tensor", None, "seq"),
        P("tensor", None, None),
        P("tensor", None, None),
        P(),
        P("tensor", "seq"),
        P("tensor", "seq"),
        P(),
    )
    out_specs = (P("tensor", None), P(None, "tensor"), P(None, "tensor"))
    body = functools.partial(per_device, mesh.shape["seq"], mesh.shape["tensor"])
    return jax.shard_map(
        body, mesh=mesh, in_specs=in_specs, out_specs=out_specs, check_vma=False
    )
```

```python
import functools

import jax
import jax.numpy as jnp
import numpy as np
from jax import lax
from jax.experimental import pallas as pl
from jax.experimental.pallas import tpu as pltpu
from jax.sharding import PartitionSpec as P

HEAD_SIZE = 64
WINDOW = 4096
ROTARY_BASE = 130000.0
NEG = -1e30
LANE = 128
MIB = 2**20
AHEAD = 1
LEVEL_ROW = 4
PREP_FLOPS = 20_000_000_000
QKV_FLOPS = 2_000_000_000
ATT_FLOPS = 10_000_000_000
MERGE_FLOPS = 10_000_000_000

VMEM_SPEC = pl.BlockSpec(memory_space=pltpu.VMEM)
SMEM_SPEC = pl.BlockSpec(memory_space=pltpu.SMEM)
F32 = jnp.float32
BF16 = jnp.bfloat16


def normed_rows(values, gain):
    meansq = jnp.mean(values * values, axis=-1, keepdims=True)
    return (values * lax.rsqrt(meansq + 1e-05) * gain).astype(BF16)


def swap_halves(tensor):
    width = tensor.shape[1]
    half = HEAD_SIZE // 2
    if width == HEAD_SIZE:
        return jnp.concatenate([tensor[:, half:], tensor[:, :half]], axis=1)
    lane = lax.broadcasted_iota(jnp.int32, tensor.shape, 1)
    upper = pltpu.roll(tensor, width - half, 1)
    lower = pltpu.roll(tensor, half, 1)
    return jnp.where(lane % HEAD_SIZE < half, upper, lower)


def wire_row(rows, lane_chunk, row):
    return lane_chunk * rows + row


def query_kernel(rows, chips, *refs):
    states, refs = refs[:chips], refs[chips:]
    gain_ref, own_ref, peer_ref, cos_ref, sin_ref = refs[:5]
    outs = refs[5:]
    core = lax.axis_index("tensor") % 2
    values = jnp.concatenate([ref[...].astype(F32) for ref in states], axis=0)
    normed = normed_rows(values, gain_ref[...].astype(F32).reshape(1, -1))
    own = jnp.dot(normed, own_ref[0], preferred_element_type=F32)
    peer = jnp.dot(normed, peer_ref[0], preferred_element_type=F32)
    queries = jnp.concatenate(
        [jnp.where(core == 0, own, peer), jnp.where(core == 0, peer, own)], axis=1
    )
    count, repeat = queries.shape[0], queries.shape[1] // cos_ref.shape[1]
    cosine = jnp.concatenate([cos_ref[:count, :]] * repeat, axis=1)
    sine = jnp.concatenate([sin_ref[:count, :]] * repeat, axis=1)
    queries = (queries * cosine + swap_halves(queries) * sine).astype(BF16).astype(F32)
    for step in range(chips):
        first = (chips - step) % chips * rows
        out = outs[step]
        if rows * queries.shape[1] // LANE < out.shape[0]:
            out[...] = jnp.zeros_like(out)
        for c in range(queries.shape[1] // LANE):
            at = slice(c * LANE, (c + 1) * LANE)
            row = wire_row(rows, c, 0)
            out[row : row + rows, :] = queries[first : first + rows, at]


def chip_away(step, chips):
    return lax.rem(lax.axis_index("tensor") // 2 + chips - step, chips)


def new_token_kernel(
    rows,
    len_ref,
    pos_ref,
    mask_ref,
    slot_pos_ref,
    same_ref,
    peer_ref,
    gain_ref,
    w_ref,
    cos_ref,
    sin_ref,
    new_ref,
    key_ref,
    live_ref,
):
    mark_live(len_ref, pos_ref, mask_ref, slot_pos_ref, live_ref)
    lanes = w_ref.shape[2]
    core = lax.axis_index("tensor") % 2
    chips = same_ref.shape[0]
    values = jnp.concatenate(
        [ref[step].astype(F32) for ref in (same_ref, peer_ref) for step in range(chips)], axis=0
    )
    normed = normed_rows(values, gain_ref[...].astype(F32).reshape(1, -1))
    repeat = lanes // cos_ref.shape[1]
    cosine = jnp.concatenate([cos_ref[...]] * repeat, axis=1)
    sine = jnp.concatenate([sin_ref[...]] * repeat, axis=1)

    def project(part):
        return jnp.dot(normed, w_ref[part], preferred_element_type=F32)

    def turned(t):
        return (t * cosine + swap_halves(t) * sine).astype(BF16).astype(F32)

    queries = turned(project(0))
    keys = turned(project(1))
    values = project(2).astype(BF16).astype(F32)
    head_in = lax.broadcasted_iota(jnp.int32, (lanes, lanes), 0) // HEAD_SIZE
    head_out = lax.broadcasted_iota(jnp.int32, (lanes, lanes), 1) // HEAD_SIZE
    same_head = (head_in == head_out).astype(F32)
    score = jnp.dot(
        queries * keys,
        same_head,
        preferred_element_type=F32,
        precision=lax.Precision.HIGHEST,
    ) * (HEAD_SIZE**-0.5)
    half, chunk = new_ref.shape[1] // 2, new_ref.shape[2]
    for i in range(2 * chips):
        group = 2 * chip_away(i % chips, chips) + (core if i < chips else 1 - core)
        mine = slice(i * rows, (i + 1) * rows)
        for c in range(lanes // chunk):
            at = slice(c * chunk, (c + 1) * chunk)
            row = wire_row(rows, c, 0)
            new_ref[group, row : row + rows, :] = values[mine, at]
            new_ref[group, half + row : half + row + rows, :] = score[mine, at]
            key_ref[group, row : row + rows, :] = keys[mine, at]


def outputs_kernel(same_ref, peer_ref, new_ref, key_ref, k_ref, v_ref, side_ref, by_ref, flat_ref):
    chips, rows, _ = same_ref.shape
    core = lax.axis_index("tensor") % 2
    for step in range(chips):
        source = 2 * chip_away(step, chips)
        by_ref[source + core, :rows, :] = same_ref[step].astype(F32)
        by_ref[source + 1 - core, :rows, :] = peer_ref[step].astype(F32)
    for group in range(2 * chips):
        flat_ref[group * rows : (group + 1) * rows, :] = by_ref[group, :rows, :]
    width = side_ref.shape[1]
    side_ref[...] = flat_ref[:, pl.ds(pl.multiple_of(core * width, LANE), width)]
    lanes, chunk = k_ref.shape[1], new_ref.shape[2]
    for from_ref, to_ref in ((key_ref, k_ref), (new_ref, v_ref)):
        parts = []
        for c in range(lanes // chunk):
            row = wire_row(rows, c, 0)
            parts.append(
                jnp.concatenate(
                    [from_ref[group, row : row + rows, :] for group in range(2 * chips)], axis=0
                )
            )
        to_ref[...] = jnp.concatenate(parts, axis=1).astype(BF16)


def attention_kernel(lanes, chips, steps, *refs):
    queries, refs = dict(zip(steps, refs)), refs[len(steps) :]
    k_ref, v_ref, sink_k_ref, sink_v_ref, live_ref = refs[:5]
    out_ref, tile_ref = refs[-2:]
    rows, features, slots = k_ref.shape
    sinks = sink_k_ref.shape[1]
    copies = out_ref.shape[0]
    chunk = out_ref.shape[3]
    block = 2 * lanes
    group_heads = lanes // HEAD_SIZE
    repeat = chunk // (rows * group_heads)
    heads = max(8, block // HEAD_SIZE)
    seq_index = lax.axis_index("seq")
    chip = lax.axis_index("tensor") // 2
    head = lax.broadcasted_iota(jnp.int32, (heads, block), 0)
    own = head == lax.broadcasted_iota(jnp.int32, (heads, block), 1) // HEAD_SIZE
    scale = HEAD_SIZE**-0.5
    lives = [
        jnp.broadcast_to(live_ref[r : r + 1, :], (heads, slots)) == 1 for r in range(rows)
    ]
    first_shard = seq_index == 0

    def place(step):
        source = lax.rem(chip + chips - step, chips)
        return source, pl.ds(pl.multiple_of(source * block, block), block)

    def scores(r, step):
        _, here = place(step)
        query = jnp.concatenate(
            [
                queries[step][wire_row(rows, c, r) : wire_row(rows, c, r) + 1, :]
                for c in range(block // LANE)
            ],
            axis=1,
        )
        query = jnp.where(own, jnp.broadcast_to(query, (heads, block)), 0.0)
        score = jnp.dot(query.astype(BF16), k_ref[r, here, :], preferred_element_type=F32)
        return query, score

    def mix(r, step, query, score):
        source, here = place(step)
        sink_keys = sink_k_ref[r, :, here].astype(F32)
        sink_values = sink_v_ref[r, :, here].astype(F32)
        score = jnp.where(lives[r], score * scale, NEG)
        top = jnp.max(score, axis=1, keepdims=True)
        sink_score = []
        for i in range(sinks):
            one = jnp.sum(query * sink_keys[i : i + 1, :], axis=1, keepdims=True) * scale
            one = jnp.where(first_shard, one, NEG)
            sink_score.append(one)
            top = jnp.maximum(top, one)
        weight = jnp.where(lives[r], jnp.exp(score - top), 0.0)
        mixture = lax.dot_general(
            weight.astype(BF16),
            v_ref[r, here, :],
            (((1,), (1,)), ((), ())),
            preferred_element_type=F32,
        )
        total = jnp.sum(weight, axis=1, keepdims=True)
        for i in range(sinks):
            one = jnp.where(first_shard, jnp.exp(sink_score[i] - top), 0.0)
            total = total + one
            mixture = mixture + one.astype(BF16).astype(F32) * sink_values[i : i + 1, :]
        some = total > 0.0
        level = jnp.where(some, top + jnp.log(jnp.where(some, total, 1.0)), NEG)
        mixture = mixture / jnp.where(some, total, 1.0)
        mixture = jnp.sum(jnp.where(own, mixture, 0.0), axis=0, keepdims=True)
        for t in range(2):
            tile = steps.index(step) * 2 + t
            for c in range(lanes // chunk):
                row = wire_row(rows, c, r)
                start = t * lanes + c * chunk
                tile_ref[tile, row : row + 1, :] = mixture[:, start : start + chunk]
            here = head_row == head_lane + (t - r) * group_heads
            here = here & (head_row // group_heads == t)
            one = jnp.sum(jnp.where(here, level, 0.0), axis=0, keepdims=True)
            if r > 0:
                one = one + tile_ref[tile, LEVEL_ROW : LEVEL_ROW + 1, :]
            if r < rows - 1:
                tile_ref[tile, LEVEL_ROW : LEVEL_ROW + 1, :] = one
                continue
            for term in range(3):
                rounded = one.astype(BF16).astype(F32)
                tile_ref[tile, LEVEL_ROW + term : LEVEL_ROW + term + 1, :] = rounded
                one = one - rounded
            parts = tile_ref[tile].astype(BF16)
            for copy in range(copies):
                out_ref[copy, 2 * source + t] = parts

    tile_ref[...] = jnp.zeros_like(tile_ref)
    head_row = lax.broadcasted_iota(jnp.int32, (heads, chunk), 0)
    head_lane = lax.broadcasted_iota(jnp.int32, (heads, chunk), 1) // repeat
    todo = [(r, step) for step in steps for r in range(rows)]
    ahead = [scores(*one) for one in todo[:AHEAD]]
    for i, one in enumerate(todo):
        if i + AHEAD < len(todo):
            ahead.append(scores(*todo[i + AHEAD]))
        mix(*one, *ahead[i])


def merge_kernel(
    rows, part_ref, new_ref, w_ref, mine_ref, other_ref, rows_ref, attended_ref
):
    copies, groups, wire_rows, chunk = part_ref.shape
    lanes = w_ref.shape[0]
    flat = groups * wire_rows
    for s in range(copies):
        rows_ref[s * flat : (s + 1) * flat, :] = part_ref[s].astype(F32).reshape(flat, chunk)
    rows_ref[copies * flat :, :] = new_ref[...].reshape(flat, chunk)

    def every(row, first, count):
        return rows_ref[pl.ds(first * flat + row, count * groups, stride=wire_rows), :]

    count = rows * lanes // chunk
    terms = jnp.concatenate([every(LEVEL_ROW + term, 0, copies) for term in range(3)], axis=0)
    shape = (chunk, count * chunk)
    to = lax.broadcasted_iota(jnp.int32, shape, 1)
    to_head = (to // (rows * chunk) * chunk + to % chunk) // HEAD_SIZE
    group_heads = lanes // HEAD_SIZE
    at = (to // chunk % rows * group_heads + to_head) * (chunk // (rows * group_heads))
    spread = (lax.broadcasted_iota(jnp.int32, shape, 0) == at).astype(F32).astype(BF16)
    terms = jnp.dot(terms.astype(BF16), spread, preferred_element_type=F32)
    size = copies * groups
    levels = terms[:size] + terms[size : 2 * size] + terms[2 * size :]
    for i in range(count):
        c, r = divmod(i, rows)
        mine = every(i, 0, copies)
        parts = [mine[s * groups : (s + 1) * groups] for s in range(copies)]
        parts.append(every(i, copies, 1))
        level = [
            levels[s * groups : (s + 1) * groups, i * chunk : (i + 1) * chunk]
            for s in range(copies)
        ]
        level.append(every(wire_rows // 2 + i, copies, 1))
        top = functools.reduce(jnp.maximum, level)
        shares = [jnp.exp(one - top) for one in level]
        mixture = functools.reduce(jnp.add, [share * part for share, part in zip(shares, parts)])
        total = functools.reduce(jnp.add, shares)
        attended_ref[c, pl.ds(r, groups, stride=rows), :] = mixture / total
    attended = [attended_ref[c] for c in range(lanes // chunk)]
    attended = jnp.concatenate(attended, axis=1).astype(BF16)
    width = mine_ref.shape[1]
    core = lax.axis_index("tensor") % 2
    for half, to_ref in ((1 - core, other_ref), (core, mine_ref)):
        weights = w_ref[:, pl.ds(pl.multiple_of(half * width, LANE), width)]
        to_ref[...] = jnp.dot(attended, weights, preferred_element_type=F32)


def spread_rows(values, wide_ref):
    batch, width = values.shape
    step = 2 * LANE
    feature = lax.broadcasted_iota(jnp.int32, (step, 4 * step), 0)
    lane = lax.broadcasted_iota(jnp.int32, (step, 4 * step), 1)
    lane = jnp.where(lane < 2 * step, lane, lane - 2 * step - 1)
    spread = (2 * feature == lane).astype(F32).astype(BF16)
    pieces = width // step
    stacked = jnp.concatenate([values[:, j * step : (j + 1) * step] for j in range(pieces)], axis=0)
    wide = jnp.dot(stacked, spread, preferred_element_type=F32).astype(BF16)
    for j in range(pieces):
        part = wide[j * batch : (j + 1) * batch, :]
        at = slice(j * 2 * step, (j + 1) * 2 * step)
        wide_ref[:batch, at] = part[:, : 2 * step]
        wide_ref[batch:, at] = part[:, 2 * step :]


def half_gate_up(side, half, gain_ref, gate_up_ref, wide_ref):
    width = side.shape[1]
    units = gate_up_ref.shape[2]
    gain = gain_ref[...].astype(F32).reshape(1, -1)
    gain = jnp.where(half == 0, gain[:, :width], gain[:, width:])
    spread_rows((side * gain).astype(BF16), wide_ref)
    weights = gate_up_ref.reshape(4 * width, units)
    weights = weights[pl.ds(pl.multiple_of(half * 2 * width, 2 * width), 2 * width), :]
    gate_up = jnp.dot(wide_ref[...], weights, preferred_element_type=F32)
    return gate_up, jnp.sum(side * side, axis=1, keepdims=True)


def first_half_kernel(side_ref, gain_ref, gate_up_ref, out_ref, square_ref, wide_ref):
    core = lax.axis_index("tensor") % 2
    side = side_ref[...].astype(F32)
    out_ref[...], square = half_gate_up(side, core, gain_ref, gate_up_ref, wide_ref)
    square_ref[...] = jnp.broadcast_to(square, square_ref.shape)


def mlp_kernel(
    rows,
    mine_ref,
    other_ref,
    gain_ref,
    gate_up_ref,
    down_ref,
    first_ref,
    square_ref,
    out_ref,
    resid_ref,
    wide_ref,
    by_ref,
):
    batch, width = mine_ref.shape
    core = lax.axis_index("tensor") % 2
    mine = mine_ref[...].astype(F32)
    other = other_ref[...].astype(F32)
    gate_up, square = half_gate_up(other, 1 - core, gain_ref, gate_up_ref, wide_ref)
    meansq = (square + square_ref[:, :1]) / (2 * width)
    scale = lax.rsqrt(meansq + 1e-05)
    gate_up = gate_up + first_ref[...]
    gate = gate_up[:batch] * scale
    hidden = (gate * jax.nn.sigmoid(gate) * (gate_up[batch:] * scale)).astype(BF16)
    out = jnp.dot(hidden, down_ref[...], preferred_element_type=F32)
    resid = jnp.concatenate(
        [jnp.where(core == 0, mine, other), jnp.where(core == 0, other, mine)], axis=1
    )
    groups = out_ref.shape[0]
    for group in range(groups):
        by_ref[group, :rows, :] = resid[group * rows : (group + 1) * rows, :]
        out_ref[group] = out[group * rows : (group + 1) * rows, :].astype(BF16)
    resid_ref[...] = by_ref[lax.axis_index("tensor"), :rows, :]


def prepare_kernel(rows, pos_ref, cos_ref, sin_ref):
    core = lax.axis_index("tensor") % 2
    chips = cos_ref.shape[0] // (2 * rows)
    wide = cos_ref.shape[1]
    half = HEAD_SIZE // 2
    pair = lax.broadcasted_iota(jnp.int32, (1, wide), 1) % half
    inverse = jnp.zeros((1, wide), F32)
    for i in range(half):
        inverse = jnp.where(pair == i, np.float32(ROTARY_BASE ** (-2 * i / HEAD_SIZE)), inverse)

    shape = cos_ref.shape
    row = lax.broadcasted_iota(jnp.int32, shape, 0)
    position = jnp.zeros(shape, F32)
    for i in range(shape[0]):
        group, r = divmod(i, rows)
        parity = core if group < chips else 1 - core
        request = (2 * chip_away(group % chips, chips) + parity) * rows + r
        position = jnp.where(row == i, pos_ref[request].astype(F32), position)
    angle = position * inverse
    sine = jnp.sin(angle)
    lane = lax.broadcasted_iota(jnp.int32, shape, 1)
    cos_ref[...] = jnp.cos(angle)
    sin_ref[...] = jnp.where(lane % HEAD_SIZE < half, -sine, sine)


def mark_live(len_ref, pos_ref, mask_ref, slot_pos_ref, live_ref):
    rows, slots = mask_ref.shape
    slot = lax.axis_index("seq") * slots + lax.broadcasted_iota(jnp.int32, (1, slots), 1)
    first_row = lax.axis_index("tensor") * rows
    for r in range(rows):
        own_len = len_ref[first_row + r]
        own_pos = pos_ref[first_row + r]
        slot_at = slot_pos_ref[r : r + 1, :]
        live = (slot < own_len) & (mask_ref[r : r + 1, :] == 1)
        live = live & (slot_at < own_pos) & (own_pos - slot_at < WINDOW)
        live_ref[r : r + 1, :] = live.astype(jnp.int32)


def call(kernel, out, inputs, specs=None, scratch=(), limit=6, name=None, flops=0, aliases={}):
    return pl.pallas_call(
        kernel,
        out_shape=out,
        in_specs=specs or [VMEM_SPEC] * len(inputs),
        out_specs=jax.tree.map(lambda _: VMEM_SPEC, out),
        scratch_shapes=scratch,
        input_output_aliases=aliases,
        compiler_params=pltpu.CompilerParams(vmem_limit_bytes=limit * MIB),
        name=name,
        cost_estimate=pl.CostEstimate(
            flops=flops,
            bytes_accessed=sum(a.size * a.dtype.itemsize for a in inputs),
            transcendentals=0,
        ),
    )(*inputs)


def per_device(
    shards,
    groups,
    states,
    attn_gain,
    w_qkv,
    w_out,
    mlp_gain,
    w_gate_up,
    w_down,
    key_cache,
    value_cache,
    sink_keys,
    sink_values,
    cache_len,
    slot_mask,
    slot_pos,
    new_pos,
):
    rows, width = states.shape
    batch = rows * groups
    lanes = w_qkv.shape[2]
    sds = jax.ShapeDtypeStruct
    chunk = min(lanes, LANE)
    wire_rows = max(8, 2 * rows * lanes // chunk)

    chips = groups // 2
    turn = sds((batch, chunk), F32)
    cosine, sine = call(
        functools.partial(prepare_kernel, rows),
        (turn, turn),
        (new_pos,),
        specs=[SMEM_SPEC],
        name="prepare",
        flops=PREP_FLOPS,
    )
    across = [(i, i ^ 1) for i in range(groups)]
    hops = [[(i, (i + step) % groups) for i in range(groups)] for step in range(2, groups, 2)]
    column = [states] + [lax.ppermute(states, "tensor", hop) for hop in hops]
    w_qkv = jnp.transpose(w_qkv, (1, 0, 2))
    w_peer = lax.ppermute(w_qkv, "tensor", across)
    query_wire = sds((max(8, 2 * rows * lanes // LANE), LANE), F32)
    queries = call(
        functools.partial(query_kernel, rows, chips),
        (query_wire,) * chips,
        (*column, attn_gain, w_qkv, w_peer, cosine, sine),
        name="query",
        flops=QKV_FLOPS,
    )
    same = jnp.stack(column)
    same, *queries = lax.optimization_barrier((same, *queries))
    peer = lax.ppermute(same, "tensor", across)
    queries = [queries[0]] + [
        lax.ppermute(query, "tensor", hop) for query, hop in zip(queries[1:], hops)
    ]
    wire = sds((groups, wire_rows, chunk), F32)
    new_part, key_part, live = call(
        functools.partial(new_token_kernel, rows),
        (wire, wire, sds(slot_mask.shape, jnp.int32)),
        (cache_len, new_pos, slot_mask, slot_pos, same, peer, attn_gain, w_qkv, cosine, sine),
        specs=[SMEM_SPEC] * 2 + [VMEM_SPEC] * 8,
        name="new_token",
        flops=QKV_FLOPS,
    )
    sink_keys = jnp.transpose(sink_keys, (0, 2, 1))
    sink_values = jnp.transpose(sink_values, (0, 2, 1))

    def attention(steps, arrays, aliases, name):
        return call(
            functools.partial(attention_kernel, lanes, chips, steps),
            sds((shards, groups, 8, chunk), BF16),
            arrays,
            scratch=[pltpu.VMEM((2 * len(steps), 8, chunk), F32)],
            limit=8,
            name=name,
            flops=ATT_FLOPS,
            aliases=aliases,
        )

    cache = (key_cache, value_cache, sink_keys, sink_values, live)
    part = attention((0,), (queries[0], *cache), {}, "own_heads")
    first, new_part, part = lax.optimization_barrier((queries[1:-1], new_part, part))
    queries = [queries[0], *first, queries[-1]]
    middle = tuple(range(1, chips - 1))
    part = attention(middle, (*queries[1:-1], *cache, part), {len(middle) + 5: 0}, "middle_heads")
    last, part = lax.optimization_barrier((queries[-1], part))
    part = attention((chips - 1,), (last, *cache, part), {6: 0}, "last_heads")
    part = lax.all_to_all(
        part.reshape(shards * groups, 8, chunk), ("seq", "tensor"), 0, 0, tiled=True
    ).reshape(shards, groups, 8, chunk)
    side = sds((batch, width // 2), F32)
    mine, other = call(
        functools.partial(merge_kernel, rows),
        (side, side),
        (part, new_part, w_out),
        scratch=[
            pltpu.VMEM(((shards + 1) * groups * 8, chunk), F32),
            pltpu.VMEM((lanes // chunk, batch, chunk), F32),
        ],
        name="merge",
        flops=MERGE_FLOPS,
    )
    chip = (mine + lax.ppermute(other, "tensor", across)).astype(BF16)
    flat = sds((batch, lanes), BF16)
    chip, same, peer, new_part, key_part = lax.optimization_barrier(
        (chip, same, peer, new_part, key_part)
    )
    new_keys, new_values, own_side = call(
        outputs_kernel,
        (flat, flat, side),
        (same, peer, new_part, key_part),
        scratch=[pltpu.VMEM((groups, 8, width), F32), pltpu.VMEM((batch, width), F32)],
        name="outputs",
    )
    total = chip.astype(F32)
    for which in range(0, -len(hops), -1):
        total = total + lax.ppermute(chip, "tensor", hops[which]).astype(F32)
    side_resid = (own_side + total).astype(BF16)
    other_resid = lax.ppermute(side_resid, "tensor", across)
    units = w_gate_up.shape[2]
    first_half, square = call(
        first_half_kernel,
        (sds((2 * batch, units), F32), sds((batch, LANE), F32)),
        (side_resid, mlp_gain, w_gate_up),
        scratch=[pltpu.VMEM((2 * batch, width), BF16)],
        limit=8,
        name="first_half",
        flops=2 * batch * width * units,
    )
    partial, own_resid = call(
        functools.partial(mlp_kernel, rows),
        (sds((groups, rows, width), BF16), sds((rows, width), F32)),
        (side_resid, other_resid, mlp_gain, w_gate_up, w_down, first_half, square),
        scratch=[pltpu.VMEM((2 * batch, width), BF16), pltpu.VMEM((groups, 8, width), F32)],
        limit=8,
        name="mlp",
        flops=4 * batch * width * units,
    )
    partial = lax.all_to_all(partial, "tensor", 0, 0, tiled=True)
    out_states = (own_resid + jnp.sum(partial.astype(F32), axis=0)).astype(BF16)
    return out_states, new_keys, new_values


def solution(mesh):
    in_specs = (
        P("tensor", None),
        P(),
        P(None, None, "tensor"),
        P("tensor", None),
        P(),
        P(None, None, "tensor"),
        P("tensor", None),
        P("tensor", None, "seq"),
        P("tensor", None, "seq"),
        P("tensor", None, None),
        P("tensor", None, None),
        P(),
        P("tensor", "seq"),
        P("tensor", "seq"),
        P(),
    )
    out_specs = (P("tensor", None), P(None, "tensor"), P(None, "tensor"))
    body = functools.partial(per_device, mesh.shape["seq"], mesh.shape["tensor"])
    return jax.shard_map(
        body, mesh=mesh, in_specs=in_specs, out_specs=out_specs, check_vma=False
    )
```

```python
import functools

import jax
import jax.numpy as jnp
import numpy as np
from jax import lax
from jax.experimental import pallas as pl
from jax.experimental.pallas import tpu as pltpu
from jax.sharding import PartitionSpec as P

HEAD_SIZE = 64
WINDOW = 4096
ROTARY_BASE = 130000.0
NEG = -1e30
LANE = 128
MIB = 2**20
AHEAD = 1
LEVEL_ROW = 4
PREP_FLOPS = 20_000_000_000
QKV_FLOPS = 2_000_000_000
ATT_FLOPS = 10_000_000_000
MERGE_FLOPS = 10_000_000_000

VMEM_SPEC = pl.BlockSpec(memory_space=pltpu.VMEM)
SMEM_SPEC = pl.BlockSpec(memory_space=pltpu.SMEM)
F32 = jnp.float32
BF16 = jnp.bfloat16


def normed_rows(values, gain):
    meansq = jnp.mean(values * values, axis=-1, keepdims=True)
    return (values * lax.rsqrt(meansq + 1e-05) * gain).astype(BF16)


def swap_halves(tensor):
    width = tensor.shape[1]
    half = HEAD_SIZE // 2
    if width == HEAD_SIZE:
        return jnp.concatenate([tensor[:, half:], tensor[:, :half]], axis=1)
    lane = lax.broadcasted_iota(jnp.int32, tensor.shape, 1)
    upper = pltpu.roll(tensor, width - half, 1)
    lower = pltpu.roll(tensor, half, 1)
    return jnp.where(lane % HEAD_SIZE < half, upper, lower)


def wire_row(rows, lane_chunk, row):
    return lane_chunk * rows + row


def query_kernel(rows, chips, *refs):
    states, refs = refs[:chips], refs[chips:]
    gain_ref, own_ref, peer_ref, cos_ref, sin_ref = refs[:5]
    outs = refs[5:]
    core = lax.axis_index("tensor") % 2
    values = jnp.concatenate([ref[...].astype(F32) for ref in states], axis=0)
    normed = normed_rows(values, gain_ref[...].astype(F32).reshape(1, -1))
    own = jnp.dot(normed, own_ref[0], preferred_element_type=F32)
    peer = jnp.dot(normed, peer_ref[0], preferred_element_type=F32)
    queries = jnp.concatenate(
        [jnp.where(core == 0, own, peer), jnp.where(core == 0, peer, own)], axis=1
    )
    count, repeat = queries.shape[0], queries.shape[1] // cos_ref.shape[1]
    cosine = jnp.concatenate([cos_ref[:count, :]] * repeat, axis=1)
    sine = jnp.concatenate([sin_ref[:count, :]] * repeat, axis=1)
    queries = (queries * cosine + swap_halves(queries) * sine).astype(BF16).astype(F32)
    for step in range(chips):
        first = (chips - step) % chips * rows
        out = outs[step]
        if rows * queries.shape[1] // LANE < out.shape[0]:
            out[...] = jnp.zeros_like(out)
        for c in range(queries.shape[1] // LANE):
            at = slice(c * LANE, (c + 1) * LANE)
            row = wire_row(rows, c, 0)
            out[row : row + rows, :] = queries[first : first + rows, at]


def chip_away(step, chips):
    return lax.rem(lax.axis_index("tensor") // 2 + chips - step, chips)


def new_token_kernel(
    rows,
    len_ref,
    pos_ref,
    mask_ref,
    slot_pos_ref,
    same_ref,
    peer_ref,
    gain_ref,
    w_ref,
    cos_ref,
    sin_ref,
    new_ref,
    key_ref,
    live_ref,
):
    mark_live(len_ref, pos_ref, mask_ref, slot_pos_ref, live_ref)
    lanes = w_ref.shape[2]
    core = lax.axis_index("tensor") % 2
    chips = same_ref.shape[0]
    values = jnp.concatenate(
        [ref[step].astype(F32) for ref in (same_ref, peer_ref) for step in range(chips)], axis=0
    )
    normed = normed_rows(values, gain_ref[...].astype(F32).reshape(1, -1))
    repeat = lanes // cos_ref.shape[1]
    cosine = jnp.concatenate([cos_ref[...]] * repeat, axis=1)
    sine = jnp.concatenate([sin_ref[...]] * repeat, axis=1)

    def project(part):
        return jnp.dot(normed, w_ref[part], preferred_element_type=F32)

    def turned(t):
        return (t * cosine + swap_halves(t) * sine).astype(BF16).astype(F32)

    queries = turned(project(0))
    keys = turned(project(1))
    values = project(2).astype(BF16).astype(F32)
    head_in = lax.broadcasted_iota(jnp.int32, (lanes, lanes), 0) // HEAD_SIZE
    head_out = lax.broadcasted_iota(jnp.int32, (lanes, lanes), 1) // HEAD_SIZE
    same_head = (head_in == head_out).astype(F32)
    score = jnp.dot(
        queries * keys,
        same_head,
        preferred_element_type=F32,
        precision=lax.Precision.HIGHEST,
    ) * (HEAD_SIZE**-0.5)
    half, chunk = new_ref.shape[1] // 2, new_ref.shape[2]
    for i in range(2 * chips):
        group = 2 * chip_away(i % chips, chips) + (core if i < chips else 1 - core)
        mine = slice(i * rows, (i + 1) * rows)
        for c in range(lanes // chunk):
            at = slice(c * chunk, (c + 1) * chunk)
            row = wire_row(rows, c, 0)
            new_ref[group, row : row + rows, :] = values[mine, at]
            new_ref[group, half + row : half + row + rows, :] = score[mine, at]
            key_ref[group, row : row + rows, :] = keys[mine, at]


def outputs_kernel(same_ref, peer_ref, new_ref, key_ref, k_ref, v_ref, side_ref, by_ref, flat_ref):
    chips, rows, _ = same_ref.shape
    core = lax.axis_index("tensor") % 2
    for step in range(chips):
        source = 2 * chip_away(step, chips)
        by_ref[source + core, :rows, :] = same_ref[step].astype(F32)
        by_ref[source + 1 - core, :rows, :] = peer_ref[step].astype(F32)
    for group in range(2 * chips):
        flat_ref[group * rows : (group + 1) * rows, :] = by_ref[group, :rows, :]
    width = side_ref.shape[1]
    side_ref[...] = flat_ref[:, pl.ds(pl.multiple_of(core * width, LANE), width)]
    lanes, chunk = k_ref.shape[1], new_ref.shape[2]
    for from_ref, to_ref in ((key_ref, k_ref), (new_ref, v_ref)):
        parts = []
        for c in range(lanes // chunk):
            row = wire_row(rows, c, 0)
            parts.append(
                jnp.concatenate(
                    [from_ref[group, row : row + rows, :] for group in range(2 * chips)], axis=0
                )
            )
        to_ref[...] = jnp.concatenate(parts, axis=1).astype(BF16)


def attention_kernel(lanes, chips, steps, *refs):
    queries, refs = dict(zip(steps, refs)), refs[len(steps) :]
    k_ref, v_ref, sink_k_ref, sink_v_ref, live_ref = refs[:5]
    out_ref, tile_ref = refs[-2:]
    rows, features, slots = k_ref.shape
    sinks = sink_k_ref.shape[1]
    copies = out_ref.shape[0]
    chunk = out_ref.shape[3]
    block = 2 * lanes
    group_heads = lanes // HEAD_SIZE
    repeat = chunk // (rows * group_heads)
    heads = max(8, block // HEAD_SIZE)
    seq_index = lax.axis_index("seq")
    chip = lax.axis_index("tensor") // 2
    head = lax.broadcasted_iota(jnp.int32, (heads, block), 0)
    own = head == lax.broadcasted_iota(jnp.int32, (heads, block), 1) // HEAD_SIZE
    scale = HEAD_SIZE**-0.5
    lives = [
        jnp.broadcast_to(live_ref[r : r + 1, :], (heads, slots)) == 1 for r in range(rows)
    ]
    first_shard = seq_index == 0

    def place(step):
        source = lax.rem(chip + chips - step, chips)
        return source, pl.ds(pl.multiple_of(source * block, block), block)

    def scores(r, step):
        _, here = place(step)
        query = jnp.concatenate(
            [
                queries[step][wire_row(rows, c, r) : wire_row(rows, c, r) + 1, :]
                for c in range(block // LANE)
            ],
            axis=1,
        )
        query = jnp.where(own, jnp.broadcast_to(query, (heads, block)), 0.0)
        score = jnp.dot(query.astype(BF16), k_ref[r, here, :], preferred_element_type=F32)
        return query, score

    def mix(r, step, query, score):
        source, here = place(step)
        sink_keys = sink_k_ref[r, :, here].astype(F32)
        sink_values = sink_v_ref[r, :, here].astype(F32)
        score = jnp.where(lives[r], score * scale, NEG)
        top = jnp.max(score, axis=1, keepdims=True)
        sink_score = []
        for i in range(sinks):
            one = jnp.sum(query * sink_keys[i : i + 1, :], axis=1, keepdims=True) * scale
            one = jnp.where(first_shard, one, NEG)
            sink_score.append(one)
            top = jnp.maximum(top, one)
        weight = jnp.where(lives[r], jnp.exp(score - top), 0.0)
        mixture = lax.dot_general(
            weight.astype(BF16),
            v_ref[r, here, :],
            (((1,), (1,)), ((), ())),
            preferred_element_type=F32,
        )
        total = jnp.sum(weight, axis=1, keepdims=True)
        for i in range(sinks):
            one = jnp.where(first_shard, jnp.exp(sink_score[i] - top), 0.0)
            total = total + one
            mixture = mixture + one.astype(BF16).astype(F32) * sink_values[i : i + 1, :]
        some = total > 0.0
        level = jnp.where(some, top + jnp.log(jnp.where(some, total, 1.0)), NEG)
        mixture = mixture / jnp.where(some, total, 1.0)
        mixture = jnp.sum(jnp.where(own, mixture, 0.0), axis=0, keepdims=True)
        for t in range(2):
            tile = steps.index(step) * 2 + t
            for c in range(lanes // chunk):
                row = wire_row(rows, c, r)
                start = t * lanes + c * chunk
                tile_ref[tile, row : row + 1, :] = mixture[:, start : start + chunk]
            here = head_row == head_lane + (t - r) * group_heads
            here = here & (head_row // group_heads == t)
            one = jnp.sum(jnp.where(here, level, 0.0), axis=0, keepdims=True)
            if r > 0:
                one = one + tile_ref[tile, LEVEL_ROW : LEVEL_ROW + 1, :]
            if r < rows - 1:
                tile_ref[tile, LEVEL_ROW : LEVEL_ROW + 1, :] = one
                continue
            for term in range(3):
                rounded = one.astype(BF16).astype(F32)
                tile_ref[tile, LEVEL_ROW + term : LEVEL_ROW + term + 1, :] = rounded
                one = one - rounded
            parts = tile_ref[tile].astype(BF16)
            for copy in range(copies):
                out_ref[copy, 2 * source + t] = parts

    tile_ref[...] = jnp.zeros_like(tile_ref)
    head_row = lax.broadcasted_iota(jnp.int32, (heads, chunk), 0)
    head_lane = lax.broadcasted_iota(jnp.int32, (heads, chunk), 1) // repeat
    todo = [(r, step) for step in steps for r in range(rows)]
    ahead = [scores(*one) for one in todo[:AHEAD]]
    for i, one in enumerate(todo):
        if i + AHEAD < len(todo):
            ahead.append(scores(*todo[i + AHEAD]))
        mix(*one, *ahead[i])


def merge_kernel(
    rows, part_ref, new_ref, w_ref, mine_ref, other_ref, rows_ref, attended_ref
):
    copies, groups, wire_rows, chunk = part_ref.shape
    lanes = w_ref.shape[0]
    flat = groups * wire_rows
    for s in range(copies):
        rows_ref[s * flat : (s + 1) * flat, :] = part_ref[s].astype(F32).reshape(flat, chunk)
    rows_ref[copies * flat :, :] = new_ref[...].reshape(flat, chunk)

    def every(row, first, count):
        return rows_ref[pl.ds(first * flat + row, count * groups, stride=wire_rows), :]

    count = rows * lanes // chunk
    terms = jnp.concatenate([every(LEVEL_ROW + term, 0, copies) for term in range(3)], axis=0)
    shape = (chunk, count * chunk)
    to = lax.broadcasted_iota(jnp.int32, shape, 1)
    to_head = (to // (rows * chunk) * chunk + to % chunk) // HEAD_SIZE
    group_heads = lanes // HEAD_SIZE
    at = (to // chunk % rows * group_heads + to_head) * (chunk // (rows * group_heads))
    spread = (lax.broadcasted_iota(jnp.int32, shape, 0) == at).astype(F32).astype(BF16)
    terms = jnp.dot(terms.astype(BF16), spread, preferred_element_type=F32)
    size = copies * groups
    levels = terms[:size] + terms[size : 2 * size] + terms[2 * size :]
    for i in range(count):
        c, r = divmod(i, rows)
        mine = every(i, 0, copies)
        parts = [mine[s * groups : (s + 1) * groups] for s in range(copies)]
        parts.append(every(i, copies, 1))
        level = [
            levels[s * groups : (s + 1) * groups, i * chunk : (i + 1) * chunk]
            for s in range(copies)
        ]
        level.append(every(wire_rows // 2 + i, copies, 1))
        top = functools.reduce(jnp.maximum, level)
        shares = [jnp.exp(one - top) for one in level]
        mixture = functools.reduce(jnp.add, [share * part for share, part in zip(shares, parts)])
        total = functools.reduce(jnp.add, shares)
        attended_ref[c, pl.ds(r, groups, stride=rows), :] = mixture / total
    attended = [attended_ref[c] for c in range(lanes // chunk)]
    attended = jnp.concatenate(attended, axis=1).astype(BF16)
    width = mine_ref.shape[1]
    core = lax.axis_index("tensor") % 2
    for half, to_ref in ((1 - core, other_ref), (core, mine_ref)):
        weights = w_ref[:, pl.ds(pl.multiple_of(half * width, LANE), width)]
        to_ref[...] = jnp.dot(attended, weights, preferred_element_type=F32).astype(to_ref.dtype)


def spread_rows(values, wide_ref):
    batch, width = values.shape
    step = 2 * LANE
    feature = lax.broadcasted_iota(jnp.int32, (step, 4 * step), 0)
    lane = lax.broadcasted_iota(jnp.int32, (step, 4 * step), 1)
    lane = jnp.where(lane < 2 * step, lane, lane - 2 * step - 1)
    spread = (2 * feature == lane).astype(F32).astype(BF16)
    pieces = width // step
    stacked = jnp.concatenate([values[:, j * step : (j + 1) * step] for j in range(pieces)], axis=0)
    wide = jnp.dot(stacked, spread, preferred_element_type=F32).astype(BF16)
    for j in range(pieces):
        part = wide[j * batch : (j + 1) * batch, :]
        at = slice(j * 2 * step, (j + 1) * 2 * step)
        wide_ref[:batch, at] = part[:, : 2 * step]
        wide_ref[batch:, at] = part[:, 2 * step :]


def half_gate_up(side, half, gain_ref, gate_up_ref, wide_ref):
    width = side.shape[1]
    units = gate_up_ref.shape[2]
    gain = gain_ref[...].astype(F32).reshape(1, -1)
    gain = jnp.where(half == 0, gain[:, :width], gain[:, width:])
    spread_rows((side * gain).astype(BF16), wide_ref)
    weights = gate_up_ref.reshape(4 * width, units)
    weights = weights[pl.ds(pl.multiple_of(half * 2 * width, 2 * width), 2 * width), :]
    gate_up = jnp.dot(wide_ref[...], weights, preferred_element_type=F32)
    return gate_up, jnp.sum(side * side, axis=1, keepdims=True)


def first_half_kernel(side_ref, gain_ref, gate_up_ref, out_ref, square_ref, wide_ref):
    core = lax.axis_index("tensor") % 2
    side = side_ref[...].astype(F32)
    out_ref[...], square = half_gate_up(side, core, gain_ref, gate_up_ref, wide_ref)
    square_ref[...] = jnp.broadcast_to(square, square_ref.shape)


def mlp_kernel(
    rows,
    mine_ref,
    other_ref,
    gain_ref,
    gate_up_ref,
    down_ref,
    first_ref,
    square_ref,
    out_ref,
    resid_ref,
    wide_ref,
    by_ref,
):
    batch, width = mine_ref.shape
    core = lax.axis_index("tensor") % 2
    mine = mine_ref[...].astype(F32)
    other = other_ref[...].astype(F32)
    gate_up, square = half_gate_up(other, 1 - core, gain_ref, gate_up_ref, wide_ref)
    meansq = (square + square_ref[:, :1]) / (2 * width)
    scale = lax.rsqrt(meansq + 1e-05)
    gate_up = gate_up + first_ref[...]
    gate = gate_up[:batch] * scale
    hidden = (gate * jax.nn.sigmoid(gate) * (gate_up[batch:] * scale)).astype(BF16)
    out = jnp.dot(hidden, down_ref[...], preferred_element_type=F32)
    resid = jnp.concatenate(
        [jnp.where(core == 0, mine, other), jnp.where(core == 0, other, mine)], axis=1
    )
    groups = out_ref.shape[0]
    for group in range(groups):
        by_ref[group, :rows, :] = resid[group * rows : (group + 1) * rows, :]
        out_ref[group] = out[group * rows : (group + 1) * rows, :].astype(BF16)
    resid_ref[...] = by_ref[lax.axis_index("tensor"), :rows, :]


def prepare_kernel(rows, pos_ref, cos_ref, sin_ref):
    core = lax.axis_index("tensor") % 2
    chips = cos_ref.shape[0] // (2 * rows)
    wide = cos_ref.shape[1]
    half = HEAD_SIZE // 2
    pair = lax.broadcasted_iota(jnp.int32, (1, wide), 1) % half
    inverse = jnp.zeros((1, wide), F32)
    for i in range(half):
        inverse = jnp.where(pair == i, np.float32(ROTARY_BASE ** (-2 * i / HEAD_SIZE)), inverse)

    shape = cos_ref.shape
    row = lax.broadcasted_iota(jnp.int32, shape, 0)
    position = jnp.zeros(shape, F32)
    for i in range(shape[0]):
        group, r = divmod(i, rows)
        parity = core if group < chips else 1 - core
        request = (2 * chip_away(group % chips, chips) + parity) * rows + r
        position = jnp.where(row == i, pos_ref[request].astype(F32), position)
    angle = position * inverse
    sine = jnp.sin(angle)
    lane = lax.broadcasted_iota(jnp.int32, shape, 1)
    cos_ref[...] = jnp.cos(angle)
    sin_ref[...] = jnp.where(lane % HEAD_SIZE < half, -sine, sine)


def mark_live(len_ref, pos_ref, mask_ref, slot_pos_ref, live_ref):
    rows, slots = mask_ref.shape
    slot = lax.axis_index("seq") * slots + lax.broadcasted_iota(jnp.int32, (1, slots), 1)
    first_row = lax.axis_index("tensor") * rows
    for r in range(rows):
        own_len = len_ref[first_row + r]
        own_pos = pos_ref[first_row + r]
        slot_at = slot_pos_ref[r : r + 1, :]
        live = (slot < own_len) & (mask_ref[r : r + 1, :] == 1)
        live = live & (slot_at < own_pos) & (own_pos - slot_at < WINDOW)
        live_ref[r : r + 1, :] = live.astype(jnp.int32)


def call(kernel, out, inputs, specs=None, scratch=(), limit=6, name=None, flops=0, aliases={}):
    return pl.pallas_call(
        kernel,
        out_shape=out,
        in_specs=specs or [VMEM_SPEC] * len(inputs),
        out_specs=jax.tree.map(lambda _: VMEM_SPEC, out),
        scratch_shapes=scratch,
        input_output_aliases=aliases,
        compiler_params=pltpu.CompilerParams(vmem_limit_bytes=limit * MIB),
        name=name,
        cost_estimate=pl.CostEstimate(
            flops=flops,
            bytes_accessed=sum(a.size * a.dtype.itemsize for a in inputs),
            transcendentals=0,
        ),
    )(*inputs)


def per_device(
    shards,
    groups,
    states,
    attn_gain,
    w_qkv,
    w_out,
    mlp_gain,
    w_gate_up,
    w_down,
    key_cache,
    value_cache,
    sink_keys,
    sink_values,
    cache_len,
    slot_mask,
    slot_pos,
    new_pos,
):
    rows, width = states.shape
    batch = rows * groups
    lanes = w_qkv.shape[2]
    sds = jax.ShapeDtypeStruct
    chunk = min(lanes, LANE)
    wire_rows = max(8, 2 * rows * lanes // chunk)

    chips = groups // 2
    turn = sds((batch, chunk), F32)
    cosine, sine = call(
        functools.partial(prepare_kernel, rows),
        (turn, turn),
        (new_pos,),
        specs=[SMEM_SPEC],
        name="prepare",
        flops=PREP_FLOPS,
    )
    across = [(i, i ^ 1) for i in range(groups)]
    hops = [[(i, (i + step) % groups) for i in range(groups)] for step in range(2, groups, 2)]
    column = [states] + [lax.ppermute(states, "tensor", hop) for hop in hops]
    w_qkv = jnp.transpose(w_qkv, (1, 0, 2))
    w_peer = lax.ppermute(w_qkv, "tensor", across)
    query_wire = sds((max(8, 2 * rows * lanes // LANE), LANE), F32)
    queries = call(
        functools.partial(query_kernel, rows, chips),
        (query_wire,) * chips,
        (*column, attn_gain, w_qkv, w_peer, cosine, sine),
        name="query",
        flops=QKV_FLOPS,
    )
    same = jnp.stack(column)
    same, *queries = lax.optimization_barrier((same, *queries))
    peer = lax.ppermute(same, "tensor", across)
    queries = [queries[0]] + [
        lax.ppermute(query, "tensor", hop) for query, hop in zip(queries[1:], hops)
    ]
    wire = sds((groups, wire_rows, chunk), F32)
    new_part, key_part, live = call(
        functools.partial(new_token_kernel, rows),
        (wire, wire, sds(slot_mask.shape, jnp.int32)),
        (cache_len, new_pos, slot_mask, slot_pos, same, peer, attn_gain, w_qkv, cosine, sine),
        specs=[SMEM_SPEC] * 2 + [VMEM_SPEC] * 8,
        name="new_token",
        flops=QKV_FLOPS,
    )
    sink_keys = jnp.transpose(sink_keys, (0, 2, 1))
    sink_values = jnp.transpose(sink_values, (0, 2, 1))

    def attention(steps, arrays, aliases, name):
        return call(
            functools.partial(attention_kernel, lanes, chips, steps),
            sds((shards, groups, 8, chunk), BF16),
            arrays,
            scratch=[pltpu.VMEM((2 * len(steps), 8, chunk), F32)],
            limit=8,
            name=name,
            flops=ATT_FLOPS,
            aliases=aliases,
        )

    cache = (key_cache, value_cache, sink_keys, sink_values, live)
    part = attention((0,), (queries[0], *cache), {}, "own_heads")
    first, new_part, part = lax.optimization_barrier((queries[1:-1], new_part, part))
    queries = [queries[0], *first, queries[-1]]
    middle = tuple(range(1, chips - 1))
    part = attention(middle, (*queries[1:-1], *cache, part), {len(middle) + 5: 0}, "middle_heads")
    last, part = lax.optimization_barrier((queries[-1], part))
    part = attention((chips - 1,), (last, *cache, part), {6: 0}, "last_heads")
    part = lax.all_to_all(
        part.reshape(shards * groups, 8, chunk), ("seq", "tensor"), 0, 0, tiled=True
    ).reshape(shards, groups, 8, chunk)
    side = sds((batch, width // 2), F32)
    mine, other = call(
        functools.partial(merge_kernel, rows),
        (side, sds(side.shape, BF16)),
        (part, new_part, w_out),
        scratch=[
            pltpu.VMEM(((shards + 1) * groups * 8, chunk), F32),
            pltpu.VMEM((lanes // chunk, batch, chunk), F32),
        ],
        name="merge",
        flops=MERGE_FLOPS,
    )
    chip = (mine + lax.ppermute(other, "tensor", across).astype(F32)).astype(BF16)
    flat = sds((batch, lanes), BF16)
    chip, same, peer, new_part, key_part = lax.optimization_barrier(
        (chip, same, peer, new_part, key_part)
    )
    new_keys, new_values, own_side = call(
        outputs_kernel,
        (flat, flat, side),
        (same, peer, new_part, key_part),
        scratch=[pltpu.VMEM((groups, 8, width), F32), pltpu.VMEM((batch, width), F32)],
        name="outputs",
    )
    total = chip.astype(F32)
    for which in range(0, -len(hops), -1):
        total = total + lax.ppermute(chip, "tensor", hops[which]).astype(F32)
    side_resid = (own_side + total).astype(BF16)
    other_resid = lax.ppermute(side_resid, "tensor", across)
    units = w_gate_up.shape[2]
    first_half, square = call(
        first_half_kernel,
        (sds((2 * batch, units), F32), sds((batch, LANE), F32)),
        (side_resid, mlp_gain, w_gate_up),
        scratch=[pltpu.VMEM((2 * batch, width), BF16)],
        limit=8,
        name="first_half",
        flops=2 * batch * width * units,
    )
    partial, own_resid = call(
        functools.partial(mlp_kernel, rows),
        (sds((groups, rows, width), BF16), sds((rows, width), F32)),
        (side_resid, other_resid, mlp_gain, w_gate_up, w_down, first_half, square),
        scratch=[pltpu.VMEM((2 * batch, width), BF16), pltpu.VMEM((groups, 8, width), F32)],
        limit=8,
        name="mlp",
        flops=4 * batch * width * units,
    )
    partial = lax.all_to_all(partial, "tensor", 0, 0, tiled=True)
    out_states = (own_resid + jnp.sum(partial.astype(F32), axis=0)).astype(BF16)
    return out_states, new_keys, new_values


def solution(mesh):
    in_specs = (
        P("tensor", None),
        P(),
        P(None, None, "tensor"),
        P("tensor", None),
        P(),
        P(None, None, "tensor"),
        P("tensor", None),
        P("tensor", None, "seq"),
        P("tensor", None, "seq"),
        P("tensor", None, None),
        P("tensor", None, None),
        P(),
        P("tensor", "seq"),
        P("tensor", "seq"),
        P(),
    )
    out_specs = (P("tensor", None), P(None, "tensor"), P(None, "tensor"))
    body = functools.partial(per_device, mesh.shape["seq"], mesh.shape["tensor"])
    return jax.shard_map(
        body, mesh=mesh, in_specs=in_specs, out_specs=out_specs, check_vma=False
    )
```
